256 devices in a mesh: tm: 4 (over y), space: 64 (over z, x, core).
Axes of the slice: x: 4, y: 4, z: 8, core: 2. Of those that a mesh axis runs over, the one named last changes fastest.
Arguments:
- latents: bfloat16 [4, 64, 8, 40, 384], P('tm', 'space'), may hold values from -8 to 8
- gain_first: float32 [384], replicated, may hold values from 0.5 to 2
- shift_first: float32 [384], replicated, may hold values from -3 to 3
- kernel_first: bfloat16 [3, 3, 3, 384, 384], P(None, None, None, 'space', 'tm'), may hold values from -0.0625 to 0.0625
- bias_first: float32 [384], replicated, may hold values from -3 to 3
- gain_second: float32 [384], replicated, may hold values from 0.5 to 2
- shift_second: float32 [384], replicated, may hold values from -3 to 3
- kernel_second: bfloat16 [3, 3, 3, 384, 384], P(None, None, None, 'space', 'tm'), may hold values from -0.0625 to 0.0625
- bias_second: float32 [384], replicated, may hold values from -3 to 3
Outputs:
- decoded: bfloat16 [4, 64, 8, 40, 384], P('tm', 'space')
The draws below stay inside these ranges and needn't reach their ends.
All inputs are finite; a program needn't handle non-finite values.
Results may differ from the reference program's by a relative error of at most 0.0085.
Values may be sent and summed in bfloat16 or wider, within the bound.
No kernel may reach another device: no remote copies, remote signals or barrier semaphores. Data moves between devices by JAX's collectives and lax.ppermute only.
A program may use at most 128 MiB of HBM per device.

```python
import math
import jax
import jax.numpy as jnp
from jax import lax

C = 384
GROUPS = 32
TH = 8
TW = 40
GX = 8
GY = 8
FRAMES = 4
TILES = 64


def draw_latents(key, part):
    key = jax.random.fold_in(key, 11)
    first_key, second_key, third_key, fourth_key = jax.random.split(key, 4)
    shape = (FRAMES, TILES, TH, TW, C)
    block_shape = (FRAMES, TILES, 1, 1, 1)
    frame_pos = lax.broadcasted_iota(jnp.float32, shape, 0)
    tile_pos = lax.broadcasted_iota(jnp.float32, shape, 1)
    ramp = (frame_pos * TILES + tile_pos) / max(FRAMES * TILES - 1, 1)
    channel_scale = jnp.exp(jax.random.uniform(second_key, (C,), jnp.float32, -0.7, 0.7))
    block_scale = jnp.exp(jax.random.uniform(third_key, block_shape, jnp.float32, -1.0, 1.0))
    block_offset = jax.random.uniform(fourth_key, block_shape, jnp.float32, -2.5, 2.5)
    values = jax.random.normal(first_key, shape, jnp.float32)
    scale = 0.5 * jnp.power(3.0, ramp)
    return jnp.clip(values * scale * channel_scale * block_scale + block_offset, -8.0, 8.0).astype(jnp.bfloat16)


def block_levels(key, dims, cuts, smallest, high):
    factor_of, own = 1.0, jax.random.fold_in(key, 6)
    for axis_at, shards_of in cuts:
        draws = jnp.exp(jax.random.uniform(jax.random.fold_in(own, axis_at), (shards_of,), jnp.float32, smallest / len(cuts), high / len(cuts)))
        factor_of = factor_of * jnp.repeat(draws, dims[axis_at] // shards_of).reshape([-1 if axis == axis_at else 1 for axis in range(len(dims))])
    return factor_of


def noise(rng, shape, scale, bound, shards=(), held_as=jnp.bfloat16):
    entries = scale * jax.random.normal(rng, shape, jnp.float32)
    if shards:
        entries = entries * block_levels(rng, shape, shards, -0.22, 0.18)
    return jnp.clip(entries, -bound, bound).astype(held_as)


def setup_inputs(seed: int = 0) -> dict:
    seeds = jax.random.split(jax.random.key(seed), 10)
    latents = draw_latents(jax.random.fold_in(seeds[9], 71), 0)
    gain_first = jnp.clip(jnp.exp(jax.random.uniform(seeds[1], (C,), jnp.float32, math.log(0.5), math.log(2.0))), 0.5, 2.0)
    shift_first = noise(seeds[2], (C,), 0.5, 3.0, (), jnp.float32)
    kernel_first = noise(seeds[3], (3, 3, 3, C, C), (27 * C) ** -0.5, 0.0625, ((3, 64), (4, 4)))
    bias_first = noise(seeds[4], (C,), 0.5, 3.0, (), jnp.float32)
    gain_second = jnp.clip(jnp.exp(jax.random.uniform(seeds[5], (C,), jnp.float32, math.log(0.5), math.log(2.0))), 0.5, 2.0)
    shift_second = noise(seeds[6], (C,), 0.5, 3.0, (), jnp.float32)
    kernel_second = noise(seeds[7], (3, 3, 3, C, C), (27 * C) ** -0.5, 0.0625, ((3, 64), (4, 4)))
    bias_second = noise(seeds[8], (C,), 0.5, 3.0, (), jnp.float32)
    return {"latents": latents, "gain_first": gain_first, "shift_first": shift_first, "kernel_first": kernel_first, "bias_first": bias_first, "gain_second": gain_second, "shift_second": shift_second, "kernel_second": kernel_second, "bias_second": bias_second}


EPS = 1e-06

def to_frame(tiles):
    shaped = tiles.reshape(FRAMES, GY, GX, TH, TW, C)
    return shaped.transpose(0, 1, 3, 2, 4, 5).reshape(FRAMES, GY * TH, GX * TW, C)

def to_tiles(field):
    shaped = field.reshape(FRAMES, GY, TH, GX, TW, C)
    return shaped.transpose(0, 1, 3, 2, 4, 5).reshape(FRAMES, GY * GX, TH, TW, C)

def group_act(field, gain, shift):
    grouped = field.reshape(FRAMES, GY * TH, GX * TW, GROUPS, C // GROUPS)
    mean = lax.optimization_barrier(jnp.mean(grouped, axis=(0, 1, 2, 4), keepdims=True))
    centered = grouped - mean
    spread = lax.optimization_barrier(jnp.mean(centered * centered, axis=(0, 1, 2, 4), keepdims=True))
    normed = (centered * lax.rsqrt(spread + EPS)).reshape(field.shape)
    return jax.nn.silu(normed * gain + shift).astype(jnp.bfloat16)

def causal_conv(act, kernel, bias):
    result = lax.conv_general_dilated(act.astype(jnp.float32)[None], kernel.astype(jnp.float32), (1, 1, 1), ((2, 0), (1, 1), (1, 1)), dimension_numbers=('NDHWC', 'DHWIO', 'NDHWC'), precision=lax.Precision.HIGHEST)
    return result[0] + bias

def reference(latents, gain_first, shift_first, kernel_first, bias_first, gain_second, shift_second, kernel_second, bias_second):
    frame = to_frame(latents).astype(jnp.float32)
    first_act = group_act(frame, gain_first, shift_first)
    first_out = causal_conv(first_act, kernel_first, bias_first)
    second_act = group_act(first_out, gain_second, shift_second)
    second_out = causal_conv(second_act, kernel_second, bias_second)
    return to_tiles((frame + second_out).astype(jnp.bfloat16))
```

```python
import functools

import jax
import jax.numpy as jnp
import numpy as np
from jax import lax
from jax.experimental import pallas as pl
from jax.experimental.pallas import tpu as pltpu
from jax.sharding import PartitionSpec as P

EPS = 1e-06
BF = jnp.bfloat16
F32 = jnp.float32
VM = pl.BlockSpec(memory_space=pltpu.VMEM)
SM = pl.BlockSpec(memory_space=pltpu.SMEM)
HIGH = lax.Precision.HIGHEST

NZ, NX, NC, NY = 8, 4, 2, 4
COLS = NX * NC
SPACE = NZ * COLS
ROWS, WIDE, PITCH = 8, 40, 48
CH, PART, WG = 384, 96, 12
FLAT = (ROWS + 2) * PITCH
GUARD = 16
BOTH = ("tm", "space")
ALONG_Z = [[z * COLS + q for z in range(NZ)] for q in range(COLS)]
ALONG_X = [[z * COLS + x * NC + c for x in range(NX)] for z in range(NZ) for c in range(NC)]
Y_CORE = [
    [y * SPACE + z * COLS + x * NC + c for y in range(NY) for c in range(NC)]
    for z in range(NZ)
    for x in range(NX)
]
SIBLING = [(s, s ^ 1) for s in range(SPACE)]
EAST = [(s, (s + 1) % SPACE) for s in range(SPACE)]
WEST = [(s, (s - 1) % SPACE) for s in range(SPACE)]
SOUTH = [(s, (s + COLS) % SPACE) for s in range(SPACE)]
NORTH = [(s, (s - COLS) % SPACE) for s in range(SPACE)]
SWAP = [
    (y * SPACE + z * COLS + q, (z // 2) * SPACE + (2 * y + z % 2) * COLS + q)
    for y in range(NY)
    for z in range(NZ)
    for q in range(COLS)
]


def one_hot(rows, cols, pairs):
    out = np.zeros((rows, cols), np.float32)
    for r, c in pairs:
        out[r, c] = 1.0
    return out


CHANNEL_LANES = one_hot(
    CH, CH, [(6 * (8 * z + q) + i, 48 * q + 6 * z + i) for z in range(8) for q in range(8) for i in range(6)]
)
GROUPS_OF = one_hot(CH, 128, [(c, c // WG) for c in range(CH)])
GROUPS_OF_LANES = CHANNEL_LANES.T @ GROUPS_OF
PART_GROUPS = one_hot(128, 128, [(c, c // WG) for c in range(PART)])
EDGES = one_hot(16, 320, [(r, 40 * r) for r in range(8)] + [(8 + r, 40 * r + 39) for r in range(8)])
FIRST_ROWS = one_hot(
    432, 512, [(48 * k + 6 * z + i, 64 * z + 6 * k + i) for k in range(9) for z in range(8) for i in range(6)]
)
SECOND_ROWS = one_hot(
    144, 128, [(16 * k + 6 * h + i, 64 * h + 6 * k + i) for k in range(9) for h in range(2) for i in range(6)]
)
SECOND_LANES = one_hot(512, CH, [(128 * y + o, PART * y + o) for y in range(4) for o in range(PART)])
PART_LANES = one_hot(
    128, 128, [(48 * h + 6 * q + i, 16 * q + 6 * h + i) for h in range(2) for q in range(8) for i in range(6)]
)


def dot(a, b):
    return jnp.dot(a, b, preferred_element_type=F32)


def exact(a, b):
    return jnp.dot(a, b, preferred_element_type=F32, precision=HIGH)


def split(x):
    hi = x.astype(BF).astype(F32)
    mid = (x - hi).astype(BF).astype(F32)
    return hi, mid, x - hi - mid


def moment_rows(mean, squares):
    rows = [*split(mean), *split(squares)]
    return jnp.concatenate(rows + [jnp.zeros((10, 128), F32)], axis=0).astype(BF)


def merge(means, squares, count):
    mean = jnp.mean(means, axis=0, keepdims=True)
    off = means - mean
    return mean, jnp.sum(squares, axis=0, keepdims=True) + count * jnp.sum(off * off, axis=0, keepdims=True)


def read_moments(blocks):
    means = [b[0:1] + b[1:2] + b[2:3] for b in blocks]
    squares = [b[3:4] + b[4:5] + b[5:6] for b in blocks]
    return jnp.concatenate(means, axis=0), jnp.concatenate(squares, axis=0)


def tall(row):
    return jnp.broadcast_to(row, (8, row.shape[1]))


def silu(u):
    return u / (1.0 + jnp.exp(-u))


def measure_tile(tile_ref, lanes_ref, groups_ref, groups_t_ref, edges_ref, placed_ref, edge_ref, moments_ref):
    tile = tile_ref[...]
    placed = dot(tile, lanes_ref[...]).astype(BF)
    placed_ref[...] = placed
    edge_ref[...] = dot(edges_ref[...], placed).astype(BF)
    wide = tile.astype(F32)
    per = 1.0 / (320 * WG)
    mean = exact(tall(jnp.sum(wide, axis=0, keepdims=True)), groups_ref[...]) * per
    off = wide - exact(mean, groups_t_ref[...])[0:1]
    squares = exact(tall(jnp.sum(off * off, axis=0, keepdims=True)), groups_ref[...])
    moments_ref[...] = moment_rows(mean[0:1], squares[0:1])


def arrange_first(got_ref, rows_ref, out_ref):
    parts = [
        jnp.concatenate([got_ref[z, 64 * d : 64 * d + 64, :] for z in range(NZ)], axis=0) for d in range(3)
    ]
    ordered = dot(rows_ref[...], jnp.concatenate(parts, axis=1)).astype(BF)
    means, squares = read_moments([got_ref[z, 192:208, :].astype(F32) for z in range(NZ)])
    mean, total = merge(means, squares, 320.0 * WG)
    moments = moment_rows(mean, total)
    for copy in range(NX):
        for d in range(3):
            for k in range(9):
                out_ref[copy, 48 * d : 48 * d + 48, 128 * k : 128 * k + 128] = ordered[
                    48 * k : 48 * k + 48, 128 * d : 128 * d + 128
                ]
        out_ref[copy, 144:160, 0:128] = moments
        out_ref[copy, 144:160, 128:] = jnp.zeros((16, 1024), BF)


def arrange_second(got_ref, rows_ref, lanes_ref, out_ref):
    by_part = []
    for y in range(NY):
        parts = [
            jnp.concatenate([got_ref[2 * y + h, 64 * d : 64 * d + 64, :] for h in range(2)], axis=0)
            for d in range(3)
        ]
        by_part.append(dot(rows_ref[...], jnp.concatenate(parts, axis=1)).astype(BF))
    tall_parts = [
        jnp.concatenate([by_part[y][:, 128 * d : 128 * d + 128] for y in range(NY)], axis=1) for d in range(3)
    ]
    out_ref[...] = dot(jnp.concatenate(tall_parts, axis=0), lanes_ref[...]).astype(BF)


def first_conv(
    pos_ref, lat_ref, own_ref, other_ref, moments_ref, gain_ref, shift_ref, bias_ref, lanes_ref, groups_ref,
    part_ref, part_t_ref, out_ref, west_ref, east_ref, sums_ref, weights, flat, stack,
):
    row, col, core = pos_ref[0], pos_ref[1], pos_ref[2]
    for mine in range(NC):

        @pl.when(core == mine)
        def _():
            for x in range(NX):
                for d in range(3):
                    at = CH * d + 48 * (NC * x + mine)
                    weights[at : at + 48, :] = own_ref[x, 48 * d : 48 * d + 48, :]
                    at = CH * d + 48 * (NC * x + 1 - mine)
                    weights[at : at + 48, :] = other_ref[x, 48 * d : 48 * d + 48, :]

    blocks = [moments_ref[g, x].astype(F32) for g in range(NY * NC) for x in range(NX)]
    means, squares = read_moments(blocks)
    mean, total = merge(means, squares, 320.0 * WG * NZ)
    spread = total * (1.0 / (320 * WG * NZ * NX * NC * NY))
    both = jnp.concatenate([mean, lax.rsqrt(spread + EPS), jnp.zeros((6, 128), F32)], axis=0)
    by_lane = exact(both, groups_ref[...])
    affine = exact(
        jnp.concatenate([gain_ref[...], shift_ref[...], jnp.zeros((6, CH), F32)], axis=0), lanes_ref[...]
    )
    mean_l, scale_l = by_lane[0:1], by_lane[1:2] * affine[0:1]
    shift_l = affine[1:2]
    has_w = (col > 0).astype(F32)
    has_e = (col < COLS - 1).astype(F32)
    has_n = (row > 0).astype(F32)
    has_s = (row < NZ - 1).astype(F32)
    at = lax.broadcasted_iota(jnp.int32, (PITCH, 1), 0)
    side = jnp.where(at == WIDE, has_e, jnp.where(at == PITCH - 1, has_w, jnp.where(at < WIDE, 1.0, 0.0)))
    flat[...] = jnp.zeros_like(flat)
    for t in range(NY):
        act = silu((lat_ref[t].astype(F32) - mean_l) * scale_l + shift_l)
        north, south = act[336:384] * (side * has_n), act[384:432] * (side * has_s)
        flat[GUARD : GUARD + PITCH, :] = north
        flat[GUARD - 8 : GUARD, :] = north[40:48]
        for r in range(ROWS):
            base = GUARD + PITCH * (r + 1)
            flat[base : base + WIDE, :] = act[WIDE * r : WIDE * r + WIDE]
            flat[base + WIDE : base + WIDE + 1, :] = act[328 + r : 329 + r] * has_e
            flat[base - 1 : base, :] = act[320 + r : 321 + r] * has_w
        base = GUARD + PITCH * (ROWS + 1)
        flat[base : base + PITCH, :] = south
        flat[base - 1 : base, :] = south[47:48]
        for d in range(3):
            stack[t, :, CH * d : CH * d + CH] = flat[GUARD + d - 1 : GUARD + d - 1 + FLAT, :].astype(BF)
    totals = [None] * NY
    for t in range(NY):
        for dt in range(3):
            to = t + 2 - dt
            if to >= NY:
                continue
            part = dot(stack[t], weights[:, CH * dt : CH * dt + CH])
            term = part[0:384, 0:128] + part[48:432, 128:256] + part[96:480, 256:384]
            totals[to] = term if totals[to] is None else totals[to] + term
    inside = (lax.broadcasted_iota(jnp.int32, (384, 1), 0) % PITCH < WIDE).astype(F32)
    sums = None
    for t in range(NY):
        totals[t] = totals[t] + bias_ref[...]
        line = jnp.sum(totals[t] * inside, axis=0, keepdims=True)
        sums = line if sums is None else sums + line
        for r in range(ROWS):
            out_ref[t, r] = totals[t][PITCH * r : PITCH * r + PITCH]
            west_ref[t, r : r + 1, :] = totals[t][PITCH * r : PITCH * r + 1]
            east_ref[t, r : r + 1, :] = totals[t][PITCH * r + WIDE - 1 : PITCH * r + WIDE]
    mean = exact(tall(sums), part_ref[...]) * (1.0 / (320 * NY * WG))
    mean_l = exact(mean, part_t_ref[...])[0:1]
    sums = None
    for t in range(NY):
        off = (totals[t] - mean_l) * inside
        line = jnp.sum(off * off, axis=0, keepdims=True)
        sums = line if sums is None else sums + line
    squares = exact(tall(sums), part_ref[...])
    sums_ref[:, 0:128] = jnp.broadcast_to(mean[0:1], (SPACE, 128))
    sums_ref[:, 128:256] = jnp.broadcast_to(squares[0:1], (SPACE, 128))


def second_conv(
    pos_ref, field_ref, west_ref, east_ref, north_ref, south_ref, sums_ref, gain_ref, shift_ref, own_ref, other_ref,
    part_t_ref, order_ref, out_ref, weights, flat, stack,
):
    row, col, core = pos_ref[0], pos_ref[1], pos_ref[2]
    for mine in range(NC):

        @pl.when(core == mine)
        def _():
            for x in range(NX):
                for d in range(3):
                    for k in range(9):
                        tap = 9 * (k // 3) + 3 * (k % 3) + d
                        source = 144 * d + 16 * k
                        at = 128 * tap + 16 * (NC * x + mine)
                        weights[at : at + 16, :] = own_ref[x, source : source + 16, :]
                        at = 128 * tap + 16 * (NC * x + 1 - mine)
                        weights[at : at + 16, :] = other_ref[x, source : source + 16, :]

    mean, total = merge(sums_ref[:, 0:128], sums_ref[:, 128:256], 320.0 * NY * WG)
    spread = total * (1.0 / (320 * NY * WG * SPACE))
    both = jnp.concatenate([mean, lax.rsqrt(spread + EPS), jnp.zeros((6, 128), F32)], axis=0)
    by_lane = exact(both, part_t_ref[...])
    mean_l, scale_l = by_lane[0:1], by_lane[1:2] * gain_ref[...]
    shift_l = shift_ref[...]

    def act_of(v):
        act = silu((v - mean_l) * scale_l + shift_l).astype(BF)
        return dot(act, order_ref[...])

    has_w = (col > 0).astype(F32)
    has_e = (col < COLS - 1).astype(F32)
    has_n = (row > 0).astype(F32)
    has_s = (row < NZ - 1).astype(F32)
    at = lax.broadcasted_iota(jnp.int32, (PITCH, 1), 0)
    side = jnp.where(at == WIDE, has_e, jnp.where(at == PITCH - 1, has_w, jnp.where(at < WIDE, 1.0, 0.0)))
    flat[...] = jnp.zeros_like(flat)
    for t in range(NY):
        north, south = act_of(north_ref[t]) * (side * has_n), act_of(south_ref[t]) * (side * has_s)
        left, right = act_of(west_ref[t]) * has_w, act_of(east_ref[t]) * has_e
        flat[GUARD : GUARD + PITCH, :] = north
        flat[GUARD - 8 : GUARD, :] = north[40:48]
        for r in range(ROWS):
            base = GUARD + PITCH * (r + 1)
            flat[base : base + WIDE, :] = act_of(field_ref[t, r])[0:WIDE]
            flat[base + WIDE : base + WIDE + 1, :] = right[r : r + 1]
            flat[base - 1 : base, :] = left[r : r + 1]
        base = GUARD + PITCH * (ROWS + 1)
        flat[base : base + PITCH, :] = south
        flat[base - 1 : base, :] = south[47:48]
        for dy in range(3):
            for dx in range(3):
                start = GUARD + PITCH * dy + dx - 1
                lane = 128 * (3 * dy + dx)
                stack[t, :, lane : lane + 128] = flat[start : start + 384, :].astype(BF)
    for t in range(NY):
        total = None
        for dt in range(3):
            source = t - 2 + dt
            if source < 0:
                continue
            term = dot(stack[source], weights[1152 * dt : 1152 * dt + 1152, :])
            total = term if total is None else total + term
        for r in range(ROWS):
            out_ref[t, r] = total[PITCH * r : PITCH * r + WIDE].astype(BF)


def call(body, outs, scratch, smem, *args):
    return pl.pallas_call(
        body,
        out_shape=outs,
        in_specs=[SM] * smem + [VM] * (len(args) - smem),
        out_specs=jax.tree.map(lambda _: VM, outs),
        scratch_shapes=scratch,
        compiler_params=pltpu.CompilerParams(vmem_limit_bytes=56 * 1024 * 1024),
    )(*args)


def shape(dims, dtype):
    return jax.ShapeDtypeStruct(dims, dtype)


def edge_row(row, west, east):
    gap = jnp.zeros(row.shape[:-2] + (PITCH - WIDE - 2, row.shape[-1]), row.dtype)
    return jnp.concatenate([row, east, gap, west], axis=-2)


def by_column(kernel):
    rows = jnp.transpose(kernel, (2, 0, 1, 3, 4)).reshape(3, 54, PART)
    return jnp.pad(rows, ((0, 0), (0, 10), (0, 32))).reshape(192, 128)


def shards(
    latents,
    gain_first,
    shift_first,
    kernel_first,
    bias_first,
    gain_second,
    shift_second,
    kernel_second,
    bias_second,
):
    space = lax.axis_index("space")
    frame = lax.axis_index("tm")
    pos = jnp.stack([space // COLS, space % COLS, space % NC]).astype(jnp.int32)
    tile = latents[0, 0]
    flat_tile = tile.reshape(ROWS * WIDE, CH)

    swapped = lax.ppermute(by_column(kernel_second), BOTH, SWAP)
    placed, edges, moments = call(
        measure_tile,
        (shape((320, CH), BF), shape((16, CH), BF), shape((16, 128), BF)),
        [],
        0,
        flat_tile,
        jnp.asarray(CHANNEL_LANES, BF),
        jnp.asarray(GROUPS_OF),
        jnp.asarray(GROUPS_OF.T),
        jnp.asarray(EDGES, BF),
    )
    from_west = lax.ppermute(edges[8:16], "space", EAST)
    from_east = lax.ppermute(edges[0:8], "space", WEST)

    letter = jnp.concatenate([by_column(kernel_first), moments], axis=0)
    got = lax.all_to_all(
        jnp.broadcast_to(letter[None], (NZ, 208, 128)), "space", 0, 0, tiled=True, axis_index_groups=ALONG_Z
    )
    from_north = lax.ppermute(edge_row(placed[280:320], from_west[7:8], from_east[7:8]), "space", SOUTH)
    from_south = lax.ppermute(edge_row(placed[0:40], from_west[0:1], from_east[0:1]), "space", NORTH)
    parcel = jnp.concatenate([placed, from_west, from_east, from_north, from_south], axis=0)
    frames = lax.all_gather(parcel, "tm")

    ordered = call(arrange_first, shape((NX, 160, 1152), BF), [], 0, got, jnp.asarray(FIRST_ROWS, BF))
    own = lax.all_to_all(ordered, "space", 0, 0, tiled=True, axis_index_groups=ALONG_X)
    other = lax.ppermute(own, "space", SIBLING)
    all_moments = lax.all_gather(own[:, 144:160, 0:128], BOTH, axis_index_groups=Y_CORE)

    swapped, all_moments = lax.optimization_barrier((swapped, all_moments))
    got_second = lax.all_to_all(
        jnp.broadcast_to(swapped[None], (NZ, 192, 128)), "space", 0, 0, tiled=True, axis_index_groups=ALONG_Z
    )
    ordered_second = call(
        arrange_second,
        shape((432, CH), BF),
        [],
        0,
        got_second,
        jnp.asarray(SECOND_ROWS, BF),
        jnp.asarray(SECOND_LANES, BF),
    )
    own_second = lax.all_gather(ordered_second, "space", axis_index_groups=ALONG_X)
    other_second = lax.ppermute(own_second, "space", SIBLING)

    def part_of(vector):
        mine = lax.dynamic_slice(vector, (frame * PART,), (PART,))
        return jnp.pad(mine, (0, 128 - PART))[None]

    field, west, east, sums = call(
        first_conv,
        (
            shape((NY, ROWS, PITCH, 128), F32),
            shape((NY, ROWS, 128), F32),
            shape((NY, ROWS, 128), F32),
            shape((SPACE, 256), F32),
        ),
        [
            pltpu.VMEM((3 * CH, 9 * 128), BF),
            pltpu.VMEM((GUARD + FLAT + GUARD, CH), F32),
            pltpu.VMEM((NY, FLAT, 3 * CH), BF),
        ],
        1,
        pos,
        frames,
        own,
        other,
        all_moments,
        gain_first[None],
        shift_first[None],
        part_of(bias_first),
        jnp.asarray(CHANNEL_LANES),
        jnp.asarray(GROUPS_OF_LANES.T),
        jnp.asarray(PART_GROUPS),
        jnp.asarray(PART_GROUPS.T),
    )
    west_side = lax.ppermute(east, "space", EAST)
    east_side = lax.ppermute(west, "space", WEST)
    north_side = lax.ppermute(
        edge_row(field[:, 7, :WIDE], west_side[:, 7:8], east_side[:, 7:8]), "space", SOUTH
    )
    south_side = lax.ppermute(
        edge_row(field[:, 0, :WIDE], west_side[:, 0:1], east_side[:, 0:1]), "space", NORTH
    )
    all_sums = lax.all_to_all(sums, "space", 0, 0, tiled=True)
    partial = call(
        second_conv,
        shape((NY, ROWS, WIDE, CH), BF),
        [
            pltpu.VMEM((27 * 128, CH), BF),
            pltpu.VMEM((GUARD + FLAT + GUARD, 128), F32),
            pltpu.VMEM((NY, 384, 9 * 128), BF),
        ],
        1,
        pos,
        field,
        west_side,
        east_side,
        north_side,
        south_side,
        all_sums,
        part_of(gain_second),
        part_of(shift_second),
        own_second,
        other_second,
        jnp.asarray(PART_GROUPS.T),
        jnp.asarray(PART_LANES, BF),
    )
    parts = lax.all_to_all(partial, "tm", 0, 0, tiled=True)
    second_out = jnp.sum(parts.astype(F32), axis=0) + bias_second
    return (tile.astype(F32) + second_out).astype(BF)[None, None]


def solution(mesh):
    placed = (
        P("tm", "space", None, None, None),
        P(),
        P(),
        P(None, None, None, "space", "tm"),
        P(),
        P(),
        P(),
        P(None, None, None, "space", "tm"),
        P(),
    )
    return jax.shard_map(
        shards,
        mesh=mesh,
        in_specs=placed,
        out_specs=P("tm", "space", None, None, None),
        check_vma=False,
    )
```

```python
import functools

import jax
import jax.numpy as jnp
import numpy as np
from jax import lax
from jax.experimental import pallas as pl
from jax.experimental.pallas import tpu as pltpu
from jax.sharding import PartitionSpec as P

EPS = 1e-06
BF = jnp.bfloat16
F32 = jnp.float32
VM = pl.BlockSpec(memory_space=pltpu.VMEM)
SM = pl.BlockSpec(memory_space=pltpu.SMEM)
HIGH = lax.Precision.HIGHEST

NZ, NX, NC, NY = 8, 4, 2, 4
COLS = NX * NC
SPACE = NZ * COLS
ROWS, WIDE, PITCH = 8, 40, 48
CH, PART, WG = 384, 96, 12
FLAT = (ROWS + 2) * PITCH
GUARD = 16
BOTH = ("tm", "space")
ALONG_Z = [[z * COLS + q for z in range(NZ)] for q in range(COLS)]
ALONG_X = [[z * COLS + x * NC + c for x in range(NX)] for z in range(NZ) for c in range(NC)]
Y_CORE = [
    [y * SPACE + z * COLS + x * NC + c for y in range(NY) for c in range(NC)]
    for z in range(NZ)
    for x in range(NX)
]
SIBLING = [(s, s ^ 1) for s in range(SPACE)]


def moved(down, right):
    return [(s, (s + COLS * down + right) % SPACE) for s in range(SPACE)]


SWAP = [
    (y * SPACE + z * COLS + q, (z // 2) * SPACE + (2 * y + z % 2) * COLS + q)
    for y in range(NY)
    for z in range(NZ)
    for q in range(COLS)
]


def one_hot(rows, cols, pairs):
    out = np.zeros((rows, cols), np.float32)
    for r, c in pairs:
        out[r, c] = 1.0
    return out


CHANNEL_LANES = one_hot(
    CH, CH, [(6 * (8 * z + q) + i, 48 * q + 6 * z + i) for z in range(8) for q in range(8) for i in range(6)]
)
GROUPS_OF = one_hot(CH, 128, [(c, c // WG) for c in range(CH)])
SQUARES_OF = np.roll(GROUPS_OF, 64, axis=1)
GROUPS_OF_LANES = (CHANNEL_LANES.T @ GROUPS_OF).T
SQUARES_OF_LANES = (CHANNEL_LANES.T @ SQUARES_OF).T
PART_GROUPS = one_hot(128, 128, [(c, c // WG) for c in range(PART)])
PART_SQUARES = np.roll(PART_GROUPS, 64, axis=1)
CORNERS = ((0, 0), (0, WIDE - 1), (ROWS - 1, 0), (ROWS - 1, WIDE - 1))
EDGES = one_hot(
    48,
    320,
    [(r, 40 * r) for r in range(8)]
    + [(8 + r, 40 * r + 39) for r in range(8)]
    + [(16 + 8 * n, 40 * r + c) for n, (r, c) in enumerate(CORNERS)],
)
FIRST_ROWS = one_hot(
    432, 512, [(48 * k + 6 * z + i, 64 * z + 6 * k + i) for k in range(9) for z in range(8) for i in range(6)]
)
SECOND_ROWS = one_hot(
    144, 128, [(16 * k + 6 * h + i, 64 * h + 6 * k + i) for k in range(9) for h in range(2) for i in range(6)]
)
SECOND_LANES = one_hot(512, CH, [(128 * y + o, PART * y + o) for y in range(4) for o in range(PART)])
PART_LANES = one_hot(
    128, 128, [(48 * h + 6 * q + i, 16 * q + 6 * h + i) for h in range(2) for q in range(8) for i in range(6)]
)


def dot(a, b):
    return jnp.dot(a, b, preferred_element_type=F32)


def exact(a, b):
    return jnp.dot(a, b, preferred_element_type=F32, precision=HIGH)


def merge(sums, count, groups_t, squares_t):
    mean = jnp.mean(sums, axis=0, keepdims=True)
    off = sums - mean
    between = count * jnp.sum(off * off, axis=0, keepdims=True)
    within = jnp.sum(sums, axis=0, keepdims=True)
    rows = jnp.concatenate([mean, between, jnp.zeros((6, 128), F32)], axis=0)
    by_lane = exact(rows, groups_t)
    spread = (by_lane[1:2] + exact(tall(within), squares_t)[0:1]) * (1.0 / (count * sums.shape[0]))
    return by_lane[0:1], lax.rsqrt(spread + EPS)


def split_rows(row):
    hi = row.astype(BF).astype(F32)
    mid = (row - hi).astype(BF).astype(F32)
    return jnp.concatenate([hi, mid, row - hi - mid, jnp.zeros((13, 128), F32)], axis=0).astype(BF)


def pool(blocks, count):
    wide = [b.astype(F32) for b in blocks]
    rows = jnp.concatenate([b[0:1] + b[1:2] + b[2:3] for b in wide], axis=0)
    mean = jnp.mean(rows, axis=0, keepdims=True)
    off = rows - mean
    between = count * jnp.sum(off * off, axis=0, keepdims=True)
    squares = jnp.sum(rows, axis=0, keepdims=True) + pltpu.roll(tall(between), 64, axis=1)[0:1]
    return jnp.where(lax.broadcasted_iota(jnp.int32, (1, 128), 1) < 64, mean, squares)


def tall(row):
    return jnp.broadcast_to(row, (8, row.shape[1]))


def chosen(part):
    channel = lax.broadcasted_iota(jnp.int32, (CH, 128), 0)
    lane = lax.broadcasted_iota(jnp.int32, (CH, 128), 1)
    return ((channel == part * PART + lane) & (lane < PART)).astype(F32)


def silu(u):
    return u / (1.0 + jnp.exp(-u))


def measure_tile(
    tile_ref, lanes_ref, groups_ref, groups_t_ref, squares_ref, edges_ref,
    placed_ref, west_ref, east_ref, nw_ref, ne_ref, sw_ref, se_ref, sums_ref,
):
    tile = tile_ref[...]
    placed = dot(tile, lanes_ref[...]).astype(BF)
    placed_ref[...] = placed
    edges = dot(edges_ref[...], placed).astype(BF)
    for n, ref in enumerate((west_ref, east_ref, nw_ref, ne_ref, sw_ref, se_ref)):
        ref[...] = edges[8 * n : 8 * n + 8]
    wide = tile.astype(F32)
    mean = exact(tall(jnp.sum(wide, axis=0, keepdims=True)), groups_ref[...]) * (1.0 / (320 * WG))
    off = wide - exact(mean, groups_t_ref[...])[0:1]
    squares = exact(tall(jnp.sum(off * off, axis=0, keepdims=True)), squares_ref[...])
    sums_ref[...] = split_rows((mean + squares)[0:1])


def gather_sums(own_ref, out_ref):
    out_ref[...] = tall(pool([own_ref[x] for x in range(NX)], 320.0 * WG * NZ))


def arrange_first(got_ref, rows_ref, out_ref):
    parts = [
        jnp.concatenate([got_ref[z, 64 * d : 64 * d + 64, :] for z in range(NZ)], axis=0) for d in range(3)
    ]
    ordered = dot(rows_ref[...], jnp.concatenate(parts, axis=1)).astype(BF)
    sums = split_rows(pool([got_ref[z, 384:400, :] for z in range(NZ)], 320.0 * WG))
    for copy in range(NX):
        out_ref[copy, 144:160, 0:128] = sums
        out_ref[copy, 144:160, 128:] = jnp.zeros((16, 1024), BF)
        for d in range(3):
            for k in range(9):
                out_ref[copy, 48 * d : 48 * d + 48, 128 * k : 128 * k + 128] = ordered[
                    48 * k : 48 * k + 48, 128 * d : 128 * d + 128
                ]


def arrange_second(got_ref, rows_ref, lanes_ref, out_ref):
    by_part = []
    for y in range(NY):
        parts = [
            jnp.concatenate([got_ref[2 * y + h, 192 + 64 * d : 256 + 64 * d, :] for h in range(2)], axis=0)
            for d in range(3)
        ]
        by_part.append(dot(rows_ref[...], jnp.concatenate(parts, axis=1)).astype(BF))
    tall_parts = [
        jnp.concatenate([by_part[y][:, 128 * d : 128 * d + 128] for y in range(NY)], axis=1) for d in range(3)
    ]
    out_ref[...] = dot(jnp.concatenate(tall_parts, axis=0), lanes_ref[...]).astype(BF)


def first_act(
    pos_ref, lat_ref, sums_ref, vectors_ref, lanes_ref, groups_t_ref, squares_t_ref, stack, flat
):
    row, col = pos_ref[0] // COLS, pos_ref[0] % COLS
    mean_l, scale_l = merge(sums_ref[...], 320.0 * WG * NZ * NX, groups_t_ref[...], squares_t_ref[...])
    affine = exact(vectors_ref[...], lanes_ref[...])
    scale_l = scale_l * affine[0:1]
    shift_l = affine[1:2]
    has_w = (col > 0).astype(F32)
    has_e = (col < COLS - 1).astype(F32)
    has_n = (row > 0).astype(F32)
    has_s = (row < NZ - 1).astype(F32)
    flat[...] = jnp.zeros_like(flat)
    for t in range(NY):
        act = silu((lat_ref[t].astype(F32) - mean_l) * scale_l + shift_l)
        base = GUARD
        flat[base : base + WIDE, :] = act[336:376] * has_n
        flat[base - 1 : base, :] = act[416:417] * (has_n * has_w)
        flat[base + WIDE : base + WIDE + 1, :] = act[424:425] * (has_n * has_e)
        for r in range(ROWS):
            base = GUARD + PITCH * (r + 1)
            flat[base : base + WIDE, :] = act[WIDE * r : WIDE * r + WIDE]
            flat[base + WIDE : base + WIDE + 1, :] = act[328 + r : 329 + r] * has_e
            flat[base - 1 : base, :] = act[320 + r : 321 + r] * has_w
        base = GUARD + PITCH * (ROWS + 1)
        flat[base : base + WIDE, :] = act[376:416] * has_s
        flat[base - 1 : base, :] = act[432:433] * (has_s * has_w)
        flat[base + WIDE : base + WIDE + 1, :] = act[440:441] * (has_s * has_e)
        for d in range(3):
            stack[t, :, CH * d : CH * d + CH] = flat[GUARD + d - 1 : GUARD + d - 1 + FLAT, :].astype(BF)


def first_conv(
    pos_ref, stack, own_ref, other_ref, vectors_ref, part_ref, part_t_ref, part_squares_ref,
    out_ref, west_ref, east_ref, north_ref, south_ref, nw_ref, ne_ref, sw_ref, se_ref, sums_ref, weights,
):
    core = pos_ref[0] % NC
    bias = exact(vectors_ref[...], chosen(pos_ref[1]))[2:3]
    for mine in range(NC):

        @pl.when(core == mine)
        def _():
            for x in range(NX):
                for d in range(3):
                    at = CH * d + 48 * (NC * x + mine)
                    weights[at : at + 48, :] = own_ref[x, 48 * d : 48 * d + 48, :]
                    at = CH * d + 48 * (NC * x + 1 - mine)
                    weights[at : at + 48, :] = other_ref[x, 48 * d : 48 * d + 48, :]

    totals = [None] * NY
    for t in range(NY):
        for dt in range(3):
            to = t + 2 - dt
            if to >= NY:
                continue
            part = dot(stack[t], weights[:, CH * dt : CH * dt + CH])
            term = part[0:384, 0:128] + part[48:432, 128:256] + part[96:480, 256:384]
            totals[to] = term if totals[to] is None else totals[to] + term
    inside = (lax.broadcasted_iota(jnp.int32, (384, 1), 0) % PITCH < WIDE).astype(F32)
    sums = None
    for t in range(NY):
        totals[t] = totals[t] + bias
        line = jnp.sum(totals[t] * inside, axis=0, keepdims=True)
        sums = line if sums is None else sums + line
        for r in range(ROWS):
            out_ref[t, r] = totals[t][PITCH * r : PITCH * r + PITCH]
            west_ref[t, r : r + 1, :] = totals[t][PITCH * r : PITCH * r + 1]
            east_ref[t, r : r + 1, :] = totals[t][PITCH * r + WIDE - 1 : PITCH * r + WIDE]
        north_ref[t] = totals[t][0:WIDE]
        south_ref[t] = totals[t][PITCH * (ROWS - 1) : PITCH * (ROWS - 1) + WIDE]
        for ref, (r, c) in zip((nw_ref, ne_ref, sw_ref, se_ref), CORNERS):
            ref[t : t + 1, :] = totals[t][PITCH * r + c : PITCH * r + c + 1]
    mean = exact(tall(sums), part_ref[...]) * (1.0 / (320 * NY * WG))
    mean_l = exact(mean, part_t_ref[...])[0:1]
    sums = None
    for t in range(NY):
        off = (totals[t] - mean_l) * inside
        line = jnp.sum(off * off, axis=0, keepdims=True)
        sums = line if sums is None else sums + line
    squares = exact(tall(sums), part_squares_ref[...])
    sums_ref[...] = jnp.broadcast_to((mean + squares)[0:1], (SPACE, 128))


def assemble_second(pos_ref, own_ref, other_ref, weights):
    core = pos_ref[0] % NC
    for mine in range(NC):

        @pl.when(core == mine)
        def _():
            for x in range(NX):
                for d in range(3):
                    for k in range(9):
                        tap = 9 * (k // 3) + 3 * (k % 3) + d
                        source = 144 * d + 16 * k
                        at = 128 * tap + 16 * (NC * x + mine)
                        weights[at : at + 16, :] = own_ref[x, source : source + 16, :]
                        at = 128 * tap + 16 * (NC * x + 1 - mine)
                        weights[at : at + 16, :] = other_ref[x, source : source + 16, :]


def second_conv(
    pos_ref, field_ref, west_ref, east_ref, north_ref, south_ref, nw_ref, ne_ref, sw_ref, se_ref, sums_ref,
    vectors_ref, weights,
    groups_t_ref, squares_t_ref, order_ref, out_ref, flat, stack,
):
    row, col = pos_ref[0] // COLS, pos_ref[0] % COLS
    mean_l, scale_l = merge(sums_ref[...], 320.0 * NY * WG, groups_t_ref[...], squares_t_ref[...])
    affine = exact(vectors_ref[...], chosen(pos_ref[1]))
    scale_l = scale_l * affine[3:4]
    shift_l = affine[4:5]

    def act_of(v):
        act = silu((v - mean_l) * scale_l + shift_l).astype(BF)
        return dot(act, order_ref[...])

    has_w = (col > 0).astype(F32)
    has_e = (col < COLS - 1).astype(F32)
    has_n = (row > 0).astype(F32)
    has_s = (row < NZ - 1).astype(F32)
    flat[...] = jnp.zeros_like(flat)
    nw, ne = act_of(nw_ref[...]) * (has_n * has_w), act_of(ne_ref[...]) * (has_n * has_e)
    sw, se = act_of(sw_ref[...]) * (has_s * has_w), act_of(se_ref[...]) * (has_s * has_e)
    for t in range(NY):
        left, right = act_of(west_ref[t]) * has_w, act_of(east_ref[t]) * has_e
        base = GUARD
        flat[base : base + WIDE, :] = act_of(north_ref[t]) * has_n
        flat[base - 1 : base, :] = nw[t : t + 1]
        flat[base + WIDE : base + WIDE + 1, :] = ne[t : t + 1]
        for r in range(ROWS):
            base = GUARD + PITCH * (r + 1)
            flat[base : base + WIDE, :] = act_of(field_ref[t, r])[0:WIDE]
            flat[base + WIDE : base + WIDE + 1, :] = right[r : r + 1]
            flat[base - 1 : base, :] = left[r : r + 1]
        base = GUARD + PITCH * (ROWS + 1)
        flat[base : base + WIDE, :] = act_of(south_ref[t]) * has_s
        flat[base - 1 : base, :] = sw[t : t + 1]
        flat[base + WIDE : base + WIDE + 1, :] = se[t : t + 1]
        for dy in range(3):
            for dx in range(3):
                start = GUARD + PITCH * dy + dx - 1
                lane = 128 * (3 * dy + dx)
                stack[t, :, lane : lane + 128] = flat[start : start + 384, :].astype(BF)
    for t in range(NY):
        total = None
        for dt in range(3):
            source = t - 2 + dt
            if source < 0:
                continue
            term = dot(stack[source], weights[1152 * dt : 1152 * dt + 1152, :])
            total = term if total is None else total + term
        for r in range(ROWS):
            out_ref[t, r] = total[PITCH * r : PITCH * r + WIDE].astype(BF)


def call(body, outs, scratch, smem, *args):
    return pl.pallas_call(
        body,
        out_shape=outs,
        in_specs=[SM] * smem + [VM] * (len(args) - smem),
        out_specs=jax.tree.map(lambda _: VM, outs),
        scratch_shapes=scratch,
        compiler_params=pltpu.CompilerParams(vmem_limit_bytes=56 * 1024 * 1024),
    )(*args)


def shape(dims, dtype):
    return jax.ShapeDtypeStruct(dims, dtype)


def neighbours(west, east, north, south, nw, ne, sw, se):
    send = functools.partial(lax.ppermute, axis_name="space")
    return (
        send(east, perm=moved(0, 1)),
        send(west, perm=moved(0, -1)),
        send(south, perm=moved(1, 0)),
        send(north, perm=moved(-1, 0)),
        send(se, perm=moved(1, 1)),
        send(sw, perm=moved(1, -1)),
        send(ne, perm=moved(-1, 1)),
        send(nw, perm=moved(-1, -1)),
    )


def by_column(kernel):
    rows = jnp.transpose(kernel, (2, 0, 1, 3, 4)).reshape(3, 54, PART)
    return jnp.pad(rows, ((0, 0), (0, 10), (0, 32))).reshape(192, 128)


def shards(
    latents,
    gain_first,
    shift_first,
    kernel_first,
    bias_first,
    gain_second,
    shift_second,
    kernel_second,
    bias_second,
):
    space = lax.axis_index("space")
    frame = lax.axis_index("tm")
    pos = jnp.stack([space, frame]).astype(jnp.int32)
    vectors = jnp.stack(
        [gain_first, shift_first, bias_first, gain_second, shift_second, bias_second, bias_second, bias_second]
    )
    tile = latents[0, 0]
    flat_tile = tile.reshape(ROWS * WIDE, CH)

    swapped = lax.ppermute(by_column(kernel_second), BOTH, SWAP)
    small = shape((8, CH), BF)
    placed, west, east, nw, ne, sw, se, sums = call(
        measure_tile,
        (shape((320, CH), BF), small, small, small, small, small, small, shape((16, 128), BF)),
        [],
        0,
        flat_tile,
        jnp.asarray(CHANNEL_LANES, BF),
        jnp.asarray(GROUPS_OF),
        jnp.asarray(GROUPS_OF.T),
        jnp.asarray(SQUARES_OF),
        jnp.asarray(EDGES, BF),
    )
    letter = jnp.concatenate([by_column(kernel_first), swapped, sums], axis=0)
    got = lax.all_to_all(
        jnp.broadcast_to(letter[None], (NZ, 400, 128)), "space", 0, 0, tiled=True, axis_index_groups=ALONG_Z
    )
    around = neighbours(west, east, placed[0:40], placed[280:320], nw, ne, sw, se)
    parcel = jnp.concatenate([placed, *around], axis=0)
    frames = lax.all_gather(parcel, "tm")
    got, _ = lax.optimization_barrier((got, parcel))

    ordered = call(arrange_first, shape((NX, 160, 1152), BF), [], 0, got, jnp.asarray(FIRST_ROWS, BF))
    own = lax.all_to_all(ordered, "space", 0, 0, tiled=True, axis_index_groups=ALONG_X)
    x_sums = pl.pallas_call(
        gather_sums,
        grid=(1,),
        in_specs=[pl.BlockSpec((NX, 16, 128), lambda i: (0, 9, 0))],
        out_specs=pl.BlockSpec((8, 128), lambda i: (0, 0)),
        out_shape=shape((8, 128), F32),
    )(own)
    all_sums = lax.all_to_all(x_sums, BOTH, 0, 0, tiled=True, axis_index_groups=Y_CORE)
    got_second, _ = lax.optimization_barrier((got, own))
    stack = call(
        first_act,
        shape((NY, FLAT, 3 * CH), BF),
        [pltpu.VMEM((GUARD + FLAT + GUARD, CH), F32)],
        1,
        pos,
        frames,
        all_sums,
        vectors,
        jnp.asarray(CHANNEL_LANES),
        jnp.asarray(GROUPS_OF_LANES),
        jnp.asarray(SQUARES_OF_LANES),
    )
    other = lax.ppermute(own, "space", SIBLING)

    ordered_second = call(
        arrange_second,
        shape((432, CH), BF),
        [],
        0,
        got_second,
        jnp.asarray(SECOND_ROWS, BF),
        jnp.asarray(SECOND_LANES, BF),
    )
    stack, _ = lax.optimization_barrier((stack, ordered_second))
    cells = shape((8, 128), F32)
    field, *edges, sums = call(
        first_conv,
        (
            shape((NY, ROWS, PITCH, 128), F32),
            shape((NY, ROWS, 128), F32),
            shape((NY, ROWS, 128), F32),
            shape((NY, WIDE, 128), F32),
            shape((NY, WIDE, 128), F32),
            cells,
            cells,
            cells,
            cells,
            shape((SPACE, 128), F32),
        ),
        [pltpu.VMEM((3 * CH, 9 * 128), BF)],
        1,
        pos,
        stack,
        own,
        other,
        vectors,
        jnp.asarray(PART_GROUPS),
        jnp.asarray(PART_GROUPS.T),
        jnp.asarray(PART_SQUARES),
    )
    around = neighbours(*edges)
    own_second = lax.all_gather(ordered_second, "space", axis_index_groups=ALONG_X)
    own_second, _ = lax.optimization_barrier((own_second, around[0]))
    other_second = lax.ppermute(own_second, "space", SIBLING)
    weights_second = call(assemble_second, shape((27 * 128, CH), BF), [], 1, pos, own_second, other_second)
    all_sums = lax.all_to_all(sums, "space", 0, 0, tiled=True)
    partial = call(
        second_conv,
        shape((NY, ROWS, WIDE, CH), BF),
        [
            pltpu.VMEM((GUARD + FLAT + GUARD, 128), F32),
            pltpu.VMEM((NY, 384, 9 * 128), BF),
        ],
        1,
        pos,
        field,
        *around,
        all_sums,
        vectors,
        weights_second,
        jnp.asarray(PART_GROUPS.T),
        jnp.asarray(PART_SQUARES.T),
        jnp.asarray(PART_LANES, BF),
    )
    parts = lax.all_to_all(partial, "tm", 0, 0, tiled=True)
    second_out = jnp.sum(parts.astype(F32), axis=0) + bias_second
    return (tile.astype(F32) + second_out).astype(BF)[None, None]


def solution(mesh):
    placed = (
        P("tm", "space", None, None, None),
        P(),
        P(),
        P(None, None, None, "space", "tm"),
        P(),
        P(),
        P(),
        P(None, None, None, "space", "tm"),
        P(),
    )
    return jax.shard_map(
        shards,
        mesh=mesh,
        in_specs=placed,
        out_specs=P("tm", "space", None, None, None),
        check_vma=False,
    )
```

```python
import functools

import jax
import jax.numpy as jnp
import numpy as np
from jax import lax
from jax.experimental import pallas as pl
from jax.experimental.pallas import tpu as pltpu
from jax.sharding import PartitionSpec as P

EPS = 1e-06
BF = jnp.bfloat16
F32 = jnp.float32
VM = pl.BlockSpec(memory_space=pltpu.VMEM)
SM = pl.BlockSpec(memory_space=pltpu.SMEM)
HIGH = lax.Precision.HIGHEST

NZ, NX, NC, NY = 8, 4, 2, 4
COLS = NX * NC
SPACE = NZ * COLS
ROWS, WIDE, PITCH = 8, 40, 48
CH, PART, WG = 384, 96, 12
GUARD = 16
LEAD = 8
RING = LEAD + (ROWS + 2) * PITCH + 8
FIELD = RING + 2 * PITCH
BOTH = ("tm", "space")
ALONG_Z = [[z * COLS + q for z in range(NZ)] for q in range(COLS)]
ALONG_X = [[z * COLS + x * NC + c for x in range(NX)] for z in range(NZ) for c in range(NC)]
PLANE = [[y * SPACE + z * COLS + q for y in range(NY) for q in range(COLS)] for z in range(NZ)]
SIBLING = [(s, s ^ 1) for s in range(SPACE)]


def moved(down, right):
    return [(s, (s + COLS * down + right) % SPACE) for s in range(SPACE)]


SWAP = [
    (y * SPACE + z * COLS + q, (z // 2) * SPACE + (2 * y + z % 2) * COLS + q)
    for y in range(NY)
    for z in range(NZ)
    for q in range(COLS)
]


def one_hot(rows, cols, pairs):
    out = np.zeros((rows, cols), np.float32)
    for r, c in pairs:
        out[r, c] = 1.0
    return out


CHANNEL_LANES = one_hot(
    CH, CH, [(6 * (8 * z + q) + i, 48 * q + 6 * z + i) for z in range(8) for q in range(8) for i in range(6)]
)
GROUPS_OF = one_hot(CH, 128, [(c, c // WG) for c in range(CH)])
SQUARES_OF = np.roll(GROUPS_OF, 64, axis=1)
GROUPS_OF_LANES = (CHANNEL_LANES.T @ GROUPS_OF).T
SQUARES_OF_LANES = (CHANNEL_LANES.T @ SQUARES_OF).T
PART_GROUPS = one_hot(128, 128, [(c, c // WG) for c in range(PART)])
PART_SQUARES = np.roll(PART_GROUPS, 64, axis=1)
EDGES = one_hot(
    32,
    320,
    [(2 * r + c, 40 * r + c) for r in range(8) for c in range(2)]
    + [(16 + 2 * r + c, 40 * r + 38 + c) for r in range(8) for c in range(2)],
)
FIRST_ROWS = one_hot(
    336, 384, [(48 * g + 6 * z + i, 48 * z + 6 * g + i) for g in range(7) for z in range(8) for i in range(6)]
)
SECOND_ROWS = one_hot(
    144, 128, [(16 * k + 6 * h + i, 64 * h + 6 * k + i) for k in range(9) for h in range(2) for i in range(6)]
)
SECOND_LANES = one_hot(512, CH, [(128 * y + o, PART * y + o) for y in range(4) for o in range(PART)])
PART_LANES = one_hot(
    128, 128, [(48 * h + 6 * q + i, 16 * q + 6 * h + i) for h in range(2) for q in range(8) for i in range(6)]
)


def dot(a, b):
    return jnp.dot(a, b, preferred_element_type=F32)


def exact(a, b):
    return jnp.dot(a, b, preferred_element_type=F32, precision=HIGH)


def merge(sums, count, groups_t, squares_t):
    mean = jnp.mean(sums, axis=0, keepdims=True)
    off = sums - mean
    between = count * jnp.sum(off * off, axis=0, keepdims=True)
    within = jnp.sum(sums, axis=0, keepdims=True)
    rows = jnp.concatenate([mean, between, jnp.zeros((6, 128), F32)], axis=0)
    by_lane = exact(rows, groups_t)
    spread = (by_lane[1:2] + exact(tall(within), squares_t)[0:1]) * (1.0 / (count * sums.shape[0]))
    return by_lane[0:1], lax.rsqrt(spread + EPS)


def pool(rows, count):
    mean = jnp.mean(rows, axis=0, keepdims=True)
    off = rows - mean
    between = count * jnp.sum(off * off, axis=0, keepdims=True)
    squares = jnp.sum(rows, axis=0, keepdims=True) + pltpu.roll(tall(between), 64, axis=1)[0:1]
    return jnp.where(lax.broadcasted_iota(jnp.int32, (1, 128), 1) < 64, mean, squares)


def tall(row):
    return jnp.broadcast_to(row, (8, row.shape[1]))


def chosen(part):
    channel = lax.broadcasted_iota(jnp.int32, (CH, 128), 0)
    lane = lax.broadcasted_iota(jnp.int32, (CH, 128), 1)
    return ((channel == part * PART + lane) & (lane < PART)).astype(F32)


def silu(u):
    return u / (1.0 + jnp.exp(-u))


def measure_tile(
    tile_ref, lanes_ref, groups_ref, groups_t_ref, squares_ref, edges_ref,
    placed_ref, west_ref, east_ref, sums_ref,
):
    tile = tile_ref[...]
    placed = dot(tile, lanes_ref[...]).astype(BF)
    placed_ref[...] = placed
    edges = dot(edges_ref[...], placed).astype(BF)
    west_ref[...] = edges[0:16]
    east_ref[...] = edges[16:32]
    wide = tile.astype(F32)
    mean = exact(tall(jnp.sum(wide, axis=0, keepdims=True)), groups_ref[...]) * (1.0 / (320 * WG))
    off = wide - exact(mean, groups_t_ref[...])[0:1]
    squares = exact(tall(jnp.sum(off * off, axis=0, keepdims=True)), squares_ref[...])
    sums_ref[...] = jnp.broadcast_to((mean + squares)[0:1], sums_ref.shape)


def pool_plane(sums_ref, out_ref):
    row = pool(sums_ref[...], 320.0 * WG)
    hi = row.astype(BF).astype(F32)
    mid = (row - hi).astype(BF).astype(F32)
    rows = jnp.concatenate([hi, mid, row - hi - mid, jnp.zeros((5, 128), F32)], axis=0)
    out_ref[...] = jnp.concatenate([rows, jnp.zeros((8, CH - 128), F32)], axis=1).astype(BF)


def arrange_first(got_ref, rows_ref, out_ref, sums_ref):
    blocks = [got_ref[z, 0:48, :] for z in range(NZ)]
    ordered = dot(rows_ref[...], jnp.concatenate(blocks, axis=0)).astype(BF)
    for copy in range(NX):
        out_ref[copy] = ordered
    wide = [b[:, 0:128].astype(F32) for b in blocks]
    sums_ref[...] = jnp.concatenate([b[42:43] + b[43:44] + b[44:45] for b in wide], axis=0)


def arrange_second(got_ref, rows_ref, lanes_ref, out_ref):
    by_part = []
    for y in range(NY):
        pair = jnp.concatenate([got_ref[2 * y + h, 48:112, :] for h in range(2)], axis=0)
        by_part.append(dot(rows_ref[...], pair).astype(BF))
    tall_parts = [
        jnp.concatenate([by_part[y][:, 128 * d : 128 * d + 128] for y in range(NY)], axis=1) for d in range(3)
    ]
    out_ref[...] = dot(jnp.concatenate(tall_parts, axis=0), lanes_ref[...]).astype(BF)


def first_act(
    pos_ref, lat_ref, sums_ref, vectors_ref, lanes_ref, groups_t_ref, squares_t_ref, stack, flat
):
    row, col = pos_ref[0] // COLS, pos_ref[0] % COLS
    mean_l, scale_l = merge(sums_ref[...], 320.0 * WG * NY * COLS, groups_t_ref[...], squares_t_ref[...])
    affine = exact(vectors_ref[...], lanes_ref[...])
    scale_l = scale_l * affine[0:1]
    shift_l = affine[1:2]
    has_w = (col > 0).astype(F32)
    has_e = (col < COLS - 1).astype(F32)
    has_n = (row > 0).astype(F32)
    has_s = (row < NZ - 1).astype(F32)
    flat[...] = jnp.zeros_like(flat)
    for t in range(NY):
        act = silu((lat_ref[t].astype(F32) - mean_l) * scale_l + shift_l)
        for r in range(-2, ROWS + 2):
            base = GUARD + PITCH * (r + 2)
            if 0 <= r < ROWS:
                cells = act[WIDE * r : WIDE * r + WIDE]
                left, right = act[320 + 2 * r : 322 + 2 * r] * has_w, act[336 + 2 * r : 338 + 2 * r] * has_e
            else:
                start, at, inside = (352, r + 2, has_n) if r < 0 else (440, r - ROWS, has_s)
                cells = act[start + WIDE * at : start + WIDE * at + WIDE] * inside
                left = act[start + 80 + 2 * at : start + 82 + 2 * at] * (inside * has_w)
                right = act[start + 84 + 2 * at : start + 86 + 2 * at] * (inside * has_e)
            flat[base : base + WIDE, :] = cells
            flat[base + WIDE : base + WIDE + 2, :] = right
            flat[base - 2 : base, :] = left
        for d in range(3):
            start = GUARD - LEAD + d - 1
            stack[t, :, CH * d : CH * d + CH] = flat[start : start + FIELD, :].astype(BF)


def first_conv(
    pos_ref, stack, own_ref, other_ref, vectors_ref, part_ref, part_t_ref, part_squares_ref, spread_ref,
    out_ref, sums_ref, packed, weights,
):
    core = pos_ref[0] % NC
    bias = exact(vectors_ref[...], chosen(pos_ref[1]))[2:3]
    for mine in range(NC):

        @pl.when(core == mine)
        def _():
            for x in range(NX):
                for g in range(7):
                    at = 48 * (NC * x + mine)
                    packed[g, at : at + 48, :] = own_ref[x, 48 * g : 48 * g + 48, :]
                    at = 48 * (NC * x + 1 - mine)
                    packed[g, at : at + 48, :] = other_ref[x, 48 * g : 48 * g + 48, :]

    for g in range(7):
        taps = dot(packed[g], spread_ref[...]).astype(BF)
        for tap in range(4 * g, min(4 * g + 4, 27)):
            down, right = CH * (tap % 3), 128 * (tap // 3)
            weights[down : down + CH, right : right + 128] = taps[:, 128 * (tap % 4) : 128 * (tap % 4) + 128]
    totals = [None] * NY
    for t in range(NY):
        for dt in range(3):
            to = t + 2 - dt
            if to >= NY:
                continue
            part = dot(stack[t], weights[:, CH * dt : CH * dt + CH])
            term = part[0:RING, 0:128]
            for dy in (1, 2):
                term = term + part[PITCH * dy : PITCH * dy + RING, 128 * dy : 128 * dy + 128]
            totals[to] = term if totals[to] is None else totals[to] + term
    at = lax.broadcasted_iota(jnp.int32, (RING, 1), 0) - (LEAD + PITCH)
    inside = ((at >= 0) & (at < PITCH * ROWS) & (at % PITCH < WIDE)).astype(F32)
    sums = None
    for t in range(NY):
        totals[t] = totals[t] + bias
        out_ref[t] = totals[t]
        line = jnp.sum(totals[t] * inside, axis=0, keepdims=True)
        sums = line if sums is None else sums + line
    mean = exact(tall(sums), part_ref[...]) * (1.0 / (320 * NY * WG))
    mean_l = exact(mean, part_t_ref[...])[0:1]
    sums = None
    for t in range(NY):
        off = (totals[t] - mean_l) * inside
        line = jnp.sum(off * off, axis=0, keepdims=True)
        sums = line if sums is None else sums + line
    squares = exact(tall(sums), part_squares_ref[...])
    sums_ref[...] = jnp.broadcast_to((mean + squares)[0:1], (SPACE, 128))


def assemble_second(pos_ref, own_ref, other_ref, weights):
    core = pos_ref[0] % NC
    for mine in range(NC):

        @pl.when(core == mine)
        def _():
            for x in range(NX):
                for d in range(3):
                    for k in range(9):
                        tap = 9 * (k // 3) + 3 * (k % 3) + d
                        source = 144 * d + 16 * k
                        at = 128 * tap + 16 * (NC * x + mine)
                        weights[at : at + 16, :] = own_ref[x, source : source + 16, :]
                        at = 128 * tap + 16 * (NC * x + 1 - mine)
                        weights[at : at + 16, :] = other_ref[x, source : source + 16, :]


def second_conv(
    pos_ref, field_ref, sums_ref, vectors_ref, weights, groups_t_ref, squares_t_ref, order_ref, out_ref, flat, stack
):
    row, col = pos_ref[0] // COLS, pos_ref[0] % COLS
    mean_l, scale_l = merge(sums_ref[...], 320.0 * NY * WG, groups_t_ref[...], squares_t_ref[...])
    affine = exact(vectors_ref[...], chosen(pos_ref[1]))
    scale_l = scale_l * affine[3:4]
    shift_l = affine[4:5]

    at = lax.broadcasted_iota(jnp.int32, (RING, 1), 0) - LEAD
    outside = (at < 0) & (row == 0) | (at < PITCH - 2) & (row == 0)
    outside = outside | (at >= PITCH * (ROWS + 1) - 1) & (row == NZ - 1)
    at = (at + PITCH) % PITCH
    outside = outside | (at == WIDE) & (col == COLS - 1) | (at == PITCH - 1) & (col == 0)
    keep = 1.0 - outside.astype(F32)
    for t in range(NY):
        act = silu((field_ref[t] - mean_l) * scale_l + shift_l) * keep
        flat[...] = dot(act.astype(BF), order_ref[...])
        for dy in range(3):
            for dx in range(3):
                start = LEAD + PITCH * dy + dx - 1
                lane = 128 * (3 * dy + dx)
                stack[t, :, lane : lane + 128] = flat[start : start + 384, :].astype(BF)
    for t in range(NY):
        total = None
        for dt in range(3):
            source = t - 2 + dt
            if source < 0:
                continue
            term = dot(stack[source], weights[1152 * dt : 1152 * dt + 1152, :])
            total = term if total is None else total + term
        for r in range(ROWS):
            out_ref[t, r] = total[PITCH * r : PITCH * r + WIDE].astype(BF)


def call(body, outs, scratch, smem, *args):
    return pl.pallas_call(
        body,
        out_shape=outs,
        in_specs=[SM] * smem + [VM] * (len(args) - smem),
        out_specs=jax.tree.map(lambda _: VM, outs),
        scratch_shapes=scratch,
        compiler_params=pltpu.CompilerParams(vmem_limit_bytes=56 * 1024 * 1024),
    )(*args)


def shape(dims, dtype):
    return jax.ShapeDtypeStruct(dims, dtype)


def by_group(kernel):
    taps = jnp.pad(kernel.reshape(27, 6, PART), ((0, 1), (0, 0), (0, 0))).reshape(7, 4, 6, PART)
    return jnp.transpose(taps, (0, 2, 1, 3)).reshape(42, CH)


def by_column(kernel):
    rows = jnp.transpose(kernel, (0, 1, 3, 2, 4)).reshape(54, 3, PART)
    return jnp.pad(rows, ((0, 10), (0, 0), (0, 32))).reshape(64, CH)


def shards(
    latents,
    gain_first,
    shift_first,
    kernel_first,
    bias_first,
    gain_second,
    shift_second,
    kernel_second,
    bias_second,
):
    space = lax.axis_index("space")
    frame = lax.axis_index("tm")
    pos = jnp.stack([space, frame]).astype(jnp.int32)
    vectors = jnp.stack(
        [gain_first, shift_first, bias_first, gain_second, shift_second, bias_second, bias_second, bias_second]
    )
    tile = latents[0, 0]
    flat_tile = tile.reshape(ROWS * WIDE, CH)

    swapped = lax.ppermute(by_column(kernel_second), BOTH, SWAP)
    placed, west, east, sums = call(
        measure_tile,
        (shape((320, CH), BF), shape((16, CH), BF), shape((16, CH), BF), shape((NY * COLS, 128), F32)),
        [],
        0,
        flat_tile,
        jnp.asarray(CHANNEL_LANES, BF),
        jnp.asarray(GROUPS_OF),
        jnp.asarray(GROUPS_OF.T),
        jnp.asarray(SQUARES_OF),
        jnp.asarray(EDGES, BF),
    )
    send = functools.partial(lax.ppermute, axis_name="space")
    from_west, from_east = send(east, perm=moved(0, 1)), send(west, perm=moved(0, -1))
    plane_sums = lax.all_to_all(sums, BOTH, 0, 0, tiled=True, axis_index_groups=PLANE)
    sums_rows = call(pool_plane, shape((8, CH), BF), [], 0, plane_sums)
    from_west, from_east, sums_rows, swapped, packed = lax.optimization_barrier(
        (from_west, from_east, sums_rows, swapped, by_group(kernel_first))
    )
    letter = jnp.concatenate([packed, sums_rows[0:6], swapped], axis=0)
    got = lax.all_to_all(
        jnp.broadcast_to(letter[None], (NZ, 112, CH)), "space", 0, 0, tiled=True, axis_index_groups=ALONG_Z
    )
    from_north = send(jnp.concatenate([placed[240:320], from_west[12:16], from_east[12:16]]), perm=moved(1, 0))
    from_south = send(jnp.concatenate([placed[0:80], from_west[0:4], from_east[0:4]]), perm=moved(-1, 0))
    parcel = jnp.concatenate([placed, from_west, from_east, from_north, from_south], axis=0)
    frames = lax.all_gather(parcel, "tm")
    ordered, all_sums = call(
        arrange_first,
        (shape((NX, 336, CH), BF), shape((8, 128), F32)),
        [],
        0,
        got,
        jnp.asarray(FIRST_ROWS, BF),
    )
    own = lax.all_to_all(ordered, "space", 0, 0, tiled=True, axis_index_groups=ALONG_X)
    stack = call(
        first_act,
        shape((NY, FIELD, 3 * CH), BF),
        [pltpu.VMEM((GUARD + (ROWS + 4) * PITCH + GUARD, CH), F32)],
        1,
        pos,
        frames,
        all_sums,
        vectors,
        jnp.asarray(CHANNEL_LANES),
        jnp.asarray(GROUPS_OF_LANES),
        jnp.asarray(SQUARES_OF_LANES),
    )
    got_second, _ = lax.optimization_barrier((got, stack))
    ordered_second = call(
        arrange_second,
        shape((432, CH), BF),
        [],
        0,
        got_second,
        jnp.asarray(SECOND_ROWS, BF),
        jnp.asarray(SECOND_LANES, BF),
    )
    own, stack, _ = lax.optimization_barrier((own, stack, ordered_second))
    other = lax.ppermute(own, "space", SIBLING)

    field, sums = call(
        first_conv,
        (shape((NY, RING, 128), F32), shape((SPACE, 128), F32)),
        [pltpu.VMEM((7, CH, CH), BF), pltpu.VMEM((3 * CH, 9 * 128), BF)],
        1,
        pos,
        stack,
        own,
        other,
        vectors,
        jnp.asarray(PART_GROUPS),
        jnp.asarray(PART_GROUPS.T),
        jnp.asarray(PART_SQUARES),
        jnp.asarray(SECOND_LANES.T, BF),
    )
    all_sums = lax.all_to_all(sums, "space", 0, 0, tiled=True)
    own_second = lax.all_gather(ordered_second, "space", axis_index_groups=ALONG_X)
    own_second, _ = lax.optimization_barrier((own_second, field))
    other_second = lax.ppermute(own_second, "space", SIBLING)
    weights_second = call(assemble_second, shape((27 * 128, CH), BF), [], 1, pos, own_second, other_second)
    partial = call(
        second_conv,
        shape((NY, ROWS, WIDE, CH), BF),
        [pltpu.VMEM((RING, 128), F32), pltpu.VMEM((NY, 384, 9 * 128), BF)],
        1,
        pos,
        field,
        all_sums,
        vectors,
        weights_second,
        jnp.asarray(PART_GROUPS.T),
        jnp.asarray(PART_SQUARES.T),
        jnp.asarray(PART_LANES, BF),
    )
    parts = lax.all_to_all(partial, "tm", 0, 0, tiled=True)
    second_out = jnp.sum(parts.astype(F32), axis=0) + bias_second
    return (tile.astype(F32) + second_out).astype(BF)[None, None]


def solution(mesh):
    placed = (
        P("tm", "space", None, None, None),
        P(),
        P(),
        P(None, None, None, "space", "tm"),
        P(),
        P(),
        P(),
        P(None, None, None, "space", "tm"),
        P(),
    )
    return jax.shard_map(
        shards,
        mesh=mesh,
        in_specs=placed,
        out_specs=P("tm", "space", None, None, None),
        check_vma=False,
    )
```

```python
import functools

import jax
import jax.numpy as jnp
import numpy as np
from jax import lax
from jax.experimental import pallas as pl
from jax.experimental.pallas import tpu as pltpu
from jax.sharding import PartitionSpec as P

EPS = 1e-06
BF = jnp.bfloat16
F32 = jnp.float32
VM = pl.BlockSpec(memory_space=pltpu.VMEM)
SM = pl.BlockSpec(memory_space=pltpu.SMEM)
HIGH = lax.Precision.HIGHEST

NZ, NX, NC, NY = 8, 4, 2, 4
COLS = NX * NC
SPACE = NZ * COLS
ROWS, WIDE, PITCH = 8, 40, 48
CH, PART, WG = 384, 96, 12
GUARD = 16
LEAD = 8
RING = LEAD + (ROWS + 2) * PITCH + 8
FIELD = RING + 2 * PITCH
BOTH = ("tm", "space")
ALONG_Z = [[z * COLS + q for z in range(NZ)] for q in range(COLS)]
ALONG_X = [[z * COLS + x * NC + c for x in range(NX)] for z in range(NZ) for c in range(NC)]
PLANE = [[y * SPACE + z * COLS + q for y in range(NY) for q in range(COLS)] for z in range(NZ)]
SIBLING = [(s, s ^ 1) for s in range(SPACE)]


def moved(down, right):
    return [(s, (s + COLS * down + right) % SPACE) for s in range(SPACE)]


SWAP = [
    (y * SPACE + z * COLS + q, (z // 2) * SPACE + (2 * y + z % 2) * COLS + q)
    for y in range(NY)
    for z in range(NZ)
    for q in range(COLS)
]


def one_hot(rows, cols, pairs):
    out = np.zeros((rows, cols), np.float32)
    for r, c in pairs:
        out[r, c] = 1.0
    return out


CHANNEL_LANES = one_hot(
    CH, CH, [(6 * (8 * z + q) + i, 48 * q + 6 * z + i) for z in range(8) for q in range(8) for i in range(6)]
)
GROUPS_OF = one_hot(CH, 128, [(c, c // WG) for c in range(CH)])
SQUARES_OF = np.roll(GROUPS_OF, 64, axis=1)
GROUPS_OF_LANES = (CHANNEL_LANES.T @ GROUPS_OF).T
SQUARES_OF_LANES = (CHANNEL_LANES.T @ SQUARES_OF).T
PART_GROUPS = one_hot(128, 128, [(c, c // WG) for c in range(PART)])
PART_SQUARES = np.roll(PART_GROUPS, 64, axis=1)
EDGES = one_hot(
    32,
    320,
    [(2 * r + c, 40 * r + c) for r in range(8) for c in range(2)]
    + [(16 + 2 * r + c, 40 * r + 38 + c) for r in range(8) for c in range(2)],
)
FIRST_ROWS = one_hot(
    336, 384, [(48 * g + 6 * z + i, 48 * z + 6 * g + i) for g in range(7) for z in range(8) for i in range(6)]
)
SECOND_ROWS = one_hot(
    144, 128, [(16 * k + 6 * h + i, 64 * h + 6 * k + i) for k in range(9) for h in range(2) for i in range(6)]
)
SECOND_LANES = one_hot(512, CH, [(128 * y + o, PART * y + o) for y in range(4) for o in range(PART)])
PART_LANES = one_hot(
    128, 128, [(48 * h + 6 * q + i, 16 * q + 6 * h + i) for h in range(2) for q in range(8) for i in range(6)]
)


def dot(a, b):
    return jnp.dot(a, b, preferred_element_type=F32)


def exact(a, b):
    return jnp.dot(a, b, preferred_element_type=F32, precision=HIGH)


def merge(sums, count, groups_t, squares_t):
    mean = jnp.mean(sums, axis=0, keepdims=True)
    off = sums - mean
    between = count * jnp.sum(off * off, axis=0, keepdims=True)
    within = jnp.sum(sums, axis=0, keepdims=True)
    rows = jnp.concatenate([mean, between, jnp.zeros((6, 128), F32)], axis=0)
    by_lane = exact(rows, groups_t)
    spread = (by_lane[1:2] + exact(tall(within), squares_t)[0:1]) * (1.0 / (count * sums.shape[0]))
    return by_lane[0:1], lax.rsqrt(spread + EPS)


def pool(rows, count):
    mean = jnp.mean(rows, axis=0, keepdims=True)
    off = rows - mean
    between = count * jnp.sum(off * off, axis=0, keepdims=True)
    squares = jnp.sum(rows, axis=0, keepdims=True) + pltpu.roll(tall(between), 64, axis=1)[0:1]
    return jnp.where(lax.broadcasted_iota(jnp.int32, (1, 128), 1) < 64, mean, squares)


def tall(row):
    return jnp.broadcast_to(row, (8, row.shape[1]))


def chosen(part):
    channel = lax.broadcasted_iota(jnp.int32, (CH, 128), 0)
    lane = lax.broadcasted_iota(jnp.int32, (CH, 128), 1)
    return ((channel == part * PART + lane) & (lane < PART)).astype(F32)


def silu(u):
    return u / (1.0 + jnp.exp(-u))


def measure_tile(
    tile_ref, lanes_ref, groups_ref, groups_t_ref, squares_ref, edges_ref,
    placed_ref, west_ref, east_ref, sums_ref,
):
    tile = tile_ref[...]
    placed = dot(tile, lanes_ref[...]).astype(BF)
    placed_ref[...] = placed
    edges = dot(edges_ref[...], placed).astype(BF)
    west_ref[...] = edges[0:16]
    east_ref[...] = edges[16:32]
    wide = tile.astype(F32)
    mean = exact(tall(jnp.sum(wide, axis=0, keepdims=True)), groups_ref[...]) * (1.0 / (320 * WG))
    off = wide - exact(mean, groups_t_ref[...])[0:1]
    squares = exact(tall(jnp.sum(off * off, axis=0, keepdims=True)), squares_ref[...])
    sums_ref[...] = jnp.broadcast_to((mean + squares)[0:1], sums_ref.shape)


def pool_plane(sums_ref, out_ref):
    row = pool(sums_ref[...], 320.0 * WG)
    hi = row.astype(BF).astype(F32)
    mid = (row - hi).astype(BF).astype(F32)
    rows = jnp.concatenate([hi, mid, row - hi - mid, jnp.zeros((5, 128), F32)], axis=0)
    out_ref[...] = jnp.concatenate([rows, jnp.zeros((8, CH - 128), F32)], axis=1).astype(BF)


def arrange_first(got_ref, rows_ref, out_ref, sums_ref):
    blocks = [got_ref[z, 0:48, :] for z in range(NZ)]
    ordered = dot(rows_ref[...], jnp.concatenate(blocks, axis=0)).astype(BF)
    for copy in range(NX):
        out_ref[copy] = ordered
    wide = [b[:, 0:128].astype(F32) for b in blocks]
    sums_ref[...] = jnp.concatenate([b[42:43] + b[43:44] + b[44:45] for b in wide], axis=0)


def arrange_second(got_ref, rows_ref, lanes_ref, out_ref):
    by_part = []
    for y in range(NY):
        pair = jnp.concatenate([got_ref[2 * y + h, 48:112, :] for h in range(2)], axis=0)
        by_part.append(dot(rows_ref[...], pair).astype(BF))
    tall_parts = [
        jnp.concatenate([by_part[y][:, 128 * d : 128 * d + 128] for y in range(NY)], axis=1) for d in range(3)
    ]
    out_ref[...] = dot(jnp.concatenate(tall_parts, axis=0), lanes_ref[...]).astype(BF)


def first_act(
    pos_ref, lat0_ref, lat1_ref, lat2_ref, lat3_ref, sums_ref, vectors_ref, lanes_ref, groups_t_ref, squares_t_ref, stack, flat
):
    row, col = pos_ref[0] // COLS, pos_ref[0] % COLS
    mean_l, scale_l = merge(sums_ref[...], 320.0 * WG * NY * COLS, groups_t_ref[...], squares_t_ref[...])
    affine = exact(vectors_ref[...], lanes_ref[...])
    scale_l = scale_l * affine[0:1]
    shift_l = affine[1:2]
    has_w = (col > 0).astype(F32)
    has_e = (col < COLS - 1).astype(F32)
    has_n = (row > 0).astype(F32)
    has_s = (row < NZ - 1).astype(F32)
    flat[...] = jnp.zeros_like(flat)
    for back, lat_ref in enumerate((lat0_ref, lat1_ref, lat2_ref, lat3_ref)):
        t = (pos_ref[1] + (NY - back)) % NY
        act = silu((lat_ref[...].astype(F32) - mean_l) * scale_l + shift_l)
        for r in range(-2, ROWS + 2):
            base = GUARD + PITCH * (r + 2)
            if 0 <= r < ROWS:
                cells = act[WIDE * r : WIDE * r + WIDE]
                left, right = act[320 + 2 * r : 322 + 2 * r] * has_w, act[336 + 2 * r : 338 + 2 * r] * has_e
            else:
                start, at, inside = (352, r + 2, has_n) if r < 0 else (440, r - ROWS, has_s)
                cells = act[start + WIDE * at : start + WIDE * at + WIDE] * inside
                left = act[start + 80 + 2 * at : start + 82 + 2 * at] * (inside * has_w)
                right = act[start + 84 + 2 * at : start + 86 + 2 * at] * (inside * has_e)
            flat[base : base + WIDE, :] = cells
            flat[base + WIDE : base + WIDE + 2, :] = right
            flat[base - 2 : base, :] = left
        for d in range(3):
            start = GUARD - LEAD + d - 1
            stack[t, :, CH * d : CH * d + CH] = flat[start : start + FIELD, :].astype(BF)


def first_conv(
    pos_ref, stack, own_ref, other_ref, vectors_ref, part_ref, part_t_ref, part_squares_ref, spread_ref,
    out_ref, sums_ref, packed, weights,
):
    core = pos_ref[0] % NC
    bias = exact(vectors_ref[...], chosen(pos_ref[1]))[2:3]
    for mine in range(NC):

        @pl.when(core == mine)
        def _():
            for x in range(NX):
                for g in range(7):
                    at = 48 * (NC * x + mine)
                    packed[g, at : at + 48, :] = own_ref[x, 48 * g : 48 * g + 48, :]
                    at = 48 * (NC * x + 1 - mine)
                    packed[g, at : at + 48, :] = other_ref[x, 48 * g : 48 * g + 48, :]

    for g in range(7):
        taps = dot(packed[g], spread_ref[...]).astype(BF)
        for tap in range(4 * g, min(4 * g + 4, 27)):
            down, right = CH * (tap % 3), 128 * (tap // 3)
            weights[down : down + CH, right : right + 128] = taps[:, 128 * (tap % 4) : 128 * (tap % 4) + 128]
    totals = [None] * NY
    for t in range(NY):
        first = max(0, t + 3 - NY)
        product = dot(stack[t], weights[:, CH * first :])
        for dt in range(first, 3):
            to = t + 2 - dt
            part = product[:, CH * (dt - first) : CH * (dt - first) + CH]
            term = part[0:RING, 0:128]
            for dy in (1, 2):
                term = term + part[PITCH * dy : PITCH * dy + RING, 128 * dy : 128 * dy + 128]
            totals[to] = term if totals[to] is None else totals[to] + term
    at = lax.broadcasted_iota(jnp.int32, (RING, 1), 0) - (LEAD + PITCH)
    inside = ((at >= 0) & (at < PITCH * ROWS) & (at % PITCH < WIDE)).astype(F32)
    sums = None
    for t in range(NY):
        totals[t] = totals[t] + bias
        out_ref[t] = totals[t]
        line = jnp.sum(totals[t] * inside, axis=0, keepdims=True)
        sums = line if sums is None else sums + line
    mean = exact(tall(sums), part_ref[...]) * (1.0 / (320 * NY * WG))
    mean_l = exact(mean, part_t_ref[...])[0:1]
    sums = None
    for t in range(NY):
        off = (totals[t] - mean_l) * inside
        line = jnp.sum(off * off, axis=0, keepdims=True)
        sums = line if sums is None else sums + line
    squares = exact(tall(sums), part_squares_ref[...])
    sums_ref[...] = jnp.broadcast_to((mean + squares)[0:1], (SPACE, 128))


def second_conv(
    pos_ref, field_ref, sums_ref, vectors_ref, own_ref, other_ref, groups_t_ref, squares_t_ref, order_ref, out_ref,
    weights, flat, stack,
):
    core = pos_ref[0] % NC
    for mine in range(NC):

        @pl.when(core == mine)
        def _():
            for x in range(NX):
                for d in range(3):
                    for k in range(9):
                        tap = 9 * (k // 3) + 3 * (k % 3) + d
                        source = 144 * d + 16 * k
                        at = 128 * tap + 16 * (NC * x + mine)
                        weights[at : at + 16, :] = own_ref[x, source : source + 16, :]
                        at = 128 * tap + 16 * (NC * x + 1 - mine)
                        weights[at : at + 16, :] = other_ref[x, source : source + 16, :]

    row, col = pos_ref[0] // COLS, pos_ref[0] % COLS
    mean_l, scale_l = merge(sums_ref[...], 320.0 * NY * WG, groups_t_ref[...], squares_t_ref[...])
    affine = exact(vectors_ref[...], chosen(pos_ref[1]))
    scale_l = scale_l * affine[3:4]
    shift_l = affine[4:5]

    at = lax.broadcasted_iota(jnp.int32, (RING, 1), 0) - LEAD
    outside = (at < 0) & (row == 0) | (at < PITCH - 2) & (row == 0)
    outside = outside | (at >= PITCH * (ROWS + 1) - 1) & (row == NZ - 1)
    at = (at + PITCH) % PITCH
    outside = outside | (at == WIDE) & (col == COLS - 1) | (at == PITCH - 1) & (col == 0)
    keep = 1.0 - outside.astype(F32)
    for t in range(NY):
        act = silu((field_ref[t] - mean_l) * scale_l + shift_l) * keep
        flat[...] = dot(act.astype(BF), order_ref[...])
        for dy in range(3):
            for dx in range(3):
                start = LEAD + PITCH * dy + dx - 1
                lane = 128 * (3 * dy + dx)
                stack[t, :, lane : lane + 128] = flat[start : start + 384, :].astype(BF)
    for t in range(NY):
        total = None
        for dt in range(3):
            source = t - 2 + dt
            if source < 0:
                continue
            term = dot(stack[source], weights[1152 * dt : 1152 * dt + 1152, :])
            total = term if total is None else total + term
        for r in range(ROWS):
            out_ref[t, r] = total[PITCH * r : PITCH * r + WIDE].astype(BF)


def call(body, outs, scratch, smem, *args, flops=0):
    return pl.pallas_call(
        body,
        out_shape=outs,
        in_specs=[SM] * smem + [VM] * (len(args) - smem),
        out_specs=jax.tree.map(lambda _: VM, outs),
        scratch_shapes=scratch,
        compiler_params=pltpu.CompilerParams(vmem_limit_bytes=56 * 1024 * 1024),
        cost_estimate=pl.CostEstimate(flops=flops, bytes_accessed=0, transcendentals=0),
    )(*args)


def shape(dims, dtype):
    return jax.ShapeDtypeStruct(dims, dtype)


def by_group(kernel):
    taps = jnp.pad(kernel.reshape(27, 6, PART), ((0, 1), (0, 0), (0, 0))).reshape(7, 4, 6, PART)
    return jnp.transpose(taps, (0, 2, 1, 3)).reshape(42, CH)


def by_column(kernel):
    rows = jnp.transpose(kernel, (0, 1, 3, 2, 4)).reshape(54, 3, PART)
    return jnp.pad(rows, ((0, 10), (0, 0), (0, 32))).reshape(64, CH)


def shards(
    latents,
    gain_first,
    shift_first,
    kernel_first,
    bias_first,
    gain_second,
    shift_second,
    kernel_second,
    bias_second,
):
    space = lax.axis_index("space")
    frame = lax.axis_index("tm")
    pos = jnp.stack([space, frame]).astype(jnp.int32)
    vectors = jnp.stack(
        [gain_first, shift_first, bias_first, gain_second, shift_second, bias_second, bias_second, bias_second]
    )
    tile = latents[0, 0]
    flat_tile = tile.reshape(ROWS * WIDE, CH)

    swapped = lax.ppermute(by_column(kernel_second), BOTH, SWAP)
    placed, west, east, sums = call(
        measure_tile,
        (shape((320, CH), BF), shape((16, CH), BF), shape((16, CH), BF), shape((NY * COLS, 128), F32)),
        [],
        0,
        flat_tile,
        jnp.asarray(CHANNEL_LANES, BF),
        jnp.asarray(GROUPS_OF),
        jnp.asarray(GROUPS_OF.T),
        jnp.asarray(SQUARES_OF),
        jnp.asarray(EDGES, BF),
    )
    send = functools.partial(lax.ppermute, axis_name="space")
    from_west, from_east = send(east, perm=moved(0, 1)), send(west, perm=moved(0, -1))
    plane_sums = lax.all_to_all(sums, BOTH, 0, 0, tiled=True, axis_index_groups=PLANE)
    sums_rows = call(pool_plane, shape((8, CH), BF), [], 0, plane_sums)
    from_north = send(jnp.concatenate([placed[240:320], from_west[12:16], from_east[12:16]]), perm=moved(1, 0))
    from_south = send(jnp.concatenate([placed[0:80], from_west[0:4], from_east[0:4]]), perm=moved(-1, 0))
    parcel = jnp.concatenate([placed, from_west, from_east, from_north, from_south], axis=0)
    sums_rows, swapped, packed = lax.optimization_barrier((sums_rows, swapped, by_group(kernel_first)))
    letter = jnp.concatenate([packed, sums_rows[0:6], swapped], axis=0)
    letters = jnp.broadcast_to(letter[None], (NZ, 112, CH))
    letters, parcel = lax.optimization_barrier((letters, parcel))
    got = lax.all_to_all(letters, "space", 0, 0, tiled=True, axis_index_groups=ALONG_Z)
    later = [lax.ppermute(parcel, "tm", [(t, (t + k) % NY) for t in range(NY)]) for k in range(1, NY)]
    ordered, all_sums = call(
        arrange_first,
        (shape((NX, 336, CH), BF), shape((8, 128), F32)),
        [],
        0,
        got,
        jnp.asarray(FIRST_ROWS, BF),
    )
    own = lax.all_to_all(ordered, "space", 0, 0, tiled=True, axis_index_groups=ALONG_X)
    stack = call(
        first_act,
        shape((NY, FIELD, 3 * CH), BF),
        [pltpu.VMEM((GUARD + (ROWS + 4) * PITCH + GUARD, CH), F32)],
        1,
        pos,
        parcel,
        *later,
        all_sums,
        vectors,
        jnp.asarray(CHANNEL_LANES),
        jnp.asarray(GROUPS_OF_LANES),
        jnp.asarray(SQUARES_OF_LANES),
        flops=int(2e10),
    )
    got_second, _ = lax.optimization_barrier((got, ordered))
    ordered_second = call(
        arrange_second,
        shape((432, CH), BF),
        [],
        0,
        got_second,
        jnp.asarray(SECOND_ROWS, BF),
        jnp.asarray(SECOND_LANES, BF),
    )
    own, stack, _ = lax.optimization_barrier((own, stack, ordered_second))
    other = lax.ppermute(own, "space", SIBLING)

    field, sums = call(
        first_conv,
        (shape((NY, RING, 128), F32), shape((SPACE, 128), F32)),
        [pltpu.VMEM((7, CH, CH), BF), pltpu.VMEM((3 * CH, 9 * 128), BF)],
        1,
        pos,
        stack,
        own,
        other,
        vectors,
        jnp.asarray(PART_GROUPS),
        jnp.asarray(PART_GROUPS.T),
        jnp.asarray(PART_SQUARES),
        jnp.asarray(SECOND_LANES.T, BF),
    )
    all_sums = lax.all_to_all(sums, "space", 0, 0, tiled=True)
    own_second = lax.all_gather(ordered_second, "space", axis_index_groups=ALONG_X)
    own_second, _ = lax.optimization_barrier((own_second, field))
    other_second = lax.ppermute(own_second, "space", SIBLING)
    partial = call(
        second_conv,
        shape((NY, ROWS, WIDE, CH), BF),
        [pltpu.VMEM((27 * 128, CH), BF), pltpu.VMEM((RING, 128), F32), pltpu.VMEM((NY, 384, 9 * 128), BF)],
        1,
        pos,
        field,
        all_sums,
        vectors,
        own_second,
        other_second,
        jnp.asarray(PART_GROUPS.T),
        jnp.asarray(PART_SQUARES.T),
        jnp.asarray(PART_LANES, BF),
    )
    parts = lax.all_to_all(partial, "tm", 0, 0, tiled=True)
    second_out = jnp.sum(parts.astype(F32), axis=0) + bias_second
    return (tile.astype(F32) + second_out).astype(BF)[None, None]


def solution(mesh):
    placed = (
        P("tm", "space", None, None, None),
        P(),
        P(),
        P(None, None, None, "space", "tm"),
        P(),
        P(),
        P(),
        P(None, None, None, "space", "tm"),
        P(),
    )
    return jax.shard_map(
        shards,
        mesh=mesh,
        in_specs=placed,
        out_specs=P("tm", "space", None, None, None),
        check_vma=False,
    )
```

```python
import functools

import jax
import jax.numpy as jnp
import numpy as np
from jax import lax
from jax.experimental import pallas as pl
from jax.experimental.pallas import tpu as pltpu
from jax.sharding import PartitionSpec as P

EPS = 1e-06
BF = jnp.bfloat16
F32 = jnp.float32
VM = pl.BlockSpec(memory_space=pltpu.VMEM)
SM = pl.BlockSpec(memory_space=pltpu.SMEM)
AT = pl.BlockSpec(memory_space=pl.ANY)
HB = pl.BlockSpec(memory_space=pltpu.HBM)
HIGH = lax.Precision.HIGHEST

NZ, NX, NC, NY = 8, 4, 2, 4
COLS = NX * NC
SPACE = NZ * COLS
ROWS, WIDE, PITCH = 8, 40, 48
CH, PART, WG = 384, 96, 12
GUARD = 16
LEAD = 8
RING = LEAD + (ROWS + 2) * PITCH + 8
FIELD = RING + 2 * PITCH
BOTH = ("tm", "space")
ALONG_Z = [[z * COLS + q for z in range(NZ)] for q in range(COLS)]
ALONG_X = [[z * COLS + x * NC + c for x in range(NX)] for z in range(NZ) for c in range(NC)]
PLANE = [[y * SPACE + z * COLS + q for y in range(NY) for q in range(COLS)] for z in range(NZ)]
SIBLING = [(s, s ^ 1) for s in range(SPACE)]


def moved(down, right):
    return [(s, (s + COLS * down + right) % SPACE) for s in range(SPACE)]


SWAP = [
    (y * SPACE + z * COLS + q, (z // 2) * SPACE + (2 * y + z % 2) * COLS + q)
    for y in range(NY)
    for z in range(NZ)
    for q in range(COLS)
]


def one_hot(rows, cols, pairs):
    out = np.zeros((rows, cols), np.float32)
    for r, c in pairs:
        out[r, c] = 1.0
    return out


CHANNEL_LANES = one_hot(
    CH, CH, [(6 * (8 * z + q) + i, 48 * q + 6 * z + i) for z in range(8) for q in range(8) for i in range(6)]
)
GROUPS_OF = one_hot(CH, 128, [(c, c // WG) for c in range(CH)])
SQUARES_OF = np.roll(GROUPS_OF, 64, axis=1)
GROUPS_OF_LANES = (CHANNEL_LANES.T @ GROUPS_OF).T
SQUARES_OF_LANES = (CHANNEL_LANES.T @ SQUARES_OF).T
PART_GROUPS = one_hot(128, 128, [(c, c // WG) for c in range(PART)])
PART_SQUARES = np.roll(PART_GROUPS, 64, axis=1)
EDGES = one_hot(
    32,
    320,
    [(2 * r + c, 40 * r + c) for r in range(8) for c in range(2)]
    + [(16 + 2 * r + c, 40 * r + 38 + c) for r in range(8) for c in range(2)],
)
FIRST_ROWS = one_hot(
    336, 384, [(48 * g + 6 * z + i, 48 * z + 6 * g + i) for g in range(7) for z in range(8) for i in range(6)]
)
SECOND_ROWS = one_hot(
    144, 128, [(16 * k + 6 * h + i, 64 * h + 6 * k + i) for k in range(9) for h in range(2) for i in range(6)]
)
SECOND_LANES = one_hot(512, CH, [(128 * y + o, PART * y + o) for y in range(4) for o in range(PART)])
PART_LANES = one_hot(
    128, 128, [(48 * h + 6 * q + i, 16 * q + 6 * h + i) for h in range(2) for q in range(8) for i in range(6)]
)


def dot(a, b):
    return jnp.dot(a, b, preferred_element_type=F32)


def exact(a, b):
    return jnp.dot(a, b, preferred_element_type=F32, precision=HIGH)


def merge(sums, count, groups_t, squares_t):
    mean = jnp.mean(sums, axis=0, keepdims=True)
    off = sums - mean
    between = count * jnp.sum(off * off, axis=0, keepdims=True)
    within = jnp.sum(sums, axis=0, keepdims=True)
    rows = jnp.concatenate([mean, between, jnp.zeros((6, 128), F32)], axis=0)
    by_lane = exact(rows, groups_t)
    spread = (by_lane[1:2] + exact(tall(within), squares_t)[0:1]) * (1.0 / (count * sums.shape[0]))
    return by_lane[0:1], lax.rsqrt(spread + EPS)


def pool(rows, count):
    mean = jnp.mean(rows, axis=0, keepdims=True)
    off = rows - mean
    between = count * jnp.sum(off * off, axis=0, keepdims=True)
    squares = jnp.sum(rows, axis=0, keepdims=True) + pltpu.roll(tall(between), 64, axis=1)[0:1]
    return jnp.where(lax.broadcasted_iota(jnp.int32, (1, 128), 1) < 64, mean, squares)


def tall(row):
    return jnp.broadcast_to(row, (8, row.shape[1]))


def chosen(part):
    channel = lax.broadcasted_iota(jnp.int32, (CH, 128), 0)
    lane = lax.broadcasted_iota(jnp.int32, (CH, 128), 1)
    return ((channel == part * PART + lane) & (lane < PART)).astype(F32)


def silu(u):
    return u / (1.0 + jnp.exp(-u))


def measure_tile(
    tile_ref, lanes_ref, groups_ref, groups_t_ref, squares_ref, edges_ref,
    placed_ref, west_ref, east_ref, sums_ref,
):
    tile = tile_ref[...]
    placed = dot(tile, lanes_ref[...]).astype(BF)
    placed_ref[...] = placed
    edges = dot(edges_ref[...], placed).astype(BF)
    west_ref[...] = edges[0:16]
    east_ref[...] = edges[16:32]
    wide = tile.astype(F32)
    mean = exact(tall(jnp.sum(wide, axis=0, keepdims=True)), groups_ref[...]) * (1.0 / (320 * WG))
    off = wide - exact(mean, groups_t_ref[...])[0:1]
    squares = exact(tall(jnp.sum(off * off, axis=0, keepdims=True)), squares_ref[...])
    sums_ref[...] = jnp.broadcast_to((mean + squares)[0:1], sums_ref.shape)


def pool_plane(sums_ref, out_ref):
    row = pool(sums_ref[...], 320.0 * WG)
    hi = row.astype(BF).astype(F32)
    mid = (row - hi).astype(BF).astype(F32)
    rows = jnp.concatenate([hi, mid, row - hi - mid, jnp.zeros((5, 128), F32)], axis=0)
    out_ref[...] = jnp.concatenate([rows, jnp.zeros((8, CH - 128), F32)], axis=1).astype(BF)


def arrange_first(got_ref, rows_ref, out_ref, sums_ref):
    blocks = [got_ref[z, 0:48, :] for z in range(NZ)]
    ordered = dot(rows_ref[...], jnp.concatenate(blocks, axis=0)).astype(BF)
    for copy in range(NX):
        out_ref[copy] = ordered
    wide = [b[:, 0:128].astype(F32) for b in blocks]
    sums_ref[...] = jnp.concatenate([b[42:43] + b[43:44] + b[44:45] for b in wide], axis=0)


def arrange_second(got_ref, rows_ref, lanes_ref, out_ref):
    by_part = []
    for y in range(NY):
        pair = jnp.concatenate([got_ref[2 * y + h, 48:112, :] for h in range(2)], axis=0)
        by_part.append(dot(rows_ref[...], pair).astype(BF))
    tall_parts = [
        jnp.concatenate([by_part[y][:, 128 * d : 128 * d + 128] for y in range(NY)], axis=1) for d in range(3)
    ]
    rows = [tall_parts[d][16 * k : 16 * k + 16] for k in range(9) for d in range(3)]
    out_ref[...] = dot(jnp.concatenate(rows, axis=0), lanes_ref[...]).astype(BF)


def first_act(
    pos_ref, lat0_ref, lat1_ref, lat2_ref, lat3_ref, sums_ref, vectors_ref, lanes_ref, groups_t_ref, squares_t_ref,
    stack_ref, flat, lats, stack, in_sems, out_sems,
):
    arrivals = [
        pltpu.make_async_copy(lat_ref, lats.at[back], in_sems.at[back])
        for back, lat_ref in enumerate((lat0_ref, lat1_ref, lat2_ref, lat3_ref))
    ]
    for arrival in arrivals:
        arrival.start()
    row, col = pos_ref[0] // COLS, pos_ref[0] % COLS
    mean_l, scale_l = merge(sums_ref[...], 320.0 * WG * NY * COLS, groups_t_ref[...], squares_t_ref[...])
    vectors = vectors_ref[...]
    high = vectors.astype(BF)
    middle = (vectors - high.astype(F32)).astype(BF)
    low = (vectors - high.astype(F32) - middle.astype(F32)).astype(BF)
    lanes = lanes_ref[...]
    affine = dot(high, lanes) + dot(middle, lanes) + dot(low, lanes)
    scale_l = scale_l * affine[0:1]
    shift_l = affine[1:2]
    has_w = (col > 0).astype(F32)
    has_e = (col < COLS - 1).astype(F32)
    has_n = (row > 0).astype(F32)
    has_s = (row < NZ - 1).astype(F32)
    flat[...] = jnp.zeros_like(flat)
    leaving = []
    for back in range(NY):
        t = (pos_ref[1] + (NY - back)) % NY
        arrivals[back].wait()
        act = silu((lats[back].astype(F32) - mean_l) * scale_l + shift_l)
        for r in range(-2, ROWS + 2):
            base = GUARD + PITCH * (r + 2)
            if 0 <= r < ROWS:
                cells = act[WIDE * r : WIDE * r + WIDE]
                left, right = act[320 + 2 * r : 322 + 2 * r] * has_w, act[336 + 2 * r : 338 + 2 * r] * has_e
            else:
                start, at, inside = (352, r + 2, has_n) if r < 0 else (440, r - ROWS, has_s)
                cells = act[start + WIDE * at : start + WIDE * at + WIDE] * inside
                left = act[start + 80 + 2 * at : start + 82 + 2 * at] * (inside * has_w)
                right = act[start + 84 + 2 * at : start + 86 + 2 * at] * (inside * has_e)
            flat[base : base + WIDE, :] = cells
            flat[base + WIDE : base + WIDE + 2, :] = right
            flat[base - 2 : base, :] = left
        for d in range(3):
            start = GUARD - LEAD + d - 1
            stack[back, :, CH * d : CH * d + CH] = flat[start : start + FIELD, :].astype(BF)
        leaving.append(pltpu.make_async_copy(stack.at[back], stack_ref.at[t], out_sems.at[back]))
        leaving[back].start()
    for leave in leaving:
        leave.wait()


def land(core, own_ref, other_ref, slots, sems):
    copies = []
    for x in range(NX):
        at = NC * x
        copies.append(pltpu.make_async_copy(own_ref.at[x], slots.at[:, at + core], sems.at[at]))
        copies.append(pltpu.make_async_copy(other_ref.at[x], slots.at[:, at + 1 - core], sems.at[at + 1]))
    for copy in copies:
        copy.start()
    return copies


def first_conv(
    pos_ref, stack_ref, own_ref, other_ref, vectors_ref, part_ref, part_t_ref, part_squares_ref, spread_ref,
    out_ref, sums_ref, packed, weights, stack, sems, stack_sems,
):
    landing = land(pos_ref[0] % NC, own_ref, other_ref, packed, sems)
    arrivals = [pltpu.make_async_copy(stack_ref.at[t], stack.at[t], stack_sems.at[t]) for t in range(NY)]
    for arrival in arrivals:
        arrival.start()
    bias = exact(vectors_ref[...], chosen(pos_ref[1]))[2:3]
    for copy in landing:
        copy.wait()
    for g in range(7):
        taps = dot(packed[g].reshape(CH, CH), spread_ref[...]).astype(BF)
        for tap in range(4 * g, min(4 * g + 4, 27)):
            down, right = CH * (tap % 3), 128 * (tap // 3)
            weights[down : down + CH, right : right + 128] = taps[:, 128 * (tap % 4) : 128 * (tap % 4) + 128]
    totals = [None] * NY
    for t in range(NY):
        first = max(0, t + 3 - NY)
        arrivals[t].wait()
        product = dot(stack[t], weights[:, CH * first :])
        for dt in range(first, 3):
            to = t + 2 - dt
            part = product[:, CH * (dt - first) : CH * (dt - first) + CH]
            term = part[0:RING, 0:128]
            for dy in (1, 2):
                term = term + part[PITCH * dy : PITCH * dy + RING, 128 * dy : 128 * dy + 128]
            totals[to] = term if totals[to] is None else totals[to] + term
    at = lax.broadcasted_iota(jnp.int32, (RING, 1), 0) - (LEAD + PITCH)
    inside = ((at >= 0) & (at < PITCH * ROWS) & (at % PITCH < WIDE)).astype(F32)
    sums = None
    for t in range(NY):
        totals[t] = totals[t] + bias
        out_ref[t] = totals[t]
        line = jnp.sum(totals[t] * inside, axis=0, keepdims=True)
        sums = line if sums is None else sums + line
    mean = exact(tall(sums), part_ref[...]) * (1.0 / (320 * NY * WG))
    mean_l = exact(mean, part_t_ref[...])[0:1]
    sums = None
    for t in range(NY):
        off = (totals[t] - mean_l) * inside
        line = jnp.sum(off * off, axis=0, keepdims=True)
        sums = line if sums is None else sums + line
    squares = exact(tall(sums), part_squares_ref[...])
    sums_ref[...] = jnp.broadcast_to((mean + squares)[0:1], (SPACE, 128))


def second_conv(
    pos_ref, field_ref, own_ref, other_ref, sums_ref, vectors_ref, groups_t_ref, squares_t_ref, order_ref, out_ref,
    weights, flat, stack, field, sems, field_sems,
):
    arrivals = [pltpu.make_async_copy(field_ref.at[t], field.at[t], field_sems.at[t]) for t in range(NY)]
    for arrival in arrivals:
        arrival.start()
    landing = land(pos_ref[0] % NC, own_ref, other_ref, weights, sems)
    row, col = pos_ref[0] // COLS, pos_ref[0] % COLS
    mean_l, scale_l = merge(sums_ref[...], 320.0 * NY * WG, groups_t_ref[...], squares_t_ref[...])
    affine = exact(vectors_ref[...], chosen(pos_ref[1]))
    scale_l = scale_l * affine[3:4]
    shift_l = affine[4:5]

    at = lax.broadcasted_iota(jnp.int32, (RING, 1), 0) - LEAD
    outside = (at < 0) & (row == 0) | (at < PITCH - 2) & (row == 0)
    outside = outside | (at >= PITCH * (ROWS + 1) - 1) & (row == NZ - 1)
    at = (at + PITCH) % PITCH
    outside = outside | (at == WIDE) & (col == COLS - 1) | (at == PITCH - 1) & (col == 0)
    keep = 1.0 - outside.astype(F32)
    for t in range(NY):
        arrivals[t].wait()
        act = silu((field[t] - mean_l) * scale_l + shift_l) * keep
        flat[...] = dot(act.astype(BF), order_ref[...])
        for dy in range(3):
            for dx in range(3):
                start = LEAD + PITCH * dy + dx - 1
                lane = 128 * (3 * dy + dx)
                stack[t, :, lane : lane + 128] = flat[start : start + 384, :].astype(BF)
    for copy in landing:
        copy.wait()
    for t in range(NY):
        total = None
        for dt in range(3):
            source = t - 2 + dt
            if source < 0:
                continue
            term = dot(stack[source], weights[9 * dt : 9 * dt + 9].reshape(1152, CH))
            total = term if total is None else total + term
        for r in range(ROWS):
            out_ref[t, r] = total[PITCH * r : PITCH * r + WIDE].astype(BF)


def call(body, outs, scratch, places, *args, flops=0, out_places=None, grant=50):
    return pl.pallas_call(
        body,
        out_shape=outs,
        in_specs=[*places, *[VM] * (len(args) - len(places))],
        out_specs=jax.tree.map(lambda _: VM, outs) if out_places is None else out_places,
        scratch_shapes=scratch,
        compiler_params=pltpu.CompilerParams(vmem_limit_bytes=grant * 1024 * 1024),
        cost_estimate=pl.CostEstimate(flops=flops, bytes_accessed=0, transcendentals=0),
    )(*args)


def shape(dims, dtype):
    return jax.ShapeDtypeStruct(dims, dtype)


def by_group(kernel):
    taps = jnp.pad(kernel.reshape(27, 6, PART), ((0, 1), (0, 0), (0, 0))).reshape(7, 4, 6, PART)
    return jnp.transpose(taps, (0, 2, 1, 3)).reshape(42, CH)


def by_column(kernel):
    rows = jnp.transpose(kernel, (0, 1, 3, 2, 4)).reshape(54, 3, PART)
    return jnp.pad(rows, ((0, 10), (0, 0), (0, 32))).reshape(64, CH)


def shards(
    latents,
    gain_first,
    shift_first,
    kernel_first,
    bias_first,
    gain_second,
    shift_second,
    kernel_second,
    bias_second,
):
    space = lax.axis_index("space")
    frame = lax.axis_index("tm")
    pos = jnp.stack([space, frame]).astype(jnp.int32)
    vectors = jnp.stack(
        [gain_first, shift_first, bias_first, gain_second, shift_second, bias_second, bias_second, bias_second]
    )
    tile = latents[0, 0]
    flat_tile = tile.reshape(ROWS * WIDE, CH)

    swapped = lax.ppermute(by_column(kernel_second), BOTH, SWAP)
    placed, west, east, sums = call(
        measure_tile,
        (shape((320, CH), BF), shape((16, CH), BF), shape((16, CH), BF), shape((NY * COLS, 128), F32)),
        [],
        [],
        flat_tile,
        jnp.asarray(CHANNEL_LANES, BF),
        jnp.asarray(GROUPS_OF),
        jnp.asarray(GROUPS_OF.T),
        jnp.asarray(SQUARES_OF),
        jnp.asarray(EDGES, BF),
        grant=60,
    )
    send = functools.partial(lax.ppermute, axis_name="space")
    from_west, from_east = send(east, perm=moved(0, 1)), send(west, perm=moved(0, -1))
    plane_sums = lax.all_to_all(sums, BOTH, 0, 0, tiled=True, axis_index_groups=PLANE)
    sums_rows = call(pool_plane, shape((8, CH), BF), [], [], plane_sums)
    from_north = send(jnp.concatenate([placed[240:320], from_west[12:16], from_east[12:16]]), perm=moved(1, 0))
    from_south = send(jnp.concatenate([placed[0:80], from_west[0:4], from_east[0:4]]), perm=moved(-1, 0))
    parcel = jnp.concatenate([placed, from_west, from_east, from_north, from_south], axis=0)
    sums_rows, swapped, packed = lax.optimization_barrier((sums_rows, swapped, by_group(kernel_first)))
    letter = jnp.concatenate([packed, sums_rows[0:6], swapped], axis=0)
    letters = jnp.broadcast_to(letter[None], (NZ, 112, CH))
    letters, parcel = lax.optimization_barrier((letters, parcel))
    got = lax.all_to_all(letters, "space", 0, 0, tiled=True, axis_index_groups=ALONG_Z)
    later = [lax.ppermute(parcel, "tm", [(t, (t + k) % NY) for t in range(NY)]) for k in range(1, NY)]
    ordered, all_sums = call(
        arrange_first,
        (shape((NX, 336, CH), BF), shape((8, 128), F32)),
        [],
        [],
        got,
        jnp.asarray(FIRST_ROWS, BF),
    )
    own = lax.all_to_all(ordered, "space", 0, 0, tiled=True, axis_index_groups=ALONG_X)
    stack = call(
        first_act,
        shape((NY, FIELD, 3 * CH), BF),
        [
            pltpu.VMEM((GUARD + (ROWS + 4) * PITCH + GUARD, CH), F32),
            pltpu.VMEM((NY, 528, CH), BF),
            pltpu.VMEM((NY, FIELD, 3 * CH), BF),
            pltpu.SemaphoreType.DMA((NY,)),
            pltpu.SemaphoreType.DMA((NY,)),
        ],
        [SM, AT, AT, AT, AT],
        pos,
        parcel,
        *later,
        all_sums,
        vectors,
        jnp.asarray(CHANNEL_LANES, BF),
        jnp.asarray(GROUPS_OF_LANES),
        jnp.asarray(SQUARES_OF_LANES),
        flops=int(2e10),
        out_places=HB,
    )
    got_second, _ = lax.optimization_barrier((got, ordered))
    ordered_second = call(
        arrange_second,
        shape((432, CH), BF),
        [],
        [],
        got_second,
        jnp.asarray(SECOND_ROWS, BF),
        jnp.asarray(SECOND_LANES, BF),
    )
    own, stack, _ = lax.optimization_barrier((own, stack, ordered_second))
    other = lax.ppermute(own, "space", SIBLING)

    field, sums = call(
        first_conv,
        (shape((NY, RING, 128), F32), shape((SPACE, 128), F32)),
        [
            pltpu.VMEM((7, COLS, 48, CH), BF),
            pltpu.VMEM((3 * CH, 9 * 128), BF),
            pltpu.VMEM((NY, FIELD, 3 * CH), BF),
            pltpu.SemaphoreType.DMA((COLS,)),
            pltpu.SemaphoreType.DMA((NY,)),
        ],
        [SM, HB, AT, AT],
        pos,
        stack,
        own.reshape(NX, 7, 48, CH),
        other.reshape(NX, 7, 48, CH),
        vectors,
        jnp.asarray(PART_GROUPS),
        jnp.asarray(PART_GROUPS.T),
        jnp.asarray(PART_SQUARES),
        jnp.asarray(SECOND_LANES.T, BF),
    )
    all_sums = lax.all_to_all(sums, "space", 0, 0, tiled=True)
    own_second = lax.all_gather(ordered_second, "space", axis_index_groups=ALONG_X)
    own_second, _ = lax.optimization_barrier((own_second, field))
    other_second = lax.ppermute(own_second, "space", SIBLING)
    partial = call(
        second_conv,
        shape((NY, ROWS, WIDE, CH), BF),
        [
            pltpu.VMEM((27, COLS, 16, CH), BF),
            pltpu.VMEM((RING, 128), F32),
            pltpu.VMEM((NY, 384, 9 * 128), BF),
            pltpu.VMEM((NY, RING, 128), F32),
            pltpu.SemaphoreType.DMA((COLS,)),
            pltpu.SemaphoreType.DMA((NY,)),
        ],
        [SM, AT, HB, AT],
        pos,
        field,
        own_second.reshape(NX, 27, 16, CH),
        other_second.reshape(NX, 27, 16, CH),
        all_sums,
        vectors,
        jnp.asarray(PART_GROUPS.T),
        jnp.asarray(PART_SQUARES.T),
        jnp.asarray(PART_LANES, BF),
        grant=46,
    )
    parts = lax.all_to_all(partial, "tm", 0, 0, tiled=True)
    second_out = jnp.sum(parts.astype(F32), axis=0) + bias_second
    return (tile.astype(F32) + second_out).astype(BF)[None, None]


def solution(mesh):
    placed = (
        P("tm", "space", None, None, None),
        P(),
        P(),
        P(None, None, None, "space", "tm"),
        P(),
        P(),
        P(),
        P(None, None, None, "space", "tm"),
        P(),
    )
    return jax.shard_map(
        shards,
        mesh=mesh,
        in_specs=placed,
        out_specs=P("tm", "space", None, None, None),
        check_vma=False,
    )
```

```python
import functools

import jax
import jax.numpy as jnp
import numpy as np
from jax import lax
from jax.experimental import pallas as pl
from jax.experimental.pallas import tpu as pltpu
from jax.sharding import PartitionSpec as P

EPS = 1e-06
BF = jnp.bfloat16
F32 = jnp.float32
VM = pl.BlockSpec(memory_space=pltpu.VMEM)
SM = pl.BlockSpec(memory_space=pltpu.SMEM)
AT = pl.BlockSpec(memory_space=pl.ANY)
HB = pl.BlockSpec(memory_space=pltpu.HBM)
HIGH = lax.Precision.HIGHEST

NZ, NX, NC, NY = 8, 4, 2, 4
COLS = NX * NC
SPACE = NZ * COLS
ROWS, WIDE, PITCH = 8, 40, 48
CH, PART, WG = 384, 96, 12
GUARD = 16
LEAD = 8
RING = LEAD + (ROWS + 2) * PITCH + 8
FIELD = RING + 2 * PITCH
BOTH = ("tm", "space")
ALONG_Z = [[z * COLS + q for z in range(NZ)] for q in range(COLS)]
ALONG_X = [[z * COLS + x * NC + c for x in range(NX)] for z in range(NZ) for c in range(NC)]
PLANE = [[y * SPACE + z * COLS + q for y in range(NY) for q in range(COLS)] for z in range(NZ)]
SIBLING = [(s, s ^ 1) for s in range(SPACE)]


def moved(down, right):
    return [(s, (s + COLS * down + right) % SPACE) for s in range(SPACE)]


SWAP = [
    (y * SPACE + z * COLS + q, (z // 2) * SPACE + (2 * y + z % 2) * COLS + q)
    for y in range(NY)
    for z in range(NZ)
    for q in range(COLS)
]


def one_hot(rows, cols, pairs):
    out = np.zeros((rows, cols), np.float32)
    for r, c in pairs:
        out[r, c] = 1.0
    return out


CHANNEL_LANES = one_hot(
    CH, CH, [(6 * (8 * z + q) + i, 48 * q + 6 * z + i) for z in range(8) for q in range(8) for i in range(6)]
)
GROUPS_OF = one_hot(CH, 128, [(c, c // WG) for c in range(CH)])
SQUARES_OF = np.roll(GROUPS_OF, 64, axis=1)
GROUPS_OF_LANES = (CHANNEL_LANES.T @ GROUPS_OF).T
SQUARES_OF_LANES = (CHANNEL_LANES.T @ SQUARES_OF).T
PART_GROUPS = one_hot(128, 128, [(c, c // WG) for c in range(PART)])
PART_SQUARES = np.roll(PART_GROUPS, 64, axis=1)
EDGES = one_hot(
    32,
    320,
    [(2 * r + c, 40 * r + c) for r in range(8) for c in range(2)]
    + [(16 + 2 * r + c, 40 * r + 38 + c) for r in range(8) for c in range(2)],
)
FIRST_ROWS = one_hot(
    336, 384, [(48 * g + 6 * z + i, 48 * z + 6 * g + i) for g in range(7) for z in range(8) for i in range(6)]
)
SECOND_ROWS = one_hot(
    112, 96, [(16 * g + 6 * h + i, 48 * h + 6 * g + i) for g in range(7) for h in range(2) for i in range(6)]
)
SECOND_LANES = one_hot(512, CH, [(128 * y + o, PART * y + o) for y in range(4) for o in range(PART)])
PART_LANES = one_hot(
    128, 128, [(48 * h + 6 * q + i, 16 * q + 6 * h + i) for h in range(2) for q in range(8) for i in range(6)]
)


def dot(a, b):
    return jnp.dot(a, b, preferred_element_type=F32)


def exact(a, b):
    return jnp.dot(a, b, preferred_element_type=F32, precision=HIGH)


def merge(sums, count, groups_t, squares_t):
    mean = jnp.mean(sums, axis=0, keepdims=True)
    off = sums - mean
    between = count * jnp.sum(off * off, axis=0, keepdims=True)
    within = jnp.sum(sums, axis=0, keepdims=True)
    rows = jnp.concatenate([mean, between, jnp.zeros((6, 128), F32)], axis=0)
    by_lane = exact(rows, groups_t)
    spread = (by_lane[1:2] + exact(tall(within), squares_t)[0:1]) * (1.0 / (count * sums.shape[0]))
    return by_lane[0:1], lax.rsqrt(spread + EPS)


def pool(rows, count):
    mean = jnp.mean(rows, axis=0, keepdims=True)
    off = rows - mean
    between = count * jnp.sum(off * off, axis=0, keepdims=True)
    squares = jnp.sum(rows, axis=0, keepdims=True) + pltpu.roll(tall(between), 64, axis=1)[0:1]
    return jnp.where(lax.broadcasted_iota(jnp.int32, (1, 128), 1) < 64, mean, squares)


def tall(row):
    return jnp.broadcast_to(row, (8, row.shape[1]))


def chosen(part):
    channel = lax.broadcasted_iota(jnp.int32, (CH, 128), 0)
    lane = lax.broadcasted_iota(jnp.int32, (CH, 128), 1)
    return ((channel == part * PART + lane) & (lane < PART)).astype(F32)


def silu(u):
    return u / (1.0 + jnp.exp(-u))


def measure_tile(
    tile_ref, lanes_ref, groups_ref, groups_t_ref, squares_ref, edges_ref,
    placed_ref, west_ref, east_ref, sums_ref,
):
    tile = tile_ref[...]
    placed = dot(tile, lanes_ref[...]).astype(BF)
    placed_ref[...] = placed
    edges = dot(edges_ref[...], placed).astype(BF)
    west_ref[...] = edges[0:16]
    east_ref[...] = edges[16:32]
    wide = tile.astype(F32)
    mean = exact(tall(jnp.sum(wide, axis=0, keepdims=True)), groups_ref[...]) * (1.0 / (320 * WG))
    off = wide - exact(mean, groups_t_ref[...])[0:1]
    squares = exact(tall(jnp.sum(off * off, axis=0, keepdims=True)), squares_ref[...])
    sums_ref[...] = jnp.broadcast_to((mean + squares)[0:1], sums_ref.shape)


def pool_plane(sums_ref, out_ref):
    row = pool(sums_ref[...], 320.0 * WG)
    hi = row.astype(BF).astype(F32)
    mid = (row - hi).astype(BF).astype(F32)
    rows = jnp.concatenate([hi, mid, row - hi - mid, jnp.zeros((5, 128), F32)], axis=0)
    out_ref[...] = jnp.concatenate([rows, jnp.zeros((8, CH - 128), F32)], axis=1).astype(BF)


def arrange_first(got_ref, rows_ref, out_ref, sums_ref):
    blocks = [got_ref[z, 0:48, :] for z in range(NZ)]
    ordered = dot(rows_ref[...], jnp.concatenate(blocks, axis=0)).astype(BF)
    for copy in range(NX):
        out_ref[copy] = ordered
    wide = [b[:, 0:128].astype(F32) for b in blocks]
    sums_ref[...] = jnp.concatenate([b[42:43] + b[43:44] + b[44:45] for b in wide], axis=0)


def arrange_second(got_ref, rows_ref, out_ref):
    parts = []
    for y in range(NY):
        pair = jnp.concatenate([got_ref[2 * y + h, 48:96, :] for h in range(2)], axis=0)
        parts.append(dot(rows_ref[...], pair))
    for k in range(4):
        whole = jnp.concatenate([part[:, PART * k : PART * k + PART] for part in parts], axis=1).astype(BF)
        for g in range(7):
            tap = 4 * g + k
            if tap < 27:
                out_ref[16 * tap : 16 * tap + 16, :] = whole[16 * g : 16 * g + 16]


def first_act(
    pos_ref, lat0_ref, lat1_ref, lat2_ref, lat3_ref, sums_ref, vectors_ref, lanes_ref, groups_t_ref, squares_t_ref,
    stack_ref, flat, lats, stack, in_sems, out_sems,
):
    arrivals = [
        pltpu.make_async_copy(lat_ref, lats.at[back], in_sems.at[back])
        for back, lat_ref in enumerate((lat0_ref, lat1_ref, lat2_ref, lat3_ref))
    ]
    for arrival in arrivals:
        arrival.start()
    row, col = pos_ref[0] // COLS, pos_ref[0] % COLS
    mean_l, scale_l = merge(sums_ref[...], 320.0 * WG * NY * COLS, groups_t_ref[...], squares_t_ref[...])
    vectors = vectors_ref[...]
    high = vectors.astype(BF)
    middle = (vectors - high.astype(F32)).astype(BF)
    low = (vectors - high.astype(F32) - middle.astype(F32)).astype(BF)
    lanes = lanes_ref[...]
    affine = dot(high, lanes) + dot(middle, lanes) + dot(low, lanes)
    scale_l = scale_l * affine[0:1]
    shift_l = affine[1:2]
    has_w = (col > 0).astype(F32)
    has_e = (col < COLS - 1).astype(F32)
    has_n = (row > 0).astype(F32)
    has_s = (row < NZ - 1).astype(F32)
    flat[...] = jnp.zeros_like(flat)
    leaving = []
    for back in range(NY):
        t = (pos_ref[1] + (NY - back)) % NY
        arrivals[back].wait()
        act = silu((lats[back].astype(F32) - mean_l) * scale_l + shift_l)
        for r in range(-2, ROWS + 2):
            base = GUARD + PITCH * (r + 2)
            if 0 <= r < ROWS:
                cells = act[WIDE * r : WIDE * r + WIDE]
                left, right = act[320 + 2 * r : 322 + 2 * r] * has_w, act[336 + 2 * r : 338 + 2 * r] * has_e
            else:
                start, at, inside = (352, r + 2, has_n) if r < 0 else (440, r - ROWS, has_s)
                cells = act[start + WIDE * at : start + WIDE * at + WIDE] * inside
                left = act[start + 80 + 2 * at : start + 82 + 2 * at] * (inside * has_w)
                right = act[start + 84 + 2 * at : start + 86 + 2 * at] * (inside * has_e)
            flat[base : base + WIDE, :] = cells
            flat[base + WIDE : base + WIDE + 2, :] = right
            flat[base - 2 : base, :] = left
        for d in range(3):
            start = GUARD - LEAD + d - 1
            stack[back, :, CH * d : CH * d + CH] = flat[start : start + FIELD, :].astype(BF)
        leaving.append(pltpu.make_async_copy(stack.at[back], stack_ref.at[t], out_sems.at[back]))
        leaving[back].start()
    for leave in leaving:
        leave.wait()


def land(core, own_ref, other_ref, slots, sems):
    copies = []
    for x in range(NX):
        at = NC * x
        copies.append(pltpu.make_async_copy(own_ref.at[x], slots.at[:, at + core], sems.at[at]))
        copies.append(pltpu.make_async_copy(other_ref.at[x], slots.at[:, at + 1 - core], sems.at[at + 1]))
    for copy in copies:
        copy.start()
    return copies


def first_conv(
    pos_ref, stack_ref, own_ref, other_ref, vectors_ref, part_ref, part_t_ref, part_squares_ref, spread_ref,
    out_ref, sums_ref, packed, weights, stack, sems, stack_sems,
):
    landing = land(pos_ref[0] % NC, own_ref, other_ref, packed, sems)
    arrivals = [pltpu.make_async_copy(stack_ref.at[t], stack.at[t], stack_sems.at[t]) for t in range(NY)]
    for arrival in arrivals:
        arrival.start()
    bias = exact(vectors_ref[...], chosen(pos_ref[1]))[2:3]
    for copy in landing:
        copy.wait()
    for g in range(7):
        taps = dot(packed[g].reshape(CH, CH), spread_ref[...]).astype(BF)
        for tap in range(4 * g, min(4 * g + 4, 27)):
            down, right = CH * (tap % 3), 128 * (tap // 3)
            weights[down : down + CH, right : right + 128] = taps[:, 128 * (tap % 4) : 128 * (tap % 4) + 128]
    totals = [None] * NY
    for t in range(NY):
        first = max(0, t + 3 - NY)
        arrivals[t].wait()
        product = dot(stack[t], weights[:, CH * first :])
        for dt in range(first, 3):
            to = t + 2 - dt
            part = product[:, CH * (dt - first) : CH * (dt - first) + CH]
            term = part[0:RING, 0:128]
            for dy in (1, 2):
                term = term + part[PITCH * dy : PITCH * dy + RING, 128 * dy : 128 * dy + 128]
            totals[to] = term if totals[to] is None else totals[to] + term
    at = lax.broadcasted_iota(jnp.int32, (RING, 1), 0) - (LEAD + PITCH)
    inside = ((at >= 0) & (at < PITCH * ROWS) & (at % PITCH < WIDE)).astype(F32)
    sums = None
    for t in range(NY):
        totals[t] = totals[t] + bias
        out_ref[t] = totals[t]
        line = jnp.sum(totals[t] * inside, axis=0, keepdims=True)
        sums = line if sums is None else sums + line
    mean = exact(tall(sums), part_ref[...]) * (1.0 / (320 * NY * WG))
    mean_l = exact(mean, part_t_ref[...])[0:1]
    sums = None
    for t in range(NY):
        off = (totals[t] - mean_l) * inside
        line = jnp.sum(off * off, axis=0, keepdims=True)
        sums = line if sums is None else sums + line
    squares = exact(tall(sums), part_squares_ref[...])
    sums_ref[...] = jnp.broadcast_to((mean + squares)[0:1], (SPACE, 128))


def second_conv(
    pos_ref, field_ref, own_ref, other_ref, sums_ref, vectors_ref, groups_t_ref, squares_t_ref, order_ref, out_ref,
    weights, flat, stack, field, sems, field_sems,
):
    arrivals = [pltpu.make_async_copy(field_ref.at[t], field.at[t], field_sems.at[t]) for t in range(NY)]
    for arrival in arrivals:
        arrival.start()
    landing = land(pos_ref[0] % NC, own_ref, other_ref, weights, sems)
    row, col = pos_ref[0] // COLS, pos_ref[0] % COLS
    mean_l, scale_l = merge(sums_ref[...], 320.0 * NY * WG, groups_t_ref[...], squares_t_ref[...])
    affine = exact(vectors_ref[...], chosen(pos_ref[1]))
    scale_l = scale_l * affine[3:4]
    shift_l = affine[4:5]

    at = lax.broadcasted_iota(jnp.int32, (RING, 1), 0) - LEAD
    outside = (at < 0) & (row == 0) | (at < PITCH - 2) & (row == 0)
    outside = outside | (at >= PITCH * (ROWS + 1) - 1) & (row == NZ - 1)
    at = (at + PITCH) % PITCH
    outside = outside | (at == WIDE) & (col == COLS - 1) | (at == PITCH - 1) & (col == 0)
    keep = 1.0 - outside.astype(F32)
    for t in range(NY):
        arrivals[t].wait()
        act = silu((field[t] - mean_l) * scale_l + shift_l) * keep
        flat[...] = dot(act.astype(BF), order_ref[...])
        for dy in range(3):
            for dx in range(3):
                start = LEAD + PITCH * dy + dx - 1
                lane = 128 * (3 * dy + dx)
                stack[t, :, lane : lane + 128] = flat[start : start + 384, :].astype(BF)
    for copy in landing:
        copy.wait()
    for t in range(NY):
        total = None
        for dt in range(3):
            source = t - 2 + dt
            if source < 0:
                continue
            term = dot(stack[source], weights[9 * dt : 9 * dt + 9].reshape(1152, CH))
            total = term if total is None else total + term
        for r in range(ROWS):
            out_ref[t, r] = total[PITCH * r : PITCH * r + WIDE].astype(BF)


def call(body, outs, scratch, places, *args, flops=0, out_places=None, grant=50):
    return pl.pallas_call(
        body,
        out_shape=outs,
        in_specs=[*places, *[VM] * (len(args) - len(places))],
        out_specs=jax.tree.map(lambda _: VM, outs) if out_places is None else out_places,
        scratch_shapes=scratch,
        compiler_params=pltpu.CompilerParams(vmem_limit_bytes=grant * 1024 * 1024),
        cost_estimate=pl.CostEstimate(flops=flops, bytes_accessed=0, transcendentals=0),
    )(*args)


def shape(dims, dtype):
    return jax.ShapeDtypeStruct(dims, dtype)


def by_group(kernel):
    taps = jnp.pad(kernel.reshape(27, 6, PART), ((0, 1), (0, 0), (0, 0))).reshape(7, 4, 6, PART)
    return jnp.transpose(taps, (0, 2, 1, 3)).reshape(42, CH)


def shards(
    latents,
    gain_first,
    shift_first,
    kernel_first,
    bias_first,
    gain_second,
    shift_second,
    kernel_second,
    bias_second,
):
    space = lax.axis_index("space")
    frame = lax.axis_index("tm")
    pos = jnp.stack([space, frame]).astype(jnp.int32)
    vectors = jnp.stack(
        [gain_first, shift_first, bias_first, gain_second, shift_second, bias_second, bias_second, bias_second]
    )
    tile = latents[0, 0]
    flat_tile = tile.reshape(ROWS * WIDE, CH)

    swapped = lax.ppermute(jnp.pad(by_group(kernel_second), ((0, 6), (0, 0))), BOTH, SWAP)
    placed, west, east, sums = call(
        measure_tile,
        (shape((320, CH), BF), shape((16, CH), BF), shape((16, CH), BF), shape((NY * COLS, 128), F32)),
        [],
        [],
        flat_tile,
        jnp.asarray(CHANNEL_LANES, BF),
        jnp.asarray(GROUPS_OF),
        jnp.asarray(GROUPS_OF.T),
        jnp.asarray(SQUARES_OF),
        jnp.asarray(EDGES, BF),
        grant=60,
    )
    send = functools.partial(lax.ppermute, axis_name="space")
    from_west, from_east = send(east, perm=moved(0, 1)), send(west, perm=moved(0, -1))
    plane_sums = lax.all_to_all(sums, BOTH, 0, 0, tiled=True, axis_index_groups=PLANE)
    sums_rows = call(pool_plane, shape((8, CH), BF), [], [], plane_sums)
    from_north = send(jnp.concatenate([placed[240:320], from_west[12:16], from_east[12:16]]), perm=moved(1, 0))
    from_south = send(jnp.concatenate([placed[0:80], from_west[0:4], from_east[0:4]]), perm=moved(-1, 0))
    parcel = jnp.concatenate([placed, from_west, from_east, from_north, from_south], axis=0)
    sums_rows, swapped, packed = lax.optimization_barrier((sums_rows, swapped, by_group(kernel_first)))
    letter = jnp.concatenate([packed, sums_rows[0:6], swapped], axis=0)
    letters = jnp.broadcast_to(letter[None], (NZ, 96, CH))
    letters, parcel = lax.optimization_barrier((letters, parcel))
    got = lax.all_to_all(letters, "space", 0, 0, tiled=True, axis_index_groups=ALONG_Z)
    later = [lax.ppermute(parcel, "tm", [(t, (t + k) % NY) for t in range(NY)]) for k in range(1, NY)]
    ordered, all_sums = call(
        arrange_first,
        (shape((NX, 336, CH), BF), shape((8, 128), F32)),
        [],
        [],
        got,
        jnp.asarray(FIRST_ROWS, BF),
    )
    got_second, _ = lax.optimization_barrier((got, ordered))
    ordered_second = call(
        arrange_second,
        shape((432, CH), BF),
        [],
        [],
        got_second,
        jnp.asarray(SECOND_ROWS, BF),
    )
    ordered, ordered_second = lax.optimization_barrier((ordered, ordered_second))
    own = lax.all_to_all(ordered, "space", 0, 0, tiled=True, axis_index_groups=ALONG_X)
    stack = call(
        first_act,
        shape((NY, FIELD, 3 * CH), BF),
        [
            pltpu.VMEM((GUARD + (ROWS + 4) * PITCH + GUARD, CH), F32),
            pltpu.VMEM((NY, 528, CH), BF),
            pltpu.VMEM((NY, FIELD, 3 * CH), BF),
            pltpu.SemaphoreType.DMA((NY,)),
            pltpu.SemaphoreType.DMA((NY,)),
        ],
        [SM, AT, AT, AT, AT],
        pos,
        parcel,
        *later,
        all_sums,
        vectors,
        jnp.asarray(CHANNEL_LANES, BF),
        jnp.asarray(GROUPS_OF_LANES),
        jnp.asarray(SQUARES_OF_LANES),
        flops=int(2e10),
        out_places=HB,
    )
    own, stack = lax.optimization_barrier((own, stack))
    other = lax.ppermute(own, "space", SIBLING)

    field, sums = call(
        first_conv,
        (shape((NY, RING, 128), F32), shape((SPACE, 128), F32)),
        [
            pltpu.VMEM((7, COLS, 48, CH), BF),
            pltpu.VMEM((3 * CH, 9 * 128), BF),
            pltpu.VMEM((NY, FIELD, 3 * CH), BF),
            pltpu.SemaphoreType.DMA((COLS,)),
            pltpu.SemaphoreType.DMA((NY,)),
        ],
        [SM, HB, AT, AT],
        pos,
        stack,
        own.reshape(NX, 7, 48, CH),
        other.reshape(NX, 7, 48, CH),
        vectors,
        jnp.asarray(PART_GROUPS),
        jnp.asarray(PART_GROUPS.T),
        jnp.asarray(PART_SQUARES),
        jnp.asarray(SECOND_LANES.T, BF),
    )
    all_sums = lax.all_to_all(sums, "space", 0, 0, tiled=True)
    own_second = lax.all_gather(ordered_second, "space", axis_index_groups=ALONG_X)
    own_second, _ = lax.optimization_barrier((own_second, field))
    other_second = lax.ppermute(own_second, "space", SIBLING)
    partial = call(
        second_conv,
        shape((NY, ROWS, WIDE, CH), BF),
        [
            pltpu.VMEM((27, COLS, 16, CH), BF),
            pltpu.VMEM((RING, 128), F32),
            pltpu.VMEM((NY, 384, 9 * 128), BF),
            pltpu.VMEM((NY, RING, 128), F32),
            pltpu.SemaphoreType.DMA((COLS,)),
            pltpu.SemaphoreType.DMA((NY,)),
        ],
        [SM, AT, HB, AT],
        pos,
        field,
        own_second.reshape(NX, 27, 16, CH),
        other_second.reshape(NX, 27, 16, CH),
        all_sums,
        vectors,
        jnp.asarray(PART_GROUPS.T),
        jnp.asarray(PART_SQUARES.T),
        jnp.asarray(PART_LANES, BF),
        grant=46,
    )
    parts = lax.all_to_all(partial, "tm", 0, 0, tiled=True)
    second_out = jnp.sum(parts.astype(F32), axis=0) + bias_second
    return (tile.astype(F32) + second_out).astype(BF)[None, None]


def solution(mesh):
    placed = (
        P("tm", "space", None, None, None),
        P(),
        P(),
        P(None, None, None, "space", "tm"),
        P(),
        P(),
        P(),
        P(None, None, None, "space", "tm"),
        P(),
    )
    return jax.shard_map(
        shards,
        mesh=mesh,
        in_specs=placed,
        out_specs=P("tm", "space", None, None, None),
        check_vma=False,
    )
```

```python
import functools

import jax
import jax.numpy as jnp
import numpy as np
from jax import lax
from jax.experimental import pallas as pl
from jax.experimental.pallas import tpu as pltpu
from jax.sharding import PartitionSpec as P

EPS = 1e-06
BF = jnp.bfloat16
F32 = jnp.float32
VM = pl.BlockSpec(memory_space=pltpu.VMEM)
SM = pl.BlockSpec(memory_space=pltpu.SMEM)
AT = pl.BlockSpec(memory_space=pl.ANY)
HB = pl.BlockSpec(memory_space=pltpu.HBM)
HIGH = lax.Precision.HIGHEST

NZ, NX, NC, NY = 8, 4, 2, 4
COLS = NX * NC
SPACE = NZ * COLS
ROWS, WIDE, PITCH = 8, 40, 48
CH, PART, WG = 384, 96, 12
GUARD = 16
LEAD = 8
RING = LEAD + (ROWS + 2) * PITCH + 8
FIELD = RING + 2 * PITCH
BOTH = ("tm", "space")
ALONG_Z = [[z * COLS + q for z in range(NZ)] for q in range(COLS)]
ALONG_X = [[z * COLS + x * NC + c for x in range(NX)] for z in range(NZ) for c in range(NC)]
PLANE = [[y * SPACE + z * COLS + q for y in range(NY) for q in range(COLS)] for z in range(NZ)]
SIBLING = [(s, s ^ 1) for s in range(SPACE)]


def moved(down, right):
    return [(s, (s + COLS * down + right) % SPACE) for s in range(SPACE)]


SWAP = [
    (y * SPACE + z * COLS + q, (z // 2) * SPACE + (2 * y + z % 2) * COLS + q)
    for y in range(NY)
    for z in range(NZ)
    for q in range(COLS)
]


def one_hot(rows, cols, pairs):
    out = np.zeros((rows, cols), np.float32)
    for r, c in pairs:
        out[r, c] = 1.0
    return out


CHANNEL_LANES = one_hot(
    CH, CH, [(6 * (8 * z + q) + i, 48 * q + 6 * z + i) for z in range(8) for q in range(8) for i in range(6)]
)
GROUPS_OF = one_hot(CH, 128, [(c, c // WG) for c in range(CH)])
SQUARES_OF = np.roll(GROUPS_OF, 64, axis=1)
GROUPS_OF_LANES = (CHANNEL_LANES.T @ GROUPS_OF).T
SQUARES_OF_LANES = (CHANNEL_LANES.T @ SQUARES_OF).T
PART_GROUPS = one_hot(128, 128, [(c, c // WG) for c in range(PART)])
PART_SQUARES = np.roll(PART_GROUPS, 64, axis=1)
EDGES = one_hot(
    32,
    320,
    [(2 * r + c, 40 * r + c) for r in range(8) for c in range(2)]
    + [(16 + 2 * r + c, 40 * r + 38 + c) for r in range(8) for c in range(2)],
)
FIRST_ROWS = one_hot(
    336, 384, [(48 * g + 6 * z + i, 48 * z + 6 * g + i) for g in range(7) for z in range(8) for i in range(6)]
)
SECOND_ROWS = one_hot(
    112, 96, [(16 * g + 6 * h + i, 48 * h + 6 * g + i) for g in range(7) for h in range(2) for i in range(6)]
)
SECOND_LANES = one_hot(512, CH, [(128 * y + o, PART * y + o) for y in range(4) for o in range(PART)])
PART_LANES = one_hot(
    128, 128, [(48 * h + 6 * q + i, 16 * q + 6 * h + i) for h in range(2) for q in range(8) for i in range(6)]
)


def dot(a, b):
    return jnp.dot(a, b, preferred_element_type=F32)


def exact(a, b):
    return jnp.dot(a, b, preferred_element_type=F32, precision=HIGH)


def merge(sums, count, groups_t, squares_t):
    mean = jnp.mean(sums, axis=0, keepdims=True)
    off = sums - mean
    between = count * jnp.sum(off * off, axis=0, keepdims=True)
    within = jnp.sum(sums, axis=0, keepdims=True)
    rows = jnp.concatenate([mean, between, jnp.zeros((6, 128), F32)], axis=0)
    by_lane = exact(rows, groups_t)
    spread = (by_lane[1:2] + exact(tall(within), squares_t)[0:1]) * (1.0 / (count * sums.shape[0]))
    return by_lane[0:1], lax.rsqrt(spread + EPS)


def pool(rows, count):
    mean = jnp.mean(rows, axis=0, keepdims=True)
    off = rows - mean
    between = count * jnp.sum(off * off, axis=0, keepdims=True)
    squares = jnp.sum(rows, axis=0, keepdims=True) + pltpu.roll(tall(between), 64, axis=1)[0:1]
    return jnp.where(lax.broadcasted_iota(jnp.int32, (1, 128), 1) < 64, mean, squares)


def tall(row):
    return jnp.broadcast_to(row, (8, row.shape[1]))


def chosen(part):
    channel = lax.broadcasted_iota(jnp.int32, (CH, 128), 0)
    lane = lax.broadcasted_iota(jnp.int32, (CH, 128), 1)
    return ((channel == part * PART + lane) & (lane < PART)).astype(F32)


def silu(u):
    return u / (1.0 + jnp.exp(-u))


def measure_tile(
    tile_ref, lanes_ref, groups_ref, groups_t_ref, squares_ref, edges_ref,
    placed_ref, west_ref, east_ref, sums_ref,
):
    tile = tile_ref[...]
    placed = dot(tile, lanes_ref[...]).astype(BF)
    placed_ref[...] = placed
    edges = dot(edges_ref[...], placed).astype(BF)
    west_ref[...] = edges[0:16]
    east_ref[...] = edges[16:32]
    wide = tile.astype(F32)
    mean = exact(tall(jnp.sum(wide, axis=0, keepdims=True)), groups_ref[...]) * (1.0 / (320 * WG))
    off = wide - exact(mean, groups_t_ref[...])[0:1]
    squares = exact(tall(jnp.sum(off * off, axis=0, keepdims=True)), squares_ref[...])
    sums_ref[...] = jnp.broadcast_to((mean + squares)[0:1], sums_ref.shape)


def pool_plane(sums_ref, out_ref):
    row = pool(sums_ref[...], 320.0 * WG)
    hi = row.astype(BF).astype(F32)
    mid = (row - hi).astype(BF).astype(F32)
    rows = jnp.concatenate([hi, mid, row - hi - mid, jnp.zeros((5, 128), F32)], axis=0)
    out_ref[...] = jnp.concatenate([rows, jnp.zeros((8, CH - 128), F32)], axis=1).astype(BF)


def arrange_first(got_ref, rows_ref, out_ref, sums_ref):
    blocks = [got_ref[z, 0:48, :] for z in range(NZ)]
    ordered = dot(rows_ref[...], jnp.concatenate(blocks, axis=0)).astype(BF)
    for copy in range(NX):
        out_ref[copy] = ordered
    wide = [b[:, 0:128].astype(F32) for b in blocks]
    sums_ref[...] = jnp.concatenate([b[42:43] + b[43:44] + b[44:45] for b in wide], axis=0)


def arrange_second(got_ref, rows_ref, out_ref):
    parts = []
    for y in range(NY):
        pair = jnp.concatenate([got_ref[2 * y + h, 48:96, :] for h in range(2)], axis=0)
        parts.append(dot(rows_ref[...], pair))
    for k in range(4):
        whole = jnp.concatenate([part[:, PART * k : PART * k + PART] for part in parts], axis=1).astype(BF)
        for g in range(7):
            tap = 4 * g + k
            if tap < 27:
                out_ref[16 * tap : 16 * tap + 16, :] = whole[16 * g : 16 * g + 16]


def first_act(
    pos_ref, lat0_ref, lat1_ref, lat2_ref, lat3_ref, sums_ref, vectors_ref, lanes_ref, groups_t_ref, squares_t_ref,
    stack_ref, flat, lats, stack, in_sems, out_sems,
):
    arrivals = [
        pltpu.make_async_copy(lat_ref, lats.at[back], in_sems.at[back])
        for back, lat_ref in enumerate((lat0_ref, lat1_ref, lat2_ref, lat3_ref))
    ]
    for arrival in arrivals:
        arrival.start()
    row, col = pos_ref[0] // COLS, pos_ref[0] % COLS
    mean_l, scale_l = merge(sums_ref[...], 320.0 * WG * NY * COLS, groups_t_ref[...], squares_t_ref[...])
    vectors = vectors_ref[...]
    high = vectors.astype(BF)
    middle = (vectors - high.astype(F32)).astype(BF)
    low = (vectors - high.astype(F32) - middle.astype(F32)).astype(BF)
    lanes = lanes_ref[...]
    affine = dot(high, lanes) + dot(middle, lanes) + dot(low, lanes)
    scale_l = scale_l * affine[0:1]
    shift_l = affine[1:2]
    has_w = (col > 0).astype(F32)
    has_e = (col < COLS - 1).astype(F32)
    has_n = (row > 0).astype(F32)
    has_s = (row < NZ - 1).astype(F32)
    flat[...] = jnp.zeros_like(flat)
    leaving = []
    for back in range(NY):
        t = (pos_ref[1] + (NY - back)) % NY
        arrivals[back].wait()
        act = silu((lats[back].astype(F32) - mean_l) * scale_l + shift_l)
        for r in range(-2, ROWS + 2):
            base = GUARD + PITCH * (r + 2)
            if 0 <= r < ROWS:
                cells = act[WIDE * r : WIDE * r + WIDE]
                left, right = act[320 + 2 * r : 322 + 2 * r] * has_w, act[336 + 2 * r : 338 + 2 * r] * has_e
            else:
                start, at, inside = (352, r + 2, has_n) if r < 0 else (440, r - ROWS, has_s)
                cells = act[start + WIDE * at : start + WIDE * at + WIDE] * inside
                left = act[start + 80 + 2 * at : start + 82 + 2 * at] * (inside * has_w)
                right = act[start + 84 + 2 * at : start + 86 + 2 * at] * (inside * has_e)
            flat[base : base + WIDE, :] = cells
            flat[base + WIDE : base + WIDE + 2, :] = right
            flat[base - 2 : base, :] = left
        for d in range(3):
            start = GUARD - LEAD + d - 1
            stack[back, :, CH * d : CH * d + CH] = flat[start : start + FIELD, :].astype(BF)
        leaving.append(pltpu.make_async_copy(stack.at[back], stack_ref.at[t], out_sems.at[back]))
        leaving[back].start()
    for leave in leaving:
        leave.wait()


def land(core, own_ref, other_ref, slots, sems):
    copies = []
    for x in range(NX):
        at = NC * x
        copies.append(pltpu.make_async_copy(own_ref.at[x], slots.at[:, at + core], sems.at[at]))
        copies.append(pltpu.make_async_copy(other_ref.at[x], slots.at[:, at + 1 - core], sems.at[at + 1]))
    for copy in copies:
        copy.start()
    return copies


def first_conv(
    pos_ref, stack_ref, own_ref, other_ref, vectors_ref, part_ref, part_t_ref, part_squares_ref, spread_ref,
    out_ref, sums_ref, packed, weights, stack, sems, stack_sems,
):
    landing = land(pos_ref[0] % NC, own_ref, other_ref, packed, sems)
    arrivals = [pltpu.make_async_copy(stack_ref.at[t], stack.at[t], stack_sems.at[t]) for t in range(NY)]
    for arrival in arrivals:
        arrival.start()
    bias = exact(vectors_ref[...], chosen(pos_ref[1]))[2:3]
    for copy in landing:
        copy.wait()
    for g in range(7):
        taps = dot(packed[g].reshape(CH, CH), spread_ref[...]).astype(BF)
        for tap in range(4 * g, min(4 * g + 4, 27)):
            down, right = CH * (tap % 3), 128 * (tap // 3)
            weights[down : down + CH, right : right + 128] = taps[:, 128 * (tap % 4) : 128 * (tap % 4) + 128]
    totals = [None] * NY
    for t in range(NY):
        first = max(0, t + 3 - NY)
        arrivals[t].wait()
        product = dot(stack[t], weights[:, CH * first :])
        for dt in range(first, 3):
            to = t + 2 - dt
            part = product[:, CH * (dt - first) : CH * (dt - first) + CH]
            term = part[0:RING, 0:128]
            for dy in (1, 2):
                term = term + part[PITCH * dy : PITCH * dy + RING, 128 * dy : 128 * dy + 128]
            totals[to] = term if totals[to] is None else totals[to] + term
    at = lax.broadcasted_iota(jnp.int32, (RING, 1), 0) - (LEAD + PITCH)
    inside = ((at >= 0) & (at < PITCH * ROWS) & (at % PITCH < WIDE)).astype(F32)
    sums = None
    for t in range(NY):
        totals[t] = totals[t] + bias
        out_ref[t] = totals[t]
        line = jnp.sum(totals[t] * inside, axis=0, keepdims=True)
        sums = line if sums is None else sums + line
    mean = exact(tall(sums), part_ref[...]) * (1.0 / (320 * NY * WG))
    mean_l = exact(mean, part_t_ref[...])[0:1]
    sums = None
    for t in range(NY):
        off = (totals[t] - mean_l) * inside
        line = jnp.sum(off * off, axis=0, keepdims=True)
        sums = line if sums is None else sums + line
    squares = exact(tall(sums), part_squares_ref[...])
    sums_ref[...] = jnp.broadcast_to((mean + squares)[0:1], (SPACE, 128))


def second_conv(
    pos_ref, field_ref, own_ref, other_ref, sums_ref, vectors_ref, groups_t_ref, squares_t_ref, order_ref, out_ref,
    weights, flat, stack, field, sems, field_sems,
):
    arrivals = [pltpu.make_async_copy(field_ref.at[t], field.at[t], field_sems.at[t]) for t in range(NY)]
    for arrival in arrivals:
        arrival.start()
    landing = land(pos_ref[0] % NC, own_ref, other_ref, weights, sems)
    row, col = pos_ref[0] // COLS, pos_ref[0] % COLS
    mean_l, scale_l = merge(sums_ref[...], 320.0 * NY * WG, groups_t_ref[...], squares_t_ref[...])
    affine = exact(vectors_ref[...], chosen(pos_ref[1]))
    scale_l = scale_l * affine[3:4]
    shift_l = affine[4:5]

    at = lax.broadcasted_iota(jnp.int32, (RING, 1), 0) - LEAD
    outside = (at < 0) & (row == 0) | (at < PITCH - 2) & (row == 0)
    outside = outside | (at >= PITCH * (ROWS + 1) - 1) & (row == NZ - 1)
    at = (at + PITCH) % PITCH
    outside = outside | (at == WIDE) & (col == COLS - 1) | (at == PITCH - 1) & (col == 0)
    keep = 1.0 - outside.astype(F32)
    for t in range(NY):
        arrivals[t].wait()
        act = silu((field[t] - mean_l) * scale_l + shift_l) * keep
        flat[...] = dot(act.astype(BF), order_ref[...])
        for dy in range(3):
            for dx in range(3):
                start = LEAD + PITCH * dy + dx - 1
                lane = 128 * (3 * dy + dx)
                stack[t, :, lane : lane + 128] = flat[start : start + 384, :].astype(BF)
    for copy in landing:
        copy.wait()
    for t in range(NY):
        total = None
        for dt in range(3):
            source = t - 2 + dt
            if source < 0:
                continue
            term = dot(stack[source], weights[9 * dt : 9 * dt + 9].reshape(1152, CH))
            total = term if total is None else total + term
        for r in range(ROWS):
            out_ref[t, r] = total[PITCH * r : PITCH * r + WIDE].astype(BF)


def call(body, outs, scratch, places, *args, flops=0, out_places=None, grant=50):
    return pl.pallas_call(
        body,
        out_shape=outs,
        in_specs=[*places, *[VM] * (len(args) - len(places))],
        out_specs=jax.tree.map(lambda _: VM, outs) if out_places is None else out_places,
        scratch_shapes=scratch,
        compiler_params=pltpu.CompilerParams(vmem_limit_bytes=grant * 1024 * 1024),
        cost_estimate=pl.CostEstimate(flops=flops, bytes_accessed=0, transcendentals=0),
    )(*args)


def shape(dims, dtype):
    return jax.ShapeDtypeStruct(dims, dtype)


def by_group(kernel):
    taps = jnp.pad(kernel.reshape(27, 6, PART), ((0, 1), (0, 0), (0, 0))).reshape(7, 4, 6, PART)
    return jnp.transpose(taps, (0, 2, 1, 3)).reshape(42, CH)


def shards(
    latents,
    gain_first,
    shift_first,
    kernel_first,
    bias_first,
    gain_second,
    shift_second,
    kernel_second,
    bias_second,
):
    space = lax.axis_index("space")
    frame = lax.axis_index("tm")
    pos = jnp.stack([space, frame]).astype(jnp.int32)
    vectors = jnp.stack(
        [gain_first, shift_first, bias_first, gain_second, shift_second, bias_second, bias_second, bias_second]
    )
    tile = latents[0, 0]
    flat_tile = tile.reshape(ROWS * WIDE, CH)

    swapped = lax.ppermute(jnp.pad(by_group(kernel_second), ((0, 6), (0, 0))), BOTH, SWAP)
    placed, west, east, sums = call(
        measure_tile,
        (shape((320, CH), BF), shape((16, CH), BF), shape((16, CH), BF), shape((NY * COLS, 128), F32)),
        [],
        [],
        flat_tile,
        jnp.asarray(CHANNEL_LANES, BF),
        jnp.asarray(GROUPS_OF),
        jnp.asarray(GROUPS_OF.T),
        jnp.asarray(SQUARES_OF),
        jnp.asarray(EDGES, BF),
        grant=60,
    )
    send = functools.partial(lax.ppermute, axis_name="space")
    from_west, from_east = send(east, perm=moved(0, 1)), send(west, perm=moved(0, -1))
    plane_sums = lax.all_to_all(sums, BOTH, 0, 0, tiled=True, axis_index_groups=PLANE)
    sums_rows = call(pool_plane, shape((8, CH), BF), [], [], plane_sums)
    from_north = send(jnp.concatenate([placed[240:320], from_west[12:16], from_east[12:16]]), perm=moved(1, 0))
    from_south = send(jnp.concatenate([placed[0:80], from_west[0:4], from_east[0:4]]), perm=moved(-1, 0))
    parcel = jnp.concatenate([placed, from_west, from_east, from_north, from_south], axis=0)
    sums_rows, swapped, packed = lax.optimization_barrier((sums_rows, swapped, by_group(kernel_first)))
    letter = jnp.concatenate([packed, sums_rows[0:6], swapped], axis=0)
    letters = jnp.broadcast_to(letter[None], (NZ, 96, CH))
    letters, parcel = lax.optimization_barrier((letters, parcel))
    got = lax.all_to_all(letters, "space", 0, 0, tiled=True, axis_index_groups=ALONG_Z)
    later = [lax.ppermute(parcel, "tm", [(t, (t + k) % NY) for t in range(NY)]) for k in range(1, NY)]
    ordered, all_sums = call(
        arrange_first,
        (shape((NX, 336, CH), BF), shape((8, 128), F32)),
        [],
        [],
        got,
        jnp.asarray(FIRST_ROWS, BF),
    )
    got_second, _ = lax.optimization_barrier((got, ordered))
    ordered_second = call(
        arrange_second,
        shape((432, CH), BF),
        [],
        [],
        got_second,
        jnp.asarray(SECOND_ROWS, BF),
    )
    ordered, ordered_second = lax.optimization_barrier((ordered, ordered_second))
    own = lax.all_to_all(ordered, "space", 0, 0, tiled=True, axis_index_groups=ALONG_X)
    stack = call(
        first_act,
        shape((NY, FIELD, 3 * CH), BF),
        [
            pltpu.VMEM((GUARD + (ROWS + 4) * PITCH + GUARD, CH), F32),
            pltpu.VMEM((NY, 528, CH), BF),
            pltpu.VMEM((NY, FIELD, 3 * CH), BF),
            pltpu.SemaphoreType.DMA((NY,)),
            pltpu.SemaphoreType.DMA((NY,)),
        ],
        [SM, AT, AT, AT, AT],
        pos,
        parcel,
        *later,
        all_sums,
        vectors,
        jnp.asarray(CHANNEL_LANES, BF),
        jnp.asarray(GROUPS_OF_LANES),
        jnp.asarray(SQUARES_OF_LANES),
        flops=int(2e10),
        out_places=HB,
        grant=48,
    )
    own, stack = lax.optimization_barrier((own, stack))
    other = lax.ppermute(own, "space", SIBLING)

    field, sums = call(
        first_conv,
        (shape((NY, RING, 128), F32), shape((SPACE, 128), F32)),
        [
            pltpu.VMEM((7, COLS, 48, CH), BF),
            pltpu.VMEM((3 * CH, 9 * 128), BF),
            pltpu.VMEM((NY, FIELD, 3 * CH), BF),
            pltpu.SemaphoreType.DMA((COLS,)),
            pltpu.SemaphoreType.DMA((NY,)),
        ],
        [SM, HB, AT, AT],
        pos,
        stack,
        own.reshape(NX, 7, 48, CH),
        other.reshape(NX, 7, 48, CH),
        vectors,
        jnp.asarray(PART_GROUPS),
        jnp.asarray(PART_GROUPS.T),
        jnp.asarray(PART_SQUARES),
        jnp.asarray(SECOND_LANES.T, BF),
    )
    all_sums = lax.all_to_all(sums, "space", 0, 0, tiled=True)
    own_second = lax.all_gather(ordered_second, "space", axis_index_groups=ALONG_X)
    own_second, _ = lax.optimization_barrier((own_second, all_sums))
    other_second = lax.ppermute(own_second, "space", SIBLING)
    partial = call(
        second_conv,
        shape((NY, ROWS, WIDE, CH), BF),
        [
            pltpu.VMEM((27, COLS, 16, CH), BF),
            pltpu.VMEM((RING, 128), F32),
            pltpu.VMEM((NY, 384, 9 * 128), BF),
            pltpu.VMEM((NY, RING, 128), F32),
            pltpu.SemaphoreType.DMA((COLS,)),
            pltpu.SemaphoreType.DMA((NY,)),
        ],
        [SM, AT, HB, AT],
        pos,
        field,
        own_second.reshape(NX, 27, 16, CH),
        other_second.reshape(NX, 27, 16, CH),
        all_sums,
        vectors,
        jnp.asarray(PART_GROUPS.T),
        jnp.asarray(PART_SQUARES.T),
        jnp.asarray(PART_LANES, BF),
        grant=46,
    )
    parts = lax.all_to_all(partial, "tm", 0, 0, tiled=True)
    second_out = jnp.sum(parts.astype(F32), axis=0) + bias_second
    return (tile.astype(F32) + second_out).astype(BF)[None, None]


def solution(mesh):
    placed = (
        P("tm", "space", None, None, None),
        P(),
        P(),
        P(None, None, None, "space", "tm"),
        P(),
        P(),
        P(),
        P(None, None, None, "space", "tm"),
        P(),
    )
    return jax.shard_map(
        shards,
        mesh=mesh,
        in_specs=placed,
        out_specs=P("tm", "space", None, None, None),
        check_vma=False,
    )
```

```python
import functools

import jax
import jax.numpy as jnp
import numpy as np
from jax import lax
from jax.experimental import pallas as pl
from jax.experimental.pallas import tpu as pltpu
from jax.sharding import PartitionSpec as P

EPS = 1e-06
BF = jnp.bfloat16
F32 = jnp.float32
VM = pl.BlockSpec(memory_space=pltpu.VMEM)
SM = pl.BlockSpec(memory_space=pltpu.SMEM)
AT = pl.BlockSpec(memory_space=pl.ANY)
HB = pl.BlockSpec(memory_space=pltpu.HBM)
HIGH = lax.Precision.HIGHEST

NZ, NX, NC, NY = 8, 4, 2, 4
COLS = NX * NC
SPACE = NZ * COLS
ROWS, WIDE, PITCH = 8, 40, 48
CH, PART, WG = 384, 96, 12
GUARD = 16
LEAD = 8
RING = LEAD + (ROWS + 2) * PITCH + 8
FIELD = RING + 2 * PITCH
BOTH = ("tm", "space")
ALONG_Z = [[z * COLS + q for z in range(NZ)] for q in range(COLS)]
ALONG_X = [[z * COLS + x * NC + c for x in range(NX)] for z in range(NZ) for c in range(NC)]
PLANE = [[y * SPACE + z * COLS + q for y in range(NY) for q in range(COLS)] for z in range(NZ)]
SIBLING = [(s, s ^ 1) for s in range(SPACE)]


def moved(down, right):
    return [(s, (s + COLS * down + right) % SPACE) for s in range(SPACE)]


SWAP = [
    (y * SPACE + z * COLS + q, (z // 2) * SPACE + (2 * y + z % 2) * COLS + q)
    for y in range(NY)
    for z in range(NZ)
    for q in range(COLS)
]


def one_hot(rows, cols, pairs):
    out = np.zeros((rows, cols), np.float32)
    for r, c in pairs:
        out[r, c] = 1.0
    return out


CHANNEL_LANES = one_hot(
    CH, CH, [(6 * (8 * z + q) + i, 48 * q + 6 * z + i) for z in range(8) for q in range(8) for i in range(6)]
)
GROUPS_OF = one_hot(CH, 128, [(c, c // WG) for c in range(CH)])
SQUARES_OF = np.roll(GROUPS_OF, 64, axis=1)
GROUPS_OF_LANES = (CHANNEL_LANES.T @ GROUPS_OF).T
SQUARES_OF_LANES = (CHANNEL_LANES.T @ SQUARES_OF).T
PART_GROUPS = one_hot(128, 128, [(c, c // WG) for c in range(PART)])
PART_SQUARES = np.roll(PART_GROUPS, 64, axis=1)
EDGES = one_hot(
    32,
    320,
    [(2 * r + c, 40 * r + c) for r in range(8) for c in range(2)]
    + [(16 + 2 * r + c, 40 * r + 38 + c) for r in range(8) for c in range(2)],
)
FIRST_ROWS = one_hot(
    336, 384, [(48 * g + 6 * z + i, 48 * z + 6 * g + i) for g in range(7) for z in range(8) for i in range(6)]
)
SECOND_ROWS = one_hot(
    112, 96, [(16 * g + 6 * h + i, 48 * h + 6 * g + i) for g in range(7) for h in range(2) for i in range(6)]
)
SECOND_LANES = one_hot(512, CH, [(128 * y + o, PART * y + o) for y in range(4) for o in range(PART)])
PART_LANES = one_hot(
    128, 128, [(48 * h + 6 * q + i, 16 * q + 6 * h + i) for h in range(2) for q in range(8) for i in range(6)]
)


def dot(a, b):
    return jnp.dot(a, b, preferred_element_type=F32)


def exact(a, b):
    return jnp.dot(a, b, preferred_element_type=F32, precision=HIGH)


def merge(sums, count, groups_t, squares_t):
    mean = jnp.mean(sums, axis=0, keepdims=True)
    off = sums - mean
    between = count * jnp.sum(off * off, axis=0, keepdims=True)
    within = jnp.sum(sums, axis=0, keepdims=True)
    rows = jnp.concatenate([mean, between, jnp.zeros((6, 128), F32)], axis=0)
    by_lane = exact(rows, groups_t)
    spread = (by_lane[1:2] + exact(tall(within), squares_t)[0:1]) * (1.0 / (count * sums.shape[0]))
    return by_lane[0:1], lax.rsqrt(spread + EPS)


def pool(rows, count):
    mean = jnp.mean(rows, axis=0, keepdims=True)
    off = rows - mean
    between = count * jnp.sum(off * off, axis=0, keepdims=True)
    squares = jnp.sum(rows, axis=0, keepdims=True) + pltpu.roll(tall(between), 64, axis=1)[0:1]
    return jnp.where(lax.broadcasted_iota(jnp.int32, (1, 128), 1) < 64, mean, squares)


def tall(row):
    return jnp.broadcast_to(row, (8, row.shape[1]))


def chosen(part):
    channel = lax.broadcasted_iota(jnp.int32, (CH, 128), 0)
    lane = lax.broadcasted_iota(jnp.int32, (CH, 128), 1)
    return ((channel == part * PART + lane) & (lane < PART)).astype(F32)


def silu(u):
    return u / (1.0 + jnp.exp(-u))


def measure_tile(
    tile_ref, lanes_ref, groups_ref, groups_t_ref, squares_ref, edges_ref,
    parcel_ref, north_ref, south_ref, west_ref, east_ref, sums_ref,
):
    tile = tile_ref[...]
    placed = dot(tile, lanes_ref[...]).astype(BF)
    parcel_ref[0:320, :] = placed
    parcel_ref[320:528, :] = jnp.zeros((208, CH), BF)
    north_ref[...] = placed[0:80]
    south_ref[...] = placed[240:320]
    edges = dot(edges_ref[...], placed).astype(BF)
    west_ref[...] = edges[0:16]
    east_ref[...] = edges[16:32]
    wide = tile.astype(F32)
    mean = exact(tall(jnp.sum(wide, axis=0, keepdims=True)), groups_ref[...]) * (1.0 / (320 * WG))
    off = wide - exact(mean, groups_t_ref[...])[0:1]
    squares = exact(tall(jnp.sum(off * off, axis=0, keepdims=True)), squares_ref[...])
    sums_ref[...] = jnp.broadcast_to((mean + squares)[0:1], sums_ref.shape)


def pool_plane(sums_ref, out_ref):
    row = pool(sums_ref[...], 320.0 * WG)
    hi = row.astype(BF).astype(F32)
    mid = (row - hi).astype(BF).astype(F32)
    rows = jnp.concatenate([hi, mid, row - hi - mid, jnp.zeros((5, 128), F32)], axis=0)
    out_ref[...] = jnp.concatenate([rows, jnp.zeros((8, CH - 128), F32)], axis=1).astype(BF)


def arrange_first(got_ref, rows_ref, out_ref, sums_ref):
    blocks = [got_ref[z, 0:48, :] for z in range(NZ)]
    ordered = dot(rows_ref[...], jnp.concatenate(blocks, axis=0)).astype(BF)
    for copy in range(NX):
        out_ref[copy] = ordered
    wide = [b[:, 0:128].astype(F32) for b in blocks]
    sums_ref[...] = jnp.concatenate([b[42:43] + b[43:44] + b[44:45] for b in wide], axis=0)


def arrange_second(got_ref, rows_ref, out_ref):
    parts = []
    for y in range(NY):
        pair = jnp.concatenate([got_ref[2 * y + h, 48:96, :] for h in range(2)], axis=0)
        parts.append(dot(rows_ref[...], pair))
    for k in range(4):
        whole = jnp.concatenate([part[:, PART * k : PART * k + PART] for part in parts], axis=1).astype(BF)
        for g in range(7):
            tap = 4 * g + k
            if tap < 27:
                out_ref[16 * tap : 16 * tap + 16, :] = whole[16 * g : 16 * g + 16]


def first_act(
    pos_ref, lat0_ref, lat1_ref, lat2_ref, lat3_ref, sums_ref, vectors_ref, lanes_ref, groups_t_ref, squares_t_ref,
    stack_ref, flat, lats, stack, in_sems, out_sems,
):
    arrivals = [
        pltpu.make_async_copy(lat_ref, lats.at[back], in_sems.at[back])
        for back, lat_ref in enumerate((lat0_ref, lat1_ref, lat2_ref, lat3_ref))
    ]
    for arrival in arrivals:
        arrival.start()
    row, col = pos_ref[0] // COLS, pos_ref[0] % COLS
    mean_l, scale_l = merge(sums_ref[...], 320.0 * WG * NY * COLS, groups_t_ref[...], squares_t_ref[...])
    vectors = vectors_ref[...]
    high = vectors.astype(BF)
    middle = (vectors - high.astype(F32)).astype(BF)
    low = (vectors - high.astype(F32) - middle.astype(F32)).astype(BF)
    lanes = lanes_ref[...]
    affine = dot(high, lanes) + dot(middle, lanes) + dot(low, lanes)
    scale_l = scale_l * affine[0:1]
    shift_l = affine[1:2]
    has_w = (col > 0).astype(F32)
    has_e = (col < COLS - 1).astype(F32)
    has_n = (row > 0).astype(F32)
    has_s = (row < NZ - 1).astype(F32)
    flat[...] = jnp.zeros_like(flat)
    leaving = []
    for back in range(NY):
        t = (pos_ref[1] + (NY - back)) % NY
        arrivals[back].wait()
        act = silu((lats[back].astype(F32) - mean_l) * scale_l + shift_l)
        for r in range(-2, ROWS + 2):
            base = GUARD + PITCH * (r + 2)
            if 0 <= r < ROWS:
                cells = act[WIDE * r : WIDE * r + WIDE]
                left, right = act[320 + 2 * r : 322 + 2 * r] * has_w, act[336 + 2 * r : 338 + 2 * r] * has_e
            else:
                start, at, inside = (352, r + 2, has_n) if r < 0 else (440, r - ROWS, has_s)
                cells = act[start + WIDE * at : start + WIDE * at + WIDE] * inside
                left = act[start + 80 + 2 * at : start + 82 + 2 * at] * (inside * has_w)
                right = act[start + 84 + 2 * at : start + 86 + 2 * at] * (inside * has_e)
            flat[base : base + WIDE, :] = cells
            flat[base + WIDE : base + WIDE + 2, :] = right
            flat[base - 2 : base, :] = left
        for d in range(3):
            start = GUARD - LEAD + d - 1
            stack[back, :, CH * d : CH * d + CH] = flat[start : start + FIELD, :].astype(BF)
        leaving.append(pltpu.make_async_copy(stack.at[back], stack_ref.at[t], out_sems.at[back]))
        leaving[back].start()
    for leave in leaving:
        leave.wait()


def land(core, own_ref, other_ref, slots, sems):
    copies = []
    for x in range(NX):
        at = NC * x
        copies.append(pltpu.make_async_copy(own_ref.at[x], slots.at[:, at + core], sems.at[at]))
        copies.append(pltpu.make_async_copy(other_ref.at[x], slots.at[:, at + 1 - core], sems.at[at + 1]))
    for copy in copies:
        copy.start()
    return copies


def first_conv(
    pos_ref, stack_ref, own_ref, other_ref, vectors_ref, part_ref, part_t_ref, part_squares_ref, spread_ref,
    out_ref, sums_ref, packed, weights, stack, sems, stack_sems,
):
    landing = land(pos_ref[0] % NC, own_ref, other_ref, packed, sems)
    arrivals = [pltpu.make_async_copy(stack_ref.at[t], stack.at[t], stack_sems.at[t]) for t in range(NY)]
    for arrival in arrivals:
        arrival.start()
    bias = exact(vectors_ref[...], chosen(pos_ref[1]))[2:3]
    for copy in landing:
        copy.wait()
    for g in range(7):
        taps = dot(packed[g].reshape(CH, CH), spread_ref[...]).astype(BF)
        for tap in range(4 * g, min(4 * g + 4, 27)):
            down, right = CH * (tap % 3), 128 * (tap // 3)
            weights[down : down + CH, right : right + 128] = taps[:, 128 * (tap % 4) : 128 * (tap % 4) + 128]
    totals = [None] * NY
    for t in range(NY):
        first = max(0, t + 3 - NY)
        arrivals[t].wait()
        product = dot(stack[t], weights[:, CH * first :])
        for dt in range(first, 3):
            to = t + 2 - dt
            part = product[:, CH * (dt - first) : CH * (dt - first) + CH]
            term = part[0:RING, 0:128]
            for dy in (1, 2):
                term = term + part[PITCH * dy : PITCH * dy + RING, 128 * dy : 128 * dy + 128]
            totals[to] = term if totals[to] is None else totals[to] + term
    at = lax.broadcasted_iota(jnp.int32, (RING, 1), 0) - (LEAD + PITCH)
    inside = ((at >= 0) & (at < PITCH * ROWS) & (at % PITCH < WIDE)).astype(F32)
    sums = None
    for t in range(NY):
        totals[t] = totals[t] + bias
        out_ref[t] = totals[t]
        line = jnp.sum(totals[t] * inside, axis=0, keepdims=True)
        sums = line if sums is None else sums + line
    mean = exact(tall(sums), part_ref[...]) * (1.0 / (320 * NY * WG))
    mean_l = exact(mean, part_t_ref[...])[0:1]
    sums = None
    for t in range(NY):
        off = (totals[t] - mean_l) * inside
        line = jnp.sum(off * off, axis=0, keepdims=True)
        sums = line if sums is None else sums + line
    squares = exact(tall(sums), part_squares_ref[...])
    sums_ref[...] = jnp.broadcast_to((mean + squares)[0:1], (SPACE, 128))


def second_conv(
    pos_ref, field_ref, own_ref, other_ref, sums_ref, vectors_ref, groups_t_ref, squares_t_ref, order_ref, out_ref,
    weights, flat, stack, field, sems, field_sems,
):
    arrivals = [pltpu.make_async_copy(field_ref.at[t], field.at[t], field_sems.at[t]) for t in range(NY)]
    for arrival in arrivals:
        arrival.start()
    landing = land(pos_ref[0] % NC, own_ref, other_ref, weights, sems)
    row, col = pos_ref[0] // COLS, pos_ref[0] % COLS
    mean_l, scale_l = merge(sums_ref[...], 320.0 * NY * WG, groups_t_ref[...], squares_t_ref[...])
    affine = exact(vectors_ref[...], chosen(pos_ref[1]))
    scale_l = scale_l * affine[3:4]
    shift_l = affine[4:5]

    at = lax.broadcasted_iota(jnp.int32, (RING, 1), 0) - LEAD
    outside = (at < 0) & (row == 0) | (at < PITCH - 2) & (row == 0)
    outside = outside | (at >= PITCH * (ROWS + 1) - 1) & (row == NZ - 1)
    at = (at + PITCH) % PITCH
    outside = outside | (at == WIDE) & (col == COLS - 1) | (at == PITCH - 1) & (col == 0)
    keep = 1.0 - outside.astype(F32)
    for t in range(NY):
        arrivals[t].wait()
        act = silu((field[t] - mean_l) * scale_l + shift_l) * keep
        flat[...] = dot(act.astype(BF), order_ref[...])
        for dy in range(3):
            for dx in range(3):
                start = LEAD + PITCH * dy + dx - 1
                lane = 128 * (3 * dy + dx)
                stack[t, :, lane : lane + 128] = flat[start : start + 384, :].astype(BF)
    for copy in landing:
        copy.wait()
    for t in range(NY):
        total = None
        for dt in range(3):
            source = t - 2 + dt
            if source < 0:
                continue
            term = dot(stack[source], weights[9 * dt : 9 * dt + 9].reshape(1152, CH))
            total = term if total is None else total + term
        for r in range(ROWS):
            out_ref[t, r] = total[PITCH * r : PITCH * r + WIDE].astype(BF)


def call(body, outs, scratch, places, *args, flops=0, out_places=None, grant=50):
    return pl.pallas_call(
        body,
        out_shape=outs,
        in_specs=[*places, *[VM] * (len(args) - len(places))],
        out_specs=jax.tree.map(lambda _: VM, outs) if out_places is None else out_places,
        scratch_shapes=scratch,
        compiler_params=pltpu.CompilerParams(vmem_limit_bytes=grant * 1024 * 1024),
        cost_estimate=pl.CostEstimate(flops=flops, bytes_accessed=0, transcendentals=0),
    )(*args)


def shape(dims, dtype):
    return jax.ShapeDtypeStruct(dims, dtype)


def by_group(kernel):
    taps = jnp.pad(kernel.reshape(27, 6, PART), ((0, 1), (0, 0), (0, 0))).reshape(7, 4, 6, PART)
    return jnp.transpose(taps, (0, 2, 1, 3)).reshape(42, CH)


def shards(
    latents,
    gain_first,
    shift_first,
    kernel_first,
    bias_first,
    gain_second,
    shift_second,
    kernel_second,
    bias_second,
):
    space = lax.axis_index("space")
    frame = lax.axis_index("tm")
    pos = jnp.stack([space, frame]).astype(jnp.int32)
    vectors = jnp.stack(
        [gain_first, shift_first, bias_first, gain_second, shift_second, bias_second, bias_second, bias_second]
    )
    tile = latents[0, 0]
    flat_tile = tile.reshape(ROWS * WIDE, CH)

    swapped = lax.ppermute(jnp.pad(by_group(kernel_second), ((0, 6), (0, 0))), BOTH, SWAP)
    parcel, north, south, west, east, sums = call(
        measure_tile,
        (
            shape((528, CH), BF),
            shape((80, CH), BF),
            shape((80, CH), BF),
            shape((16, CH), BF),
            shape((16, CH), BF),
            shape((NY * COLS, 128), F32),
        ),
        [],
        [],
        flat_tile,
        jnp.asarray(CHANNEL_LANES, BF),
        jnp.asarray(GROUPS_OF),
        jnp.asarray(GROUPS_OF.T),
        jnp.asarray(SQUARES_OF),
        jnp.asarray(EDGES, BF),
        grant=60,
    )
    send = functools.partial(lax.ppermute, axis_name="space")
    from_west, from_east = send(east, perm=moved(0, 1)), send(west, perm=moved(0, -1))
    plane_sums = lax.all_to_all(sums, BOTH, 0, 0, tiled=True, axis_index_groups=PLANE)
    sums_rows = call(pool_plane, shape((8, CH), BF), [], [], plane_sums)
    from_north = send(jnp.concatenate([south, from_west[12:16], from_east[12:16]]), perm=moved(1, 0))
    from_south = send(jnp.concatenate([north, from_west[0:4], from_east[0:4]]), perm=moved(-1, 0))
    for halo, row in ((from_west, 320), (from_east, 336), (from_north, 352), (from_south, 440)):
        parcel = lax.dynamic_update_slice(parcel, halo, (row, 0))
    sums_rows, swapped, packed = lax.optimization_barrier((sums_rows, swapped, by_group(kernel_first)))
    letter = jnp.concatenate([packed, sums_rows[0:6], swapped], axis=0)
    letters = jnp.broadcast_to(letter[None], (NZ, 96, CH))
    letters, parcel = lax.optimization_barrier((letters, parcel))
    got = lax.all_to_all(letters, "space", 0, 0, tiled=True, axis_index_groups=ALONG_Z)
    later = [lax.ppermute(parcel, "tm", [(t, (t + k) % NY) for t in range(NY)]) for k in range(1, NY)]
    ordered, all_sums = call(
        arrange_first,
        (shape((NX, 336, CH), BF), shape((8, 128), F32)),
        [],
        [],
        got,
        jnp.asarray(FIRST_ROWS, BF),
    )
    got_second, _ = lax.optimization_barrier((got, ordered))
    ordered_second = call(
        arrange_second,
        shape((432, CH), BF),
        [],
        [],
        got_second,
        jnp.asarray(SECOND_ROWS, BF),
    )
    ordered, ordered_second = lax.optimization_barrier((ordered, ordered_second))
    own = lax.all_to_all(ordered, "space", 0, 0, tiled=True, axis_index_groups=ALONG_X)
    stack = call(
        first_act,
        shape((NY, FIELD, 3 * CH), BF),
        [
            pltpu.VMEM((GUARD + (ROWS + 4) * PITCH + GUARD, CH), F32),
            pltpu.VMEM((NY, 528, CH), BF),
            pltpu.VMEM((NY, FIELD, 3 * CH), BF),
            pltpu.SemaphoreType.DMA((NY,)),
            pltpu.SemaphoreType.DMA((NY,)),
        ],
        [SM, AT, AT, AT, AT],
        pos,
        parcel,
        *later,
        all_sums,
        vectors,
        jnp.asarray(CHANNEL_LANES, BF),
        jnp.asarray(GROUPS_OF_LANES),
        jnp.asarray(SQUARES_OF_LANES),
        flops=int(2e10),
        out_places=HB,
        grant=60,
    )
    own, stack = lax.optimization_barrier((own, stack))
    other = lax.ppermute(own, "space", SIBLING)

    field, sums = call(
        first_conv,
        (shape((NY, RING, 128), F32), shape((SPACE, 128), F32)),
        [
            pltpu.VMEM((7, COLS, 48, CH), BF),
            pltpu.VMEM((3 * CH, 9 * 128), BF),
            pltpu.VMEM((NY, FIELD, 3 * CH), BF),
            pltpu.SemaphoreType.DMA((COLS,)),
            pltpu.SemaphoreType.DMA((NY,)),
        ],
        [SM, HB, AT, AT],
        pos,
        stack,
        own.reshape(NX, 7, 48, CH),
        other.reshape(NX, 7, 48, CH),
        vectors,
        jnp.asarray(PART_GROUPS),
        jnp.asarray(PART_GROUPS.T),
        jnp.asarray(PART_SQUARES),
        jnp.asarray(SECOND_LANES.T, BF),
    )
    all_sums = lax.all_to_all(sums, "space", 0, 0, tiled=True)
    own_second = lax.all_gather(ordered_second, "space", axis_index_groups=ALONG_X)
    own_second, _ = lax.optimization_barrier((own_second, all_sums))
    other_second = lax.ppermute(own_second, "space", SIBLING)
    partial = call(
        second_conv,
        shape((NY, ROWS, WIDE, CH), BF),
        [
            pltpu.VMEM((27, COLS, 16, CH), BF),
            pltpu.VMEM((RING, 128), F32),
            pltpu.VMEM((NY, 384, 9 * 128), BF),
            pltpu.VMEM((NY, RING, 128), F32),
            pltpu.SemaphoreType.DMA((COLS,)),
            pltpu.SemaphoreType.DMA((NY,)),
        ],
        [SM, AT, HB, AT],
        pos,
        field,
        own_second.reshape(NX, 27, 16, CH),
        other_second.reshape(NX, 27, 16, CH),
        all_sums,
        vectors,
        jnp.asarray(PART_GROUPS.T),
        jnp.asarray(PART_SQUARES.T),
        jnp.asarray(PART_LANES, BF),
        grant=46,
    )
    parts = lax.all_to_all(partial, "tm", 0, 0, tiled=True)
    second_out = jnp.sum(parts.astype(F32), axis=0) + bias_second
    return (tile.astype(F32) + second_out).astype(BF)[None, None]


def solution(mesh):
    placed = (
        P("tm", "space", None, None, None),
        P(),
        P(),
        P(None, None, None, "space", "tm"),
        P(),
        P(),
        P(),
        P(None, None, None, "space", "tm"),
        P(),
    )
    return jax.shard_map(
        shards,
        mesh=mesh,
        in_specs=placed,
        out_specs=P("tm", "space", None, None, None),
        check_vma=False,
    )
```

```python
import functools

import jax
import jax.numpy as jnp
import numpy as np
from jax import lax
from jax.experimental import pallas as pl
from jax.experimental.pallas import tpu as pltpu
from jax.sharding import PartitionSpec as P

EPS = 1e-06
BF = jnp.bfloat16
F32 = jnp.float32
VM = pl.BlockSpec(memory_space=pltpu.VMEM)
SM = pl.BlockSpec(memory_space=pltpu.SMEM)
AT = pl.BlockSpec(memory_space=pl.ANY)
HB = pl.BlockSpec(memory_space=pltpu.HBM)
HIGH = lax.Precision.HIGHEST

NZ, NX, NC, NY = 8, 4, 2, 4
COLS = NX * NC
SPACE = NZ * COLS
ROWS, WIDE, PITCH = 8, 40, 48
CH, PART, WG = 384, 96, 12
GUARD = 16
LEAD = 8
RING = LEAD + (ROWS + 2) * PITCH + 8
FIELD = RING + 2 * PITCH
BOTH = ("tm", "space")
ALONG_Z = [[z * COLS + q for z in range(NZ)] for q in range(COLS)]
ALONG_X = [[z * COLS + x * NC + c for x in range(NX)] for z in range(NZ) for c in range(NC)]
PLANE = [[y * SPACE + z * COLS + q for y in range(NY) for q in range(COLS)] for z in range(NZ)]
SIBLING = [(s, s ^ 1) for s in range(SPACE)]


def moved(down, right):
    return [(s, (s + COLS * down + right) % SPACE) for s in range(SPACE)]


SWAP = [
    (y * SPACE + z * COLS + q, (z // 2) * SPACE + (2 * y + z % 2) * COLS + q)
    for y in range(NY)
    for z in range(NZ)
    for q in range(COLS)
]


def one_hot(rows, cols, pairs):
    out = np.zeros((rows, cols), np.float32)
    for r, c in pairs:
        out[r, c] = 1.0
    return out


CHANNEL_LANES = one_hot(
    CH, CH, [(6 * (8 * z + q) + i, 48 * q + 6 * z + i) for z in range(8) for q in range(8) for i in range(6)]
)
GROUPS_OF = one_hot(CH, 128, [(c, c // WG) for c in range(CH)])
SQUARES_OF = np.roll(GROUPS_OF, 64, axis=1)
GROUPS_OF_LANES = (CHANNEL_LANES.T @ GROUPS_OF).T
SQUARES_OF_LANES = (CHANNEL_LANES.T @ SQUARES_OF).T
PART_GROUPS = one_hot(128, 128, [(c, c // WG) for c in range(PART)])
PART_SQUARES = np.roll(PART_GROUPS, 64, axis=1)
EDGES = one_hot(
    32,
    320,
    [(2 * r + c, 40 * r + c) for r in range(8) for c in range(2)]
    + [(16 + 2 * r + c, 40 * r + 38 + c) for r in range(8) for c in range(2)],
)
FIRST_ROWS = one_hot(
    336, 384, [(48 * g + 6 * z + i, 48 * z + 6 * g + i) for g in range(7) for z in range(8) for i in range(6)]
)
SECOND_ROWS = one_hot(
    112, 96, [(16 * g + 6 * h + i, 48 * h + 6 * g + i) for g in range(7) for h in range(2) for i in range(6)]
)
SECOND_LANES = one_hot(512, CH, [(128 * y + o, PART * y + o) for y in range(4) for o in range(PART)])
PART_LANES = one_hot(
    128, 128, [(48 * h + 6 * q + i, 16 * q + 6 * h + i) for h in range(2) for q in range(8) for i in range(6)]
)


def dot(a, b):
    return jnp.dot(a, b, preferred_element_type=F32)


def exact(a, b):
    return jnp.dot(a, b, preferred_element_type=F32, precision=HIGH)


def merge(sums, count, groups_t, squares_t):
    mean = jnp.mean(sums, axis=0, keepdims=True)
    off = sums - mean
    between = count * jnp.sum(off * off, axis=0, keepdims=True)
    within = jnp.sum(sums, axis=0, keepdims=True)
    rows = jnp.concatenate([mean, between, jnp.zeros((6, 128), F32)], axis=0)
    by_lane = exact(rows, groups_t)
    spread = (by_lane[1:2] + exact(tall(within), squares_t)[0:1]) * (1.0 / (count * sums.shape[0]))
    return by_lane[0:1], lax.rsqrt(spread + EPS)


def pool(rows, count):
    mean = jnp.mean(rows, axis=0, keepdims=True)
    off = rows - mean
    between = count * jnp.sum(off * off, axis=0, keepdims=True)
    squares = jnp.sum(rows, axis=0, keepdims=True) + pltpu.roll(tall(between), 64, axis=1)[0:1]
    return jnp.where(lax.broadcasted_iota(jnp.int32, (1, 128), 1) < 64, mean, squares)


def tall(row):
    return jnp.broadcast_to(row, (8, row.shape[1]))


def chosen(part):
    channel = lax.broadcasted_iota(jnp.int32, (CH, 128), 0)
    lane = lax.broadcasted_iota(jnp.int32, (CH, 128), 1)
    return ((channel == part * PART + lane) & (lane < PART)).astype(F32)


def silu(u):
    return u / (1.0 + jnp.exp(-u))


def measure_tile(
    tile_ref, lanes_ref, groups_ref, groups_t_ref, squares_ref, edges_ref,
    placed_ref, west_ref, east_ref, sums_ref,
):
    tile = tile_ref[...]
    placed = dot(tile, lanes_ref[...]).astype(BF)
    placed_ref[...] = placed
    edges = dot(edges_ref[...], placed).astype(BF)
    west_ref[...] = edges[0:16]
    east_ref[...] = edges[16:32]
    wide = tile.astype(F32)
    mean = exact(tall(jnp.sum(wide, axis=0, keepdims=True)), groups_ref[...]) * (1.0 / (320 * WG))
    off = wide - exact(mean, groups_t_ref[...])[0:1]
    squares = exact(tall(jnp.sum(off * off, axis=0, keepdims=True)), squares_ref[...])
    sums_ref[...] = jnp.broadcast_to((mean + squares)[0:1], sums_ref.shape)


def pool_plane(sums_ref, out_ref):
    row = pool(sums_ref[...], 320.0 * WG)
    hi = row.astype(BF).astype(F32)
    mid = (row - hi).astype(BF).astype(F32)
    rows = jnp.concatenate([hi, mid, row - hi - mid, jnp.zeros((5, 128), F32)], axis=0)
    out_ref[...] = jnp.concatenate([rows, jnp.zeros((8, CH - 128), F32)], axis=1).astype(BF)


def arrange_first(got_ref, rows_ref, out_ref, sums_ref):
    blocks = [got_ref[z, 0:48, :] for z in range(NZ)]
    ordered = dot(rows_ref[...], jnp.concatenate(blocks, axis=0)).astype(BF)
    for copy in range(NX):
        out_ref[copy] = ordered
    wide = [b[:, 0:128].astype(F32) for b in blocks]
    sums_ref[...] = jnp.concatenate([b[42:43] + b[43:44] + b[44:45] for b in wide], axis=0)


def arrange_second(got_ref, rows_ref, out_ref):
    parts = []
    for y in range(NY):
        pair = jnp.concatenate([got_ref[2 * y + h, 48:96, :] for h in range(2)], axis=0)
        parts.append(dot(rows_ref[...], pair))
    for k in range(4):
        whole = jnp.concatenate([part[:, PART * k : PART * k + PART] for part in parts], axis=1).astype(BF)
        for g in range(7):
            tap = 4 * g + k
            if tap < 27:
                out_ref[16 * tap : 16 * tap + 16, :] = whole[16 * g : 16 * g + 16]


def first_act(
    pos_ref, lat0_ref, lat1_ref, lat2_ref, lat3_ref, sums_ref, vectors_ref, lanes_ref, groups_t_ref, squares_t_ref,
    stack_ref, flat, lats, stack, in_sems, out_sems,
):
    arrivals = [
        pltpu.make_async_copy(lat_ref, lats.at[back], in_sems.at[back])
        for back, lat_ref in enumerate((lat0_ref, lat1_ref, lat2_ref, lat3_ref))
    ]
    for arrival in arrivals:
        arrival.start()
    row, col = pos_ref[0] // COLS, pos_ref[0] % COLS
    mean_l, scale_l = merge(sums_ref[...], 320.0 * WG * NY * COLS, groups_t_ref[...], squares_t_ref[...])
    vectors = vectors_ref[...]
    high = vectors.astype(BF)
    middle = (vectors - high.astype(F32)).astype(BF)
    low = (vectors - high.astype(F32) - middle.astype(F32)).astype(BF)
    lanes = lanes_ref[...]
    affine = dot(high, lanes) + dot(middle, lanes) + dot(low, lanes)
    scale_l = scale_l * affine[0:1]
    shift_l = affine[1:2]
    has_w = (col > 0).astype(F32)
    has_e = (col < COLS - 1).astype(F32)
    has_n = (row > 0).astype(F32)
    has_s = (row < NZ - 1).astype(F32)
    flat[...] = jnp.zeros_like(flat)
    leaving = []
    for back in range(NY):
        t = (pos_ref[1] + (NY - back)) % NY
        arrivals[back].wait()
        act = silu((lats[back].astype(F32) - mean_l) * scale_l + shift_l)
        for r in range(-2, ROWS + 2):
            base = GUARD + PITCH * (r + 2)
            if 0 <= r < ROWS:
                cells = act[WIDE * r : WIDE * r + WIDE]
                left, right = act[320 + 2 * r : 322 + 2 * r] * has_w, act[336 + 2 * r : 338 + 2 * r] * has_e
            else:
                start, at, inside = (352, r + 2, has_n) if r < 0 else (440, r - ROWS, has_s)
                cells = act[start + WIDE * at : start + WIDE * at + WIDE] * inside
                left = act[start + 80 + 2 * at : start + 82 + 2 * at] * (inside * has_w)
                right = act[start + 84 + 2 * at : start + 86 + 2 * at] * (inside * has_e)
            flat[base : base + WIDE, :] = cells
            flat[base + WIDE : base + WIDE + 2, :] = right
            flat[base - 2 : base, :] = left
        for d in range(3):
            start = GUARD - LEAD + d - 1
            stack[back, :, CH * d : CH * d + CH] = flat[start : start + FIELD, :].astype(BF)
        leaving.append(pltpu.make_async_copy(stack.at[back], stack_ref.at[t], out_sems.at[back]))
        leaving[back].start()
    for leave in leaving:
        leave.wait()


def land(core, own_ref, other_ref, slots, sems):
    copies = []
    for x in range(NX):
        at = NC * x
        copies.append(pltpu.make_async_copy(own_ref.at[x], slots.at[:, at + core], sems.at[at]))
        copies.append(pltpu.make_async_copy(other_ref.at[x], slots.at[:, at + 1 - core], sems.at[at + 1]))
    for copy in copies:
        copy.start()
    return copies


def first_conv(
    pos_ref, stack_ref, own_ref, other_ref, vectors_ref, part_ref, part_t_ref, part_squares_ref, spread_ref,
    out_ref, sums_ref, packed, weights, stack, sems, stack_sems,
):
    landing = land(pos_ref[0] % NC, own_ref, other_ref, packed, sems)
    arrivals = [pltpu.make_async_copy(stack_ref.at[t], stack.at[t], stack_sems.at[t]) for t in range(NY)]
    for arrival in arrivals:
        arrival.start()
    bias = exact(vectors_ref[...], chosen(pos_ref[1]))[2:3]
    for copy in landing:
        copy.wait()
    for g in range(7):
        taps = dot(packed[g].reshape(CH, CH), spread_ref[...]).astype(BF)
        for tap in range(4 * g, min(4 * g + 4, 27)):
            down, right = CH * (tap % 3), 128 * (tap // 3)
            weights[down : down + CH, right : right + 128] = taps[:, 128 * (tap % 4) : 128 * (tap % 4) + 128]
    totals = [None] * NY
    for t in range(NY):
        first = max(0, t + 3 - NY)
        arrivals[t].wait()
        product = dot(stack[t], weights[:, CH * first :])
        for dt in range(first, 3):
            to = t + 2 - dt
            part = product[:, CH * (dt - first) : CH * (dt - first) + CH]
            term = part[0:RING, 0:128]
            for dy in (1, 2):
                term = term + part[PITCH * dy : PITCH * dy + RING, 128 * dy : 128 * dy + 128]
            totals[to] = term if totals[to] is None else totals[to] + term
    at = lax.broadcasted_iota(jnp.int32, (RING, 1), 0) - (LEAD + PITCH)
    inside = ((at >= 0) & (at < PITCH * ROWS) & (at % PITCH < WIDE)).astype(F32)
    sums = None
    for t in range(NY):
        totals[t] = totals[t] + bias
        out_ref[t] = totals[t]
        line = jnp.sum(totals[t] * inside, axis=0, keepdims=True)
        sums = line if sums is None else sums + line
    mean = exact(tall(sums), part_ref[...]) * (1.0 / (320 * NY * WG))
    mean_l = exact(mean, part_t_ref[...])[0:1]
    sums = None
    for t in range(NY):
        off = (totals[t] - mean_l) * inside
        line = jnp.sum(off * off, axis=0, keepdims=True)
        sums = line if sums is None else sums + line
    squares = exact(tall(sums), part_squares_ref[...])
    sums_ref[...] = jnp.broadcast_to((mean + squares)[0:1], (SPACE, 128))


def second_conv(
    pos_ref, field_ref, own_ref, other_ref, sums_ref, vectors_ref, groups_t_ref, squares_t_ref, order_ref, out_ref,
    weights, flat, stack, field, sems, field_sems,
):
    arrivals = [pltpu.make_async_copy(field_ref.at[t], field.at[t], field_sems.at[t]) for t in range(NY)]
    for arrival in arrivals:
        arrival.start()
    landing = land(pos_ref[0] % NC, own_ref, other_ref, weights, sems)
    row, col = pos_ref[0] // COLS, pos_ref[0] % COLS
    mean_l, scale_l = merge(sums_ref[...], 320.0 * NY * WG, groups_t_ref[...], squares_t_ref[...])
    affine = exact(vectors_ref[...], chosen(pos_ref[1]))
    scale_l = scale_l * affine[3:4]
    shift_l = affine[4:5]

    at = lax.broadcasted_iota(jnp.int32, (RING, 1), 0) - LEAD
    outside = (at < 0) & (row == 0) | (at < PITCH - 2) & (row == 0)
    outside = outside | (at >= PITCH * (ROWS + 1) - 1) & (row == NZ - 1)
    at = (at + PITCH) % PITCH
    outside = outside | (at == WIDE) & (col == COLS - 1) | (at == PITCH - 1) & (col == 0)
    keep = 1.0 - outside.astype(F32)
    for t in range(NY):
        arrivals[t].wait()
        act = silu((field[t] - mean_l) * scale_l + shift_l) * keep
        flat[...] = dot(act.astype(BF), order_ref[...])
        for dy in range(3):
            for dx in range(3):
                start = LEAD + PITCH * dy + dx - 1
                lane = 128 * (3 * dy + dx)
                stack[t, :, lane : lane + 128] = flat[start : start + 384, :].astype(BF)
    for copy in landing:
        copy.wait()
    for t in range(NY):
        total = None
        for dt in range(3):
            source = t - 2 + dt
            if source < 0:
                continue
            term = dot(stack[source], weights[9 * dt : 9 * dt + 9].reshape(1152, CH))
            total = term if total is None else total + term
        for r in range(ROWS):
            out_ref[t, r] = total[PITCH * r : PITCH * r + WIDE].astype(BF)


def call(body, outs, scratch, places, *args, flops=0, out_places=None, grant=50):
    return pl.pallas_call(
        body,
        out_shape=outs,
        in_specs=[*places, *[VM] * (len(args) - len(places))],
        out_specs=jax.tree.map(lambda _: VM, outs) if out_places is None else out_places,
        scratch_shapes=scratch,
        compiler_params=pltpu.CompilerParams(vmem_limit_bytes=grant * 1024 * 1024),
        cost_estimate=pl.CostEstimate(flops=flops, bytes_accessed=0, transcendentals=0),
    )(*args)


def shape(dims, dtype):
    return jax.ShapeDtypeStruct(dims, dtype)


def by_group(kernel):
    taps = jnp.pad(kernel.reshape(27, 6, PART), ((0, 1), (0, 0), (0, 0))).reshape(7, 4, 6, PART)
    return jnp.transpose(taps, (0, 2, 1, 3)).reshape(42, CH)


def shards(
    latents,
    gain_first,
    shift_first,
    kernel_first,
    bias_first,
    gain_second,
    shift_second,
    kernel_second,
    bias_second,
):
    space = lax.axis_index("space")
    frame = lax.axis_index("tm")
    pos = jnp.stack([space, frame]).astype(jnp.int32)
    vectors = jnp.stack(
        [gain_first, shift_first, bias_first, gain_second, shift_second, bias_second, bias_second, bias_second]
    )
    tile = latents[0, 0]
    flat_tile = tile.reshape(ROWS * WIDE, CH)

    swapped = lax.ppermute(jnp.pad(by_group(kernel_second), ((0, 6), (0, 0))), BOTH, SWAP)
    placed, west, east, sums = call(
        measure_tile,
        (shape((320, CH), BF), shape((16, CH), BF), shape((16, CH), BF), shape((NY * COLS, 128), F32)),
        [],
        [],
        flat_tile,
        jnp.asarray(CHANNEL_LANES, BF),
        jnp.asarray(GROUPS_OF),
        jnp.asarray(GROUPS_OF.T),
        jnp.asarray(SQUARES_OF),
        jnp.asarray(EDGES, BF),
        grant=60,
    )
    send = functools.partial(lax.ppermute, axis_name="space")
    from_west, from_east = send(east, perm=moved(0, 1)), send(west, perm=moved(0, -1))
    plane_sums = lax.all_to_all(sums, BOTH, 0, 0, tiled=True, axis_index_groups=PLANE)
    sums_rows = call(pool_plane, shape((8, CH), BF), [], [], plane_sums)
    from_north = send(jnp.concatenate([placed[240:320], from_west[12:16], from_east[12:16]]), perm=moved(1, 0))
    from_south = send(jnp.concatenate([placed[0:80], from_west[0:4], from_east[0:4]]), perm=moved(-1, 0))
    parcel = jnp.concatenate([placed, from_west, from_east, from_north, from_south], axis=0)
    sums_rows, swapped, packed = lax.optimization_barrier((sums_rows, swapped, by_group(kernel_first)))
    letter = jnp.concatenate([packed, sums_rows[0:6], swapped], axis=0)
    letters = jnp.broadcast_to(letter[None], (NZ, 96, CH))
    letters, parcel = lax.optimization_barrier((letters, parcel))
    got = lax.all_to_all(letters, "space", 0, 0, tiled=True, axis_index_groups=ALONG_Z)
    later = [lax.ppermute(parcel, "tm", [(t, (t + k) % NY) for t in range(NY)]) for k in range(1, NY)]
    ordered, all_sums = call(
        arrange_first,
        (shape((NX, 336, CH), BF), shape((8, 128), F32)),
        [],
        [],
        got,
        jnp.asarray(FIRST_ROWS, BF),
    )
    got_second, _ = lax.optimization_barrier((got, ordered))
    ordered_second = call(
        arrange_second,
        shape((432, CH), BF),
        [],
        [],
        got_second,
        jnp.asarray(SECOND_ROWS, BF),
    )
    ordered, ordered_second = lax.optimization_barrier((ordered, ordered_second))
    own = lax.all_to_all(ordered, "space", 0, 0, tiled=True, axis_index_groups=ALONG_X)
    stack = call(
        first_act,
        shape((NY, FIELD, 3 * CH), BF),
        [
            pltpu.VMEM((GUARD + (ROWS + 4) * PITCH + GUARD, CH), F32),
            pltpu.VMEM((NY, 528, CH), BF),
            pltpu.VMEM((NY, FIELD, 3 * CH), BF),
            pltpu.SemaphoreType.DMA((NY,)),
            pltpu.SemaphoreType.DMA((NY,)),
        ],
        [SM, AT, AT, AT, AT],
        pos,
        parcel,
        *later,
        all_sums,
        vectors,
        jnp.asarray(CHANNEL_LANES, BF),
        jnp.asarray(GROUPS_OF_LANES),
        jnp.asarray(SQUARES_OF_LANES),
        flops=int(2e10),
        out_places=HB,
        grant=60,
    )
    own, stack = lax.optimization_barrier((own, stack))
    other = lax.ppermute(own, "space", SIBLING)

    field, sums = call(
        first_conv,
        (shape((NY, RING, 128), F32), shape((SPACE, 128), F32)),
        [
            pltpu.VMEM((7, COLS, 48, CH), BF),
            pltpu.VMEM((3 * CH, 9 * 128), BF),
            pltpu.VMEM((NY, FIELD, 3 * CH), BF),
            pltpu.SemaphoreType.DMA((COLS,)),
            pltpu.SemaphoreType.DMA((NY,)),
        ],
        [SM, HB, AT, AT],
        pos,
        stack,
        own.reshape(NX, 7, 48, CH),
        other.reshape(NX, 7, 48, CH),
        vectors,
        jnp.asarray(PART_GROUPS),
        jnp.asarray(PART_GROUPS.T),
        jnp.asarray(PART_SQUARES),
        jnp.asarray(SECOND_LANES.T, BF),
    )
    all_sums = lax.all_to_all(sums, "space", 0, 0, tiled=True)
    own_second = lax.all_gather(ordered_second, "space", axis_index_groups=ALONG_X)
    own_second, _ = lax.optimization_barrier((own_second, all_sums))
    other_second = lax.ppermute(own_second, "space", SIBLING)
    partial = call(
        second_conv,
        shape((NY, ROWS, WIDE, CH), BF),
        [
            pltpu.VMEM((27, COLS, 16, CH), BF),
            pltpu.VMEM((RING, 128), F32),
            pltpu.VMEM((NY, 384, 9 * 128), BF),
            pltpu.VMEM((NY, RING, 128), F32),
            pltpu.SemaphoreType.DMA((COLS,)),
            pltpu.SemaphoreType.DMA((NY,)),
        ],
        [SM, AT, HB, AT],
        pos,
        field,
        own_second.reshape(NX, 27, 16, CH),
        other_second.reshape(NX, 27, 16, CH),
        all_sums,
        vectors,
        jnp.asarray(PART_GROUPS.T),
        jnp.asarray(PART_SQUARES.T),
        jnp.asarray(PART_LANES, BF),
        grant=46,
    )
    parts = lax.all_to_all(partial, "tm", 0, 0, tiled=True)
    second_out = jnp.sum(parts.astype(F32), axis=0) + bias_second
    return (tile.astype(F32) + second_out).astype(BF)[None, None]


def solution(mesh):
    placed = (
        P("tm", "space", None, None, None),
        P(),
        P(),
        P(None, None, None, "space", "tm"),
        P(),
        P(),
        P(),
        P(None, None, None, "space", "tm"),
        P(),
    )
    return jax.shard_map(
        shards,
        mesh=mesh,
        in_specs=placed,
        out_specs=P("tm", "space", None, None, None),
        check_vma=False,
    )
```
